512 devices in a mesh: replica: 8 (over x, core), shard: 64 (over y, z).
Axes of the slice: x: 4, y: 4, z: 16, core: 2. Of those that a mesh axis runs over, the one named last changes fastest.
Arguments:
- grads: bfloat16 [8, 128, 512, 512], P('replica', None, 'shard')
- block_slot: int32 [128], replicated, may hold values from 0 to 255, as said below
- left_stat: float32 [256, 512, 512], P('shard', 'replica'), may hold values from 0 to 2
- right_stat: float32 [256, 512, 512], P('shard', 'replica'), may hold values from 0 to 2
- left_root: bfloat16 [256, 512, 512], P('shard', 'replica'), as said below
- right_root: bfloat16 [256, 512, 512], P('shard', 'replica'), as said below
Outputs:
- update: bfloat16 [128, 512, 512], P(None, 'shard')
- left_new: float32 [256, 512, 512], P('shard', 'replica')
- right_new: float32 [256, 512, 512], P('shard', 'replica')
The draws below stay inside these ranges and needn't reach their ends.
Inputs may be any that keep to these rules, and one draw needn't show every extreme that they name: `block_slot`: slot k belongs to index k // 4 of shard. No two blocks share a slot; some index of shard owns 4 blocks. `left_root`: every slot's matrix is exactly symmetric. `right_root`: every slot's matrix is exactly symmetric.
All inputs are finite; a program needn't handle non-finite values.
Results may differ from the reference program's by a relative error of at most 0.02.
Values may be sent and summed in bfloat16 or wider, within the bound.
No kernel may reach another device: no remote copies, remote signals or barrier semaphores. Data moves between devices by JAX's collectives and lax.ppermute only.
A program may use at most 64 MiB of HBM per device.

```python
import math
import jax
import jax.numpy as jnp
from jax import lax

B = 512
CAP = 4
NB = 128
SLOTS = 256
N_REPLICA = 8
N_SHARD = 64


def draw_grads(key, part):
    key = jax.random.fold_in(key, 11)
    key_rows, key_cols, key_noise = jax.random.split(key, 3)
    row_scale = jnp.exp(jax.random.uniform(key_rows, (NB, B, 1), jnp.float32) * math.log(10.0))
    ramp = jnp.exp(jnp.arange(B, dtype=jnp.float32) / (B - 1) * math.log(3.0))
    col_scale = jnp.exp(jax.random.uniform(key_cols, (NB, 1, B), jnp.float32) * math.log(10.0)) * ramp
    noise = jax.random.normal(key_noise, (N_REPLICA, NB, B, B), jnp.float32)
    return (noise * row_scale * col_scale * (0.5 / B)).astype(jnp.bfloat16)


def draw_block_slot(key, part):
    key = jax.random.fold_in(key, 31)
    key_busy, key_other, key_order = jax.random.split(key, 3)
    busiest = jax.random.randint(key_busy, (), 1, N_SHARD - 1).astype(jnp.int32)
    pool = jax.random.permutation(key_other, (N_SHARD - 1) * CAP - 2)[:NB - CAP - 2].astype(jnp.int32) + 1
    owner = pool // CAP
    owner = owner + (owner >= busiest).astype(jnp.int32)
    other_slots = owner * CAP + pool % CAP
    full_slots = busiest * CAP + jnp.arange(CAP, dtype=jnp.int32)
    end_slots = jnp.array([0, SLOTS - 1], dtype=jnp.int32)
    slots = jnp.concatenate([full_slots, end_slots, other_slots])
    return slots[jax.random.permutation(key_order, NB)].astype(jnp.int32)


def symmetric_draw(key, off_scale, diag_lo, diag_hi):
    key_noise, key_diag = jax.random.split(key)
    noise = jax.random.normal(key_noise, (SLOTS, B, B), jnp.float32)
    off_part = (noise + jnp.swapaxes(noise, 1, 2)) * (off_scale / math.sqrt(2.0 * B))
    diagonal = jax.random.uniform(key_diag, (SLOTS, B, 1), jnp.float32, diag_lo, diag_hi)
    identity = (jnp.arange(B)[:, None] == jnp.arange(B)[None, :]).astype(jnp.float32)
    return (off_part + diagonal * identity).astype(jnp.bfloat16)


def draw_left_root(key, part):
    key = jax.random.fold_in(key, 21)
    return symmetric_draw(key, 1.0, 1.0, 2.0)


def draw_right_root(key, part):
    key = jax.random.fold_in(key, 22)
    return symmetric_draw(key, 1.0, 1.0, 2.0)


def steps_of(stream_key, dims, cuts, low, top_value):
    gain, own = 1.0, jax.random.fold_in(stream_key, 6)
    for dim, parts in cuts:
        heights = jnp.exp(jax.random.uniform(jax.random.fold_in(own, dim), (parts,), jnp.float32, low / len(cuts), top_value / len(cuts)))
        gain = gain * jnp.repeat(heights, dims[dim] // parts).reshape([-1 if axis == dim else 1 for axis in range(len(dims))])
    return gain


def setup_inputs(seed: int = 0) -> dict:
    seeds = jax.random.split(jax.random.key(seed), 7)
    grads = draw_grads(jax.random.fold_in(seeds[6], 71), 0)
    block_slot = draw_block_slot(jax.random.fold_in(seeds[6], 71), 0)
    left_stat = jnp.clip(2.0 * jax.random.uniform(seeds[2], (SLOTS, B, B), jnp.float32) ** steps_of(seeds[2], (SLOTS, B, B), ((0, 64), (1, 8)), -0.2, 0.2), 0.0, 2.0)
    right_stat = jnp.clip(2.0 * jax.random.uniform(seeds[3], (SLOTS, B, B), jnp.float32) ** steps_of(seeds[3], (SLOTS, B, B), ((0, 64), (1, 8)), -0.2, 0.2), 0.0, 2.0)
    left_root = draw_left_root(jax.random.fold_in(seeds[6], 71), 0)
    right_root = draw_right_root(jax.random.fold_in(seeds[6], 71), 0)
    return dict(grads=grads, block_slot=block_slot, left_stat=left_stat, right_stat=right_stat, left_root=left_root, right_root=right_root)


STAT_DECAY = 0.9
NORM_EPS = 1e-12

def reference(grads, block_slot, left_stat, right_stat, left_root, right_root):

    def one_block(index):
        partials = lax.dynamic_index_in_dim(grads, index, axis=1, keepdims=False)
        slot_id = lax.dynamic_index_in_dim(block_slot, index, axis=0, keepdims=False).astype(jnp.int32)
        grad_mat = lax.optimization_barrier(jnp.sum(partials.astype(jnp.float32), axis=0)).astype(jnp.bfloat16)
        left_mat = lax.dynamic_index_in_dim(left_root, slot_id, axis=0, keepdims=False)
        right_mat = lax.dynamic_index_in_dim(right_root, slot_id, axis=0, keepdims=False)
        left_term = jnp.dot(grad_mat, grad_mat.T, preferred_element_type=jnp.float32)
        right_term = jnp.dot(grad_mat.T, grad_mat, preferred_element_type=jnp.float32)
        shaped = jnp.dot(grad_mat, right_mat, preferred_element_type=jnp.float32).astype(jnp.bfloat16)
        direction = jnp.dot(left_mat, shaped, preferred_element_type=jnp.float32)
        grad_sq = jnp.sum(jnp.square(grad_mat.astype(jnp.float32)))
        dir_sq = jnp.sum(jnp.square(direction))
        update = (-direction * (jnp.sqrt(grad_sq) / jnp.sqrt(dir_sq + NORM_EPS))).astype(jnp.bfloat16)
        return (update, left_term, right_term)
    update, left_terms, right_terms = lax.map(one_block, jnp.arange(NB, dtype=jnp.int32))
    left_new = (STAT_DECAY * left_stat).at[block_slot].set(STAT_DECAY * left_stat[block_slot] + (1.0 - STAT_DECAY) * left_terms)
    right_new = (STAT_DECAY * right_stat).at[block_slot].set(STAT_DECAY * right_stat[block_slot] + (1.0 - STAT_DECAY) * right_terms)
    return (update, left_new, right_new)
```

```python
import functools

import jax
import jax.numpy as jnp
from jax import lax
from jax.experimental import pallas as pl
from jax.experimental.pallas import tpu as pltpu
from jax.sharding import Mesh, PartitionSpec as P

STAT_DECAY = 0.9
NORM_EPS = 1e-12
F32 = jnp.float32
BF16 = jnp.bfloat16
VMEM_SPEC = pl.BlockSpec(memory_space=pltpu.VMEM)
SMEM_SPEC = pl.BlockSpec(memory_space=pltpu.SMEM)
PARAMS = pltpu.CompilerParams(vmem_limit_bytes=32 * 1024 * 1024)


def dot(a, b, dims):
    return lax.dot_general(a, b, (dims, ((), ())), preferred_element_type=F32)


def pair_sum_kernel(order, core, own, other, out):
    chips, depth = out.shape[0], out.shape[1]
    width = out.shape[3]
    cols = pl.ds(pl.multiple_of(core[0] * width, 128), width)

    def body(i, carry):
        for x in range(chips):
            block = order[i * chips + x]
            mine = own[block, :, cols].astype(F32)
            out[x, i] = (mine + other[block].astype(F32)).astype(BF16)
        return carry

    lax.fori_loop(0, depth, body, 0, unroll=4)


def chip_sum_kernel(place, parts, out, total):
    depth = parts.shape[1]
    acc = parts[0].astype(F32)
    for x in range(1, parts.shape[0]):
        acc = acc + parts[x].astype(F32)
    total[0:depth] = acc.astype(BF16)
    total[depth] = jnp.zeros(total.shape[1:], BF16)

    def body(o, carry):
        out[o] = total[place[o]]
        return carry

    lax.fori_loop(0, out.shape[0], body, 0, unroll=8)


def direction_kernel(info, own, other, left, right, out):
    core = info[0]
    half = own.shape[1]
    groups = left.shape[0]
    size = groups * left.shape[2]
    slot = info[1]
    left_mat = left[:, slot].reshape(size, size)
    g_own = own[...]
    g_other = other[...]
    grad_sq = jnp.sum(jnp.square(g_own.astype(F32))) + jnp.sum(jnp.square(g_other.astype(F32)))

    def columns(h):
        cols = pl.ds(pl.multiple_of(h * half, 128), half)
        upper = right[pl.ds(core * (groups // 2), groups // 2), slot, :, cols].reshape(half, half)
        lower = right[pl.ds((1 - core) * (groups // 2), groups // 2), slot, :, cols].reshape(half, half)
        shaped = dot(g_own, upper, ((1,), (0,))) + dot(g_other, lower, ((1,), (0,)))
        return dot(left_mat, shaped.astype(BF16), ((1,), (0,)))

    far = columns(1 - core)
    dir_sq = jnp.sum(jnp.square(far))
    near = columns(core)
    dir_sq = dir_sq + jnp.sum(jnp.square(near))
    grad_sq = jnp.full((1, 1), grad_sq, F32)
    dir_sq = jnp.full((1, 1), dir_sq, F32)
    ratio = jnp.sqrt(grad_sq) / jnp.sqrt(dir_sq + NORM_EPS)
    out[...] = (-near * ratio).astype(BF16)


def stats_kernel(info, chip_of_slot, grads, left, right, left_out, right_out):
    x, core = info[0], info[1]
    rows = left.shape[1]
    half = grads.shape[2]
    row_at = pl.multiple_of((2 * x + core) * rows, 16)
    col_at = pl.multiple_of((x % 2) * 2 * rows, 128)
    for j in range(left.shape[0]):
        chip = chip_of_slot[j]

        @pl.when(chip >= 0)
        def _():
            g0 = grads[2 * chip]
            g1 = grads[2 * chip + 1]
            r0 = grads[2 * chip, pl.ds(row_at, rows)]
            r1 = grads[2 * chip + 1, pl.ds(row_at, rows)]
            term = dot(r0, g0, ((1,), (1,))) + dot(r1, g1, ((1,), (1,)))
            left_out[j] = STAT_DECAY * left[j] + (1.0 - STAT_DECAY) * term
            cols = grads[2 * chip + x // 2, :, pl.ds(col_at, 2 * rows)]
            for h, g in ((0, g0), (1, g1)):
                prod = dot(cols, g, ((0,), (0,)))
                term = jnp.where(core == 0, prod[:rows], prod[rows:])
                at = pl.ds(h * half, half)
                right_out[j, :, at] = STAT_DECAY * right[j, :, at] + (1.0 - STAT_DECAY) * term

        @pl.when(chip < 0)
        def _():
            left_out[j] = STAT_DECAY * left[j]
            right_out[j] = STAT_DECAY * right[j]


def compact_kernel(owner, rows, out):
    def body(i, carry):
        block = rows[owner[i]]
        for x in range(out.shape[0]):
            out[x, i] = block
        return carry

    lax.fori_loop(0, out.shape[1], body, 0, unroll=4)


def place_kernel(rank, core, own, other, out):
    chips = own.shape[0]
    width = own.shape[3]
    near = pl.ds(pl.multiple_of(core[0] * width, 128), width)
    far = pl.ds(pl.multiple_of((1 - core[0]) * width, 128), width)

    def body(b, carry):
        x = rank[b] % chips
        i = rank[b] // chips
        out[b, :, near] = own[x, i]
        out[b, :, far] = other[x, i]
        return carry

    lax.fori_loop(0, out.shape[0], body, 0, unroll=4)


def call(kernel, out_shape, in_specs, scratch=()):
    multi = isinstance(out_shape, (tuple, list))
    return pl.pallas_call(
        kernel,
        out_shape=out_shape,
        in_specs=in_specs,
        out_specs=tuple(VMEM_SPEC for _ in out_shape) if multi else VMEM_SPEC,
        scratch_shapes=list(scratch),
        compiler_params=PARAMS,
    )


def exchange(value, axis):
    return lax.all_to_all(value, axis, 0, 0, tiled=True)


def swap_cores(value):
    return lax.ppermute(value, "core", [(0, 1), (1, 0)])


def local(grads, block_slot, left_stat, right_stat, left_root, right_root):
    grads = grads[0]
    chips = lax.axis_size("x")
    x = lax.axis_index("x")
    core = lax.axis_index("core")
    me = lax.axis_index("y") * lax.axis_size("z") + lax.axis_index("z")
    owners = lax.axis_size("y") * lax.axis_size("z")
    capacity = left_stat.shape[0]
    blocks, shard_rows, width = grads.shape
    half = width // 2
    depth = blocks // chips
    core1 = core.reshape(1)

    left_all = lax.all_gather(left_root, ("x", "core"), axis=0)
    right_all = lax.all_gather(right_root, ("x", "core"), axis=0)

    sent = lax.dynamic_slice_in_dim(grads, (1 - core) * half, half, 2)
    other = swap_cores(sent)

    rank = jnp.sum((block_slot[None, :] < block_slot[:, None]).astype(jnp.int32), axis=1)
    ids = jnp.arange(blocks, dtype=jnp.int32)
    at_rank = (rank[None, :] == ids[:, None]).astype(jnp.int32)
    order = jnp.sum(at_rank * ids[None, :], axis=1)
    slots = jnp.sum(at_rank * block_slot[None, :], axis=1)
    owner_of = slots // capacity
    mine = slots.reshape(depth, chips)
    mine = jnp.sum(jnp.where(jnp.arange(chips)[None, :] == x, mine, 0), axis=1)
    owner_here = mine // capacity
    hits = owner_here[None, :] == jnp.arange(owners, dtype=jnp.int32)[:, None]
    place = jnp.sum(jnp.where(hits, jnp.arange(depth, dtype=jnp.int32)[None, :] - depth, 0), axis=1) + depth
    slot_here = jnp.sum(jnp.where(owner_here == me, mine % capacity, 0))
    local_slot = jnp.arange(capacity, dtype=jnp.int32) + me * capacity
    chip_of_slot = jnp.sum(
        jnp.where(slots[None, :] == local_slot[:, None], ids[None, :] % chips + 1, 0), axis=1
    ) - 1

    parts = call(
        pair_sum_kernel,
        jax.ShapeDtypeStruct((chips, depth, shard_rows, half), BF16),
        [SMEM_SPEC, SMEM_SPEC, VMEM_SPEC, VMEM_SPEC],
    )(order, core1, grads, other)
    parts = exchange(parts, "x")
    outgoing = call(
        chip_sum_kernel,
        jax.ShapeDtypeStruct((owners, shard_rows, half), BF16),
        [SMEM_SPEC, VMEM_SPEC],
        [pltpu.VMEM((depth + 1, shard_rows, half), BF16)],
    )(place, parts)
    own = exchange(outgoing, ("y", "z")).reshape(width, half)
    far = swap_cores(own)
    grads_all = lax.all_gather(own, ("x", "core"), axis=0)

    update = call(
        direction_kernel,
        jax.ShapeDtypeStruct((width, half), BF16),
        [SMEM_SPEC] + [VMEM_SPEC] * 4,
    )(jnp.stack([core, slot_here]), own, far, left_all, right_all)

    rows = exchange(update.reshape(owners, shard_rows, half), ("y", "z"))
    packed = call(
        compact_kernel,
        jax.ShapeDtypeStruct((chips, depth, shard_rows, half), BF16),
        [SMEM_SPEC, VMEM_SPEC],
    )(owner_here, rows)
    near = exchange(packed, "x")
    near, grads_all = lax.optimization_barrier((near, grads_all))
    beyond = swap_cores(near)
    left_new, right_new = call(
        stats_kernel,
        (jax.ShapeDtypeStruct(left_stat.shape, F32), jax.ShapeDtypeStruct(right_stat.shape, F32)),
        [SMEM_SPEC, SMEM_SPEC] + [VMEM_SPEC] * 3,
    )(jnp.stack([x, core]), chip_of_slot, grads_all, left_stat, right_stat)
    result = call(
        place_kernel,
        jax.ShapeDtypeStruct((blocks, shard_rows, width), BF16),
        [SMEM_SPEC, SMEM_SPEC, VMEM_SPEC, VMEM_SPEC],
    )(rank, core1, near, beyond)
    return (result, left_new, right_new)


def solution(mesh):
    fine = Mesh(mesh.devices.reshape(4, 2, 4, 16), ("x", "core", "y", "z"))
    replica, shard = ("x", "core"), ("y", "z")
    in_specs = (
        P(replica, None, shard, None),
        P(),
        P(shard, replica, None),
        P(shard, replica, None),
        P(shard, replica, None),
        P(shard, replica, None),
    )
    out_specs = (P(None, shard, None), P(shard, replica, None), P(shard, replica, None))
    return jax.shard_map(local, mesh=fine, in_specs=in_specs, out_specs=out_specs, check_vma=False)
```

```python
import functools

import jax
import jax.numpy as jnp
from jax import lax
from jax.experimental import pallas as pl
from jax.experimental.pallas import tpu as pltpu
from jax.sharding import Mesh, PartitionSpec as P

STAT_DECAY = 0.9
NORM_EPS = 1e-12
F32 = jnp.float32
BF16 = jnp.bfloat16
VMEM_SPEC = pl.BlockSpec(memory_space=pltpu.VMEM)
HBM_SPEC = pl.BlockSpec(memory_space=pltpu.HBM)
SMEM_SPEC = pl.BlockSpec(memory_space=pltpu.SMEM)
PARAMS = pltpu.CompilerParams(vmem_limit_bytes=32 * 1024 * 1024)


def dot(a, b, dims):
    return lax.dot_general(a, b, (dims, ((), ())), preferred_element_type=F32)


def split_kernel(core_ref, grads, left_root, right_root, kept, sent, roots, sems):
    core = core_ref[0]
    width = kept.shape[2]
    capacity = left_root.shape[0]
    near = pl.ds(pl.multiple_of(core * width, 128), width)
    far = pl.ds(pl.multiple_of((1 - core) * width, 128), width)
    copies = [
        pltpu.make_async_copy(grads.at[:, :, far], sent, sems.at[0]),
        pltpu.make_async_copy(grads.at[:, :, near], kept, sems.at[1]),
        pltpu.make_async_copy(left_root, roots.at[pl.ds(0, capacity)], sems.at[2]),
        pltpu.make_async_copy(right_root, roots.at[pl.ds(capacity, capacity)], sems.at[3]),
    ]
    for copy in copies:
        copy.start()
    for copy in copies:
        copy.wait()


def pair_sum_kernel(order, own, other, out):
    chips, depth = out.shape[:2]

    def body(i, carry):
        for x in range(chips):
            block = order[i * chips + x]
            out[x, i] = own[block] + other[block]
        return carry

    lax.fori_loop(0, depth, body, 0, unroll=4)


def chip_sum_kernel(at, table, parts, out, total):
    depth = parts.shape[1]
    acc = parts[0].astype(F32)
    for x in range(1, parts.shape[0]):
        acc = acc + parts[x].astype(F32)
    total[0:depth] = acc.astype(BF16)
    total[depth] = jnp.zeros(total.shape[1:], BF16)

    def body(o, carry):
        out[o] = total[table[at + o]]
        return carry

    lax.fori_loop(0, out.shape[0], body, 0, unroll=8)


def direction_kernel(at, table, own_hbm, other, roots, out, own, left, right, sems):
    core, slot = table[at], table[at + 1]
    capacity = roots.shape[1] // 2
    copies = [
        pltpu.make_async_copy(own_hbm, own, sems.at[0]),
        pltpu.make_async_copy(roots.at[:, capacity + slot], right, sems.at[1]),
        pltpu.make_async_copy(roots.at[:, slot], left, sems.at[2]),
    ]
    for copy in copies:
        copy.start()
    half = own.shape[1]
    groups, rows, size = left.shape
    copies[0].wait()
    g_own = own[...]
    g_other = other[...]
    grad_sq = jnp.sum(jnp.square(g_own.astype(F32))) + jnp.sum(jnp.square(g_other.astype(F32)))
    copies[1].wait()

    def shaped(h):
        cols = pl.ds(pl.multiple_of(h * half, 128), half)
        upper = right[pl.ds(core * (groups // 2), groups // 2), :, cols].reshape(half, half)
        lower = right[pl.ds((1 - core) * (groups // 2), groups // 2), :, cols].reshape(half, half)
        return (dot(g_own, upper, ((1,), (0,))) + dot(g_other, lower, ((1,), (0,)))).astype(BF16)

    shaped_far = shaped(1 - core)
    shaped_near = shaped(core)
    copies[2].wait()
    left_mat = left[...].reshape(size, size)
    dir_sq = jnp.sum(jnp.square(dot(left_mat, shaped_far, ((1,), (0,)))))
    near = dot(left_mat, shaped_near, ((1,), (0,)))
    dir_sq = dir_sq + jnp.sum(jnp.square(near))
    grad_sq = jnp.full((1, 1), grad_sq, F32)
    dir_sq = jnp.full((1, 1), dir_sq, F32)
    ratio = jnp.sqrt(grad_sq) / jnp.sqrt(dir_sq + NORM_EPS)
    out[...] = (-near * ratio).astype(BF16)


def stats_kernel(at, table, grads_hbm, left, right, left_hbm, right_hbm, grads, left_out, right_out, sems, out_sems):
    core, x = table[at], table[at + 2]
    capacity, rows, _ = left.shape
    half = grads.shape[3]
    loads = [
        pltpu.make_async_copy(grads_hbm.at[table[at + 3 + capacity + j]], grads.at[j], sems.at[j])
        for j in range(capacity)
    ]
    stores = []
    for load in loads:
        load.start()
    for j in range(capacity):
        full = table[at + 3 + j] > 0
        loads[j].wait()

        @pl.when(full)
        def _():
            g0 = grads[j, 0]
            g1 = grads[j, 1]
            own = pl.ds(pl.multiple_of((2 * x + core) * rows, 16), rows)
            term = dot(grads[j, 0, own], g0, ((1,), (1,))) + dot(grads[j, 1, own], g1, ((1,), (1,)))
            left_out[j] = STAT_DECAY * left[j] + (1.0 - STAT_DECAY) * term
            cols = grads[j, x // 2, :, pl.ds(pl.multiple_of((x % 2) * 2 * rows, 128), 2 * rows)]
            for h, g in ((0, g0), (1, g1)):
                prod = dot(cols, g, ((0,), (0,)))
                term = jnp.where(core == 0, prod[:rows], prod[rows:])
                at_cols = pl.ds(h * half, half)
                right_out[j, :, at_cols] = STAT_DECAY * right[j, :, at_cols] + (1.0 - STAT_DECAY) * term

        @pl.when(jnp.logical_not(full))
        def _():
            left_out[j] = STAT_DECAY * left[j]
            right_out[j] = STAT_DECAY * right[j]

        stores.append(pltpu.make_async_copy(left_out.at[j], left_hbm.at[j], out_sems.at[0, j]))
        stores.append(pltpu.make_async_copy(right_out.at[j], right_hbm.at[j], out_sems.at[1, j]))
        stores[-2].start()
        stores[-1].start()
    for store in stores:
        store.wait()


def compact_kernel(at, table, rows, out):
    def body(i, carry):
        block = rows[table[at + i]]
        for x in range(out.shape[0]):
            out[x, i] = block
        return carry

    lax.fori_loop(0, out.shape[1], body, 0, unroll=8)


def place_kernel(at, core_at, table, own, other, out):
    width = own.shape[2]
    core = table[core_at]
    near = pl.ds(pl.multiple_of(core * width, 128), width)
    far = pl.ds(pl.multiple_of((1 - core) * width, 128), width)
    first = pl.program_id(0) * out.shape[0]

    def body(b, carry):
        source = table[at + first + b]
        out[b, :, near] = own[source]
        out[b, :, far] = other[source]
        return carry

    lax.fori_loop(0, out.shape[0], body, 0, unroll=8)


def call(kernel, out_shape, in_specs, scratch=()):
    return pl.pallas_call(
        kernel,
        out_shape=out_shape,
        in_specs=in_specs,
        out_specs=VMEM_SPEC,
        scratch_shapes=list(scratch),
        compiler_params=PARAMS,
    )


def exchange(value, axis):
    return lax.all_to_all(value, axis, 0, 0, tiled=True)


def in_hbm(value):
    return pltpu.with_memory_space_constraint(value, pltpu.HBM)


def swap_cores(value):
    return lax.ppermute(value, "core", [(0, 1), (1, 0)])


def local(grads, block_slot, left_stat, right_stat, left_root, right_root):
    grads = grads[0]
    chips = lax.axis_size("x")
    x = lax.axis_index("x")
    core = lax.axis_index("core")
    owners = lax.axis_size("y") * lax.axis_size("z")
    me = lax.axis_index("y") * lax.axis_size("z") + lax.axis_index("z")
    capacity, stat_rows, _ = left_stat.shape
    blocks, shard_rows, width = grads.shape
    half = width // 2
    depth = blocks // chips

    kept, sent, roots = pl.pallas_call(
        split_kernel,
        out_shape=[
            jax.ShapeDtypeStruct((blocks, shard_rows, half), BF16),
            jax.ShapeDtypeStruct((blocks, shard_rows, half), BF16),
            jax.ShapeDtypeStruct((2 * capacity, stat_rows, width), BF16),
        ],
        in_specs=[SMEM_SPEC, HBM_SPEC, HBM_SPEC, HBM_SPEC],
        out_specs=[VMEM_SPEC, VMEM_SPEC, HBM_SPEC],
        scratch_shapes=[pltpu.SemaphoreType.DMA((4,))],
        compiler_params=PARAMS,
    )(core.reshape(1), in_hbm(grads), in_hbm(left_root), in_hbm(right_root))
    other = swap_cores(sent)
    roots = lax.all_gather(roots, ("x", "core"), axis=0)

    ids = jnp.arange(blocks, dtype=jnp.int32)
    rank = jnp.sum((block_slot[None, :] < block_slot[:, None]).astype(jnp.int32), axis=1)
    order = jnp.sum(jnp.where(rank[None, :] == ids[:, None], ids[None, :], 0), axis=1)
    owner = block_slot // capacity
    here = rank % chips == x
    spot = rank // chips
    owner_ids = jnp.arange(owners, dtype=jnp.int32)
    hits = here[None, :] & (owner[None, :] == owner_ids[:, None])
    place = jnp.sum(jnp.where(hits, spot[None, :] - depth, 0), axis=1) + depth
    hits = here[None, :] & (spot[None, :] == ids[:depth, None])
    owner_here = jnp.sum(jnp.where(hits, owner[None, :], 0), axis=1)
    slot_here = jnp.sum(jnp.where(here & (owner == me), block_slot % capacity, 0))
    mine = block_slot[None, :] == me * capacity + ids[:capacity, None]
    full = jnp.sum(mine.astype(jnp.int32), axis=1)
    chip_of_slot = jnp.sum(jnp.where(mine, rank[None, :] % chips, 0), axis=1)
    source = (rank % chips) * depth + spot
    info = jnp.stack([core, slot_here, x])
    table = jnp.concatenate([source, place, owner_here, info, full, chip_of_slot])
    at_place = blocks
    at_owner = at_place + owners
    at_info = at_owner + depth

    parts = call(
        pair_sum_kernel,
        jax.ShapeDtypeStruct((chips, depth, shard_rows, half), BF16),
        [SMEM_SPEC, VMEM_SPEC, VMEM_SPEC],
    )(order, kept, other)
    parts = exchange(parts, "x")
    outgoing = call(
        functools.partial(chip_sum_kernel, at_place),
        jax.ShapeDtypeStruct((owners, shard_rows, half), BF16),
        [SMEM_SPEC, VMEM_SPEC],
        [pltpu.VMEM((depth + 1, shard_rows, half), BF16)],
    )(table, parts)
    own = exchange(outgoing, ("y", "z")).reshape(width, half)
    far = swap_cores(own)
    grads_all = lax.all_gather(own, ("x", "core"), axis=0)

    update = call(
        functools.partial(direction_kernel, at_info),
        jax.ShapeDtypeStruct((width, half), BF16),
        [SMEM_SPEC, HBM_SPEC, VMEM_SPEC, HBM_SPEC],
        [
            pltpu.VMEM((width, half), BF16),
            pltpu.VMEM((width // stat_rows, stat_rows, width), BF16),
            pltpu.VMEM((width // stat_rows, stat_rows, width), BF16),
            pltpu.SemaphoreType.DMA((3,)),
        ],
    )(table, in_hbm(own), far, in_hbm(roots))

    rows = exchange(update.reshape(owners, shard_rows, half), ("y", "z"))
    packed = call(
        functools.partial(compact_kernel, at_owner),
        jax.ShapeDtypeStruct((chips, depth, shard_rows, half), BF16),
        [SMEM_SPEC, VMEM_SPEC],
    )(table, rows)
    packed, grads_all = lax.optimization_barrier((packed, grads_all))
    near = exchange(packed, "x").reshape(blocks, shard_rows, half)
    beyond = swap_cores(near)

    left_new, right_new = pl.pallas_call(
        functools.partial(stats_kernel, at_info),
        out_shape=[jax.ShapeDtypeStruct(left_stat.shape, F32), jax.ShapeDtypeStruct(right_stat.shape, F32)],
        in_specs=[SMEM_SPEC, HBM_SPEC, VMEM_SPEC, VMEM_SPEC],
        out_specs=[HBM_SPEC, HBM_SPEC],
        scratch_shapes=[
            pltpu.VMEM((capacity, 2, width, half), BF16),
            pltpu.VMEM(left_stat.shape, F32),
            pltpu.VMEM(right_stat.shape, F32),
            pltpu.SemaphoreType.DMA((capacity,)),
            pltpu.SemaphoreType.DMA((2, capacity)),
        ],
        compiler_params=PARAMS,
        cost_estimate=pl.CostEstimate(flops=400_000_000, bytes_accessed=6_000_000, transcendentals=0),
    )(table, in_hbm(grads_all.reshape(chips, 2, width, half)), left_stat, right_stat)

    steps = 4
    whole = pl.BlockSpec((blocks, shard_rows, half), lambda i, table: (0, 0, 0))
    result = pl.pallas_call(
        functools.partial(place_kernel, 0, at_info),
        out_shape=jax.ShapeDtypeStruct((blocks, shard_rows, width), BF16),
        grid_spec=pltpu.PrefetchScalarGridSpec(
            num_scalar_prefetch=1,
            grid=(steps,),
            in_specs=[whole, whole],
            out_specs=pl.BlockSpec((blocks // steps, shard_rows, width), lambda i, table: (i, 0, 0)),
        ),
        compiler_params=PARAMS,
    )(table, near, beyond)
    return (result, left_new, right_new)


def solution(mesh):
    fine = Mesh(mesh.devices.reshape(4, 2, 4, 16), ("x", "core", "y", "z"))
    replica, shard = ("x", "core"), ("y", "z")
    in_specs = (
        P(replica, None, shard, None),
        P(),
        P(shard, replica, None),
        P(shard, replica, None),
        P(shard, replica, None),
        P(shard, replica, None),
    )
    out_specs = (P(None, shard, None), P(shard, replica, None), P(shard, replica, None))
    return jax.shard_map(local, mesh=fine, in_specs=in_specs, out_specs=out_specs, check_vma=False)
```

```python
import functools

import jax
import jax.numpy as jnp
from jax import lax
from jax.experimental import pallas as pl
from jax.experimental.pallas import tpu as pltpu
from jax.sharding import Mesh, PartitionSpec as P

STAT_DECAY = 0.9
NORM_EPS = 1e-12
F32 = jnp.float32
BF16 = jnp.bfloat16
VMEM_SPEC = pl.BlockSpec(memory_space=pltpu.VMEM)
HBM_SPEC = pl.BlockSpec(memory_space=pltpu.HBM)
SMEM_SPEC = pl.BlockSpec(memory_space=pltpu.SMEM)
PARAMS = pltpu.CompilerParams(vmem_limit_bytes=32 * 1024 * 1024)


def dot(a, b, dims):
    return lax.dot_general(a, b, (dims, ((), ())), preferred_element_type=F32)


ORDER, SOURCE, PLACE, OWNER, SLOT, FULL, CHIP, WHERE = range(8)


def fill_table(slots, core, x, me, capacity, chips, table):
    blocks = slots.shape[1]
    square = (blocks, blocks)
    cap_bits, chip_bits = capacity.bit_length() - 1, chips.bit_length() - 1
    depth = blocks // chips
    lane = lax.broadcasted_iota(jnp.int32, square, 1)
    sublane = lax.broadcasted_iota(jnp.int32, square, 0)
    across = jnp.broadcast_to(slots[...], square)
    slot = across.T

    def total(mask, value):
        return jnp.sum(jnp.where(mask, value, 0), axis=0, keepdims=True)

    rank_row = total(slot < across, 1)
    rank = jnp.broadcast_to(rank_row, square).T
    here = (rank & (chips - 1)) == x
    spot = rank >> chip_bits
    owner = slot >> cap_bits
    local_slot = slot == me * capacity + lane
    table[pl.ds(ORDER, 1)] = total(rank == lane, sublane)
    table[pl.ds(SOURCE, 1)] = (rank_row & (chips - 1)) * depth + (rank_row >> chip_bits)
    table[pl.ds(PLACE, 1)] = total(here & (owner == lane), spot - depth) + depth
    table[pl.ds(OWNER, 1)] = total(here & (spot == lane), owner)
    table[pl.ds(SLOT, 1)] = total(here & (owner == me), slot & (capacity - 1))
    table[pl.ds(FULL, 1)] = total(local_slot, 1)
    table[pl.ds(CHIP, 1)] = total(local_slot, rank & (chips - 1))
    row = lax.broadcasted_iota(jnp.int32, (1, blocks), 1)
    table[pl.ds(WHERE, 1)] = jnp.where(row == 0, core, x)


def split_kernel(chips, core_ref, x_ref, me_ref, slots, grads, left_root, right_root, kept, sent, roots, table, held, sems):
    core = core_ref[0]
    width = kept.shape[2]
    capacity = left_root.shape[0]
    near = pl.ds(pl.multiple_of(core * width, 128), width)
    far = pl.ds(pl.multiple_of((1 - core) * width, 128), width)
    loads = [
        pltpu.make_async_copy(left_root, held.at[pl.ds(0, capacity)], sems.at[0]),
        pltpu.make_async_copy(right_root, held.at[pl.ds(capacity, capacity)], sems.at[1]),
        pltpu.make_async_copy(grads.at[:, :, far], sent, sems.at[2]),
        pltpu.make_async_copy(grads.at[:, :, near], kept, sems.at[3]),
    ]
    store = pltpu.make_async_copy(held, roots, sems.at[4])
    for load in loads:
        load.start()
    loads[0].wait()
    loads[1].wait()
    store.start()
    fill_table(slots, core, x_ref[0], me_ref[0], capacity, chips, table)
    loads[2].wait()
    loads[3].wait()
    store.wait()


def pair_sum_kernel(table, own, other, out):
    chips, depth = out.shape[:2]

    def body(i, carry):
        for x in range(chips):
            block = table[ORDER, i * chips + x]
            out[x, i] = own[block] + other[block]
        return carry

    lax.fori_loop(0, depth, body, 0, unroll=8)


def chip_sum_kernel(table, parts, out, total):
    depth = parts.shape[1]
    acc = parts[0].astype(F32)
    for x in range(1, parts.shape[0]):
        acc = acc + parts[x].astype(F32)
    total[0:depth] = acc.astype(BF16)
    total[depth] = jnp.zeros(total.shape[1:], BF16)

    def body(o, carry):
        out[o] = total[table[PLACE, o]]
        return carry

    lax.fori_loop(0, out.shape[0], body, 0, unroll=8)


def near_kernel(table, own_hbm, roots, partial, left, lower, grad_sq, own, upper, sems):
    core, slot = table[WHERE, 0], table[SLOT, 0]
    capacity = roots.shape[1] // 2
    groups = upper.shape[0]
    half = own.shape[1]
    loads = [
        pltpu.make_async_copy(own_hbm, own, sems.at[0]),
        pltpu.make_async_copy(roots.at[pl.ds(core * groups, groups), capacity + slot], upper, sems.at[1]),
        pltpu.make_async_copy(roots.at[pl.ds((1 - core) * groups, groups), capacity + slot], lower, sems.at[2]),
        pltpu.make_async_copy(roots.at[:, slot], left, sems.at[3]),
    ]
    for load in loads:
        load.start()
    loads[0].wait()
    grad = own[...]
    grad_sq[...] = jnp.full(grad_sq.shape, jnp.sum(jnp.square(grad.astype(F32))), F32)
    loads[1].wait()
    partial[...] = dot(grad, upper[...].reshape(half, 2 * half), ((1,), (0,)))
    loads[2].wait()
    loads[3].wait()


def direction_kernel(table, other, partial, left, lower, grad_sq_near, out):
    core = table[WHERE, 0]
    half = other.shape[1]
    size = 2 * half
    grad = other[...]
    grad_sq = grad_sq_near[0:1, 0:1] + jnp.full((1, 1), jnp.sum(jnp.square(grad.astype(F32))), F32)
    left_mat = left[...].reshape(size, size)

    def columns(h):
        cols = pl.ds(pl.multiple_of(h * half, 128), half)
        shaped = partial[:, cols] + dot(grad, lower[:, :, cols].reshape(half, half), ((1,), (0,)))
        return dot(left_mat, shaped.astype(BF16), ((1,), (0,)))

    dir_sq = jnp.sum(jnp.square(columns(1 - core)))
    near = columns(core)
    dir_sq = jnp.full((1, 1), dir_sq + jnp.sum(jnp.square(near)), F32)
    ratio = jnp.sqrt(grad_sq) / jnp.sqrt(dir_sq + NORM_EPS)
    out[...] = (-near * ratio).astype(BF16)


def stats_kernel(table, grads_hbm, left, right, left_hbm, right_hbm, grads, left_out, right_out, sems, out_sems):
    core, x = table[WHERE, 0], table[WHERE, 1]
    capacity, rows, _ = left.shape
    half = grads.shape[3]
    loads = [
        pltpu.make_async_copy(grads_hbm.at[table[CHIP, j]], grads.at[j], sems.at[j]) for j in range(capacity)
    ]
    stores = []
    for load in loads:
        load.start()
    for j in range(capacity):
        full = table[FULL, j] > 0
        loads[j].wait()

        @pl.when(full)
        def _():
            g0 = grads[j, 0]
            g1 = grads[j, 1]
            own = pl.ds(pl.multiple_of((2 * x + core) * rows, 16), rows)
            term = dot(grads[j, 0, own], g0, ((1,), (1,))) + dot(grads[j, 1, own], g1, ((1,), (1,)))
            left_out[j] = STAT_DECAY * left[j] + (1.0 - STAT_DECAY) * term
            cols = grads[j, x // 2, :, pl.ds(pl.multiple_of((x % 2) * 2 * rows, 128), 2 * rows)]
            for h, g in ((0, g0), (1, g1)):
                prod = dot(cols, g, ((0,), (0,)))
                term = jnp.where(core == 0, prod[:rows], prod[rows:])
                at_cols = pl.ds(h * half, half)
                right_out[j, :, at_cols] = STAT_DECAY * right[j, :, at_cols] + (1.0 - STAT_DECAY) * term

        @pl.when(jnp.logical_not(full))
        def _():
            left_out[j] = STAT_DECAY * left[j]
            right_out[j] = STAT_DECAY * right[j]

        stores.append(pltpu.make_async_copy(left_out.at[j], left_hbm.at[j], out_sems.at[0, j]))
        stores.append(pltpu.make_async_copy(right_out.at[j], right_hbm.at[j], out_sems.at[1, j]))
        stores[-2].start()
        stores[-1].start()
    for store in stores:
        store.wait()


def compact_kernel(table, rows, out):
    def body(i, carry):
        block = rows[table[OWNER, i]]
        for x in range(out.shape[0]):
            out[x, i] = block
        return carry

    lax.fori_loop(0, out.shape[1], body, 0, unroll=8)


def place_half(core, table, rows, out_hbm, ordered, sems):
    steps = sems.shape[0]
    step = rows.shape[0] // steps
    width = rows.shape[2]
    cols = pl.ds(pl.multiple_of(core * width, 128), width)
    stores = []
    for i in range(steps):

        def body(b, carry):
            ordered[i * step + b] = rows[table[SOURCE, i * step + b]]
            return carry

        lax.fori_loop(0, step, body, 0, unroll=8)
        part = pl.ds(i * step, step)
        stores.append(pltpu.make_async_copy(ordered.at[part], out_hbm.at[part, :, cols], sems.at[i]))
        stores[-1].start()
    for store in stores:
        store.wait()


def place_near_kernel(table, rows, out_hbm, ordered, sems):
    place_half(table[WHERE, 0], table, rows, out_hbm, ordered, sems)


def place_far_kernel(table, rows, begun, out_hbm, ordered, sems):
    del begun
    place_half(1 - table[WHERE, 0], table, rows, out_hbm, ordered, sems)


def call(kernel, out_shape, in_specs, scratch=()):
    return pl.pallas_call(
        kernel,
        out_shape=out_shape,
        in_specs=in_specs,
        out_specs=VMEM_SPEC,
        scratch_shapes=list(scratch),
        compiler_params=PARAMS,
    )


def exchange(value, axis):
    return lax.all_to_all(value, axis, 0, 0, tiled=True)


def in_hbm(value):
    return pltpu.with_memory_space_constraint(value, pltpu.HBM)


def swap_cores(value):
    return lax.ppermute(value, "core", [(0, 1), (1, 0)])


def local(grads, block_slot, left_stat, right_stat, left_root, right_root):
    grads = grads[0]
    chips = lax.axis_size("x")
    x = lax.axis_index("x")
    core = lax.axis_index("core")
    owners = lax.axis_size("y") * lax.axis_size("z")
    me = lax.axis_index("y") * lax.axis_size("z") + lax.axis_index("z")
    capacity, stat_rows, _ = left_stat.shape
    blocks, shard_rows, width = grads.shape
    half = width // 2
    depth = blocks // chips

    kept, sent, roots, table = pl.pallas_call(
        functools.partial(split_kernel, chips),
        out_shape=[
            jax.ShapeDtypeStruct((blocks, shard_rows, half), BF16),
            jax.ShapeDtypeStruct((blocks, shard_rows, half), BF16),
            jax.ShapeDtypeStruct((2 * capacity, stat_rows, width), BF16),
            jax.ShapeDtypeStruct((8, blocks), jnp.int32),
        ],
        in_specs=[SMEM_SPEC] * 3 + [VMEM_SPEC] + [HBM_SPEC] * 3,
        out_specs=[VMEM_SPEC, VMEM_SPEC, HBM_SPEC, VMEM_SPEC],
        scratch_shapes=[
            pltpu.VMEM((2 * capacity, stat_rows, width), BF16),
            pltpu.SemaphoreType.DMA((5,)),
        ],
        compiler_params=PARAMS,
    )(
        core.reshape(1),
        x.reshape(1),
        me.reshape(1),
        block_slot.reshape(1, blocks),
        in_hbm(grads),
        in_hbm(left_root),
        in_hbm(right_root),
    )
    other = swap_cores(sent)
    roots = lax.all_gather(roots, ("x", "core"), axis=0)

    parts = call(
        pair_sum_kernel,
        jax.ShapeDtypeStruct((chips, depth, shard_rows, half), BF16),
        [SMEM_SPEC, VMEM_SPEC, VMEM_SPEC],
    )(table, kept, other)
    parts = exchange(parts, "x")
    outgoing = call(
        chip_sum_kernel,
        jax.ShapeDtypeStruct((owners, shard_rows, half), BF16),
        [SMEM_SPEC, VMEM_SPEC],
        [pltpu.VMEM((depth + 1, shard_rows, half), BF16)],
    )(table, parts)
    own = exchange(outgoing, ("y", "z")).reshape(width, half)
    far = swap_cores(own)
    grads_all = lax.all_gather(own, ("x", "core"), axis=0)

    groups = width // stat_rows
    partial, left, lower, grad_sq = pl.pallas_call(
        near_kernel,
        out_shape=[
            jax.ShapeDtypeStruct((width, width), F32),
            jax.ShapeDtypeStruct((groups, stat_rows, width), BF16),
            jax.ShapeDtypeStruct((groups // 2, stat_rows, width), BF16),
            jax.ShapeDtypeStruct((8, 128), F32),
        ],
        in_specs=[SMEM_SPEC, HBM_SPEC, HBM_SPEC],
        out_specs=[VMEM_SPEC] * 4,
        scratch_shapes=[
            pltpu.VMEM((width, half), BF16),
            pltpu.VMEM((groups // 2, stat_rows, width), BF16),
            pltpu.SemaphoreType.DMA((4,)),
        ],
        compiler_params=PARAMS,
        cost_estimate=pl.CostEstimate(flops=270_000_000, bytes_accessed=4_000_000, transcendentals=0),
    )(table, in_hbm(own), in_hbm(roots))
    update = call(
        direction_kernel,
        jax.ShapeDtypeStruct((width, half), BF16),
        [SMEM_SPEC] + [VMEM_SPEC] * 5,
    )(table, far, partial, left, lower, grad_sq)

    rows = exchange(update.reshape(owners, shard_rows, half), ("y", "z"))
    packed = call(
        compact_kernel,
        jax.ShapeDtypeStruct((chips, depth, shard_rows, half), BF16),
        [SMEM_SPEC, VMEM_SPEC],
    )(table, rows)
    packed, grads_all = lax.optimization_barrier((packed, grads_all))
    near = exchange(packed, "x").reshape(blocks, shard_rows, half)

    left_new, right_new = pl.pallas_call(
        stats_kernel,
        out_shape=[jax.ShapeDtypeStruct(left_stat.shape, F32), jax.ShapeDtypeStruct(right_stat.shape, F32)],
        in_specs=[SMEM_SPEC, HBM_SPEC, VMEM_SPEC, VMEM_SPEC],
        out_specs=[HBM_SPEC, HBM_SPEC],
        scratch_shapes=[
            pltpu.VMEM((capacity, 2, width, half), BF16),
            pltpu.VMEM(left_stat.shape, F32),
            pltpu.VMEM(right_stat.shape, F32),
            pltpu.SemaphoreType.DMA((capacity,)),
            pltpu.SemaphoreType.DMA((2, capacity)),
        ],
        compiler_params=PARAMS,
        cost_estimate=pl.CostEstimate(flops=400_000_000, bytes_accessed=6_000_000, transcendentals=0),
    )(table, in_hbm(grads_all.reshape(chips, 2, width, half)), left_stat, right_stat)

    near, left_new, right_new = lax.optimization_barrier((near, left_new, right_new))
    beyond = swap_cores(near)
    scratch = [pltpu.VMEM((blocks, shard_rows, half), BF16), pltpu.SemaphoreType.DMA((4,))]
    begun = pl.pallas_call(
        place_near_kernel,
        out_shape=jax.ShapeDtypeStruct((blocks, shard_rows, width), BF16),
        in_specs=[SMEM_SPEC, VMEM_SPEC],
        out_specs=HBM_SPEC,
        scratch_shapes=scratch,
        compiler_params=PARAMS,
        cost_estimate=pl.CostEstimate(flops=0, bytes_accessed=4_000_000, transcendentals=0),
    )(table, near)
    result = pl.pallas_call(
        place_far_kernel,
        out_shape=jax.ShapeDtypeStruct((blocks, shard_rows, width), BF16),
        in_specs=[SMEM_SPEC, VMEM_SPEC, HBM_SPEC],
        out_specs=HBM_SPEC,
        scratch_shapes=scratch,
        input_output_aliases={2: 0},
        compiler_params=PARAMS,
    )(table, beyond, begun)
    return (result, left_new, right_new)


def solution(mesh):
    fine = Mesh(mesh.devices.reshape(4, 2, 4, 16), ("x", "core", "y", "z"))
    replica, shard = ("x", "core"), ("y", "z")
    in_specs = (
        P(replica, None, shard, None),
        P(),
        P(shard, replica, None),
        P(shard, replica, None),
        P(shard, replica, None),
        P(shard, replica, None),
    )
    out_specs = (P(None, shard, None), P(shard, replica, None), P(shard, replica, None))
    return jax.shard_map(local, mesh=fine, in_specs=in_specs, out_specs=out_specs, check_vma=False)
```

```python
import functools

import jax
import jax.numpy as jnp
from jax import lax
from jax.experimental import pallas as pl
from jax.experimental.pallas import tpu as pltpu
from jax.sharding import Mesh, PartitionSpec as P

STAT_DECAY = 0.9
NORM_EPS = 1e-12
F32 = jnp.float32
BF16 = jnp.bfloat16
VMEM_SPEC = pl.BlockSpec(memory_space=pltpu.VMEM)
HBM_SPEC = pl.BlockSpec(memory_space=pltpu.HBM)
SMEM_SPEC = pl.BlockSpec(memory_space=pltpu.SMEM)
PARAMS = pltpu.CompilerParams(vmem_limit_bytes=32 * 1024 * 1024)


def dot(a, b, dims):
    return lax.dot_general(a, b, (dims, ((), ())), preferred_element_type=F32)


ORDER, SOURCE, PLACE, OWNER, SLOT, FULL, CHIP, WHERE = range(8)


def fill_table(slots, core, x, me, capacity, chips, table):
    blocks = slots.shape[1]
    square = (blocks, blocks)
    cap_bits, chip_bits = capacity.bit_length() - 1, chips.bit_length() - 1
    depth = blocks // chips
    lane = lax.broadcasted_iota(jnp.int32, square, 1)
    sublane = lax.broadcasted_iota(jnp.int32, square, 0)
    across = jnp.broadcast_to(slots[...], square)
    slot = across.T

    def total(mask, value):
        return jnp.sum(jnp.where(mask, value, 0), axis=0, keepdims=True)

    rank_row = total(slot < across, 1)
    rank = jnp.broadcast_to(rank_row, square).T
    chip = rank & (chips - 1)
    spot = rank >> chip_bits
    owner = slot >> cap_bits
    local_slot = slot == me * capacity + lane
    table[pl.ds(ORDER, 1)] = total(rank == lane, sublane)
    table[pl.ds(SOURCE, 1)] = (rank_row & (chips - 1)) * depth + (rank_row >> chip_bits)
    table[pl.ds(PLACE, 1)] = total((chip == x) & (owner == lane), spot - depth) + depth
    table[pl.ds(OWNER, 1)] = total((chip == x) & (spot == lane), owner)
    table[pl.ds(SLOT, 1)] = total((owner == me) & (chip == lane), slot & (capacity - 1))
    table[pl.ds(FULL, 1)] = total(local_slot, 1)
    table[pl.ds(CHIP, 1)] = total(local_slot, chip)
    row = lax.broadcasted_iota(jnp.int32, (1, blocks), 1)
    table[pl.ds(WHERE, 1)] = jnp.where(row == 0, core, x)


def send_kernel(core_ref, grads, sent, sem):
    width = sent.shape[2]
    far = pl.ds(pl.multiple_of((1 - core_ref[0]) * width, 128), width)
    load = pltpu.make_async_copy(grads.at[:, :, far], sent, sem)
    load.start()
    load.wait()


def keep_kernel(chips, capacity, core_ref, x_ref, me_ref, slots_hbm, grads, kept, table, slots, sems):
    core = core_ref[0]
    width = kept.shape[2]
    near = pl.ds(pl.multiple_of(core * width, 128), width)
    slots_load = pltpu.make_async_copy(slots_hbm, slots, sems.at[0])
    load = pltpu.make_async_copy(grads.at[:, :, near], kept, sems.at[1])
    slots_load.start()
    load.start()
    slots_load.wait()
    fill_table(slots, core, x_ref[0], me_ref[0], capacity, chips, table)
    load.wait()


def select_roots_kernel(table, left_root, right_root, *refs):
    pieces, sems = refs[:-1], refs[-1]
    chips = len(pieces)
    loads = []
    for k, piece in enumerate(pieces):
        slot = table[SLOT, lax.rem(table[WHERE, 1] + k, chips)]
        for side, root in enumerate((left_root, right_root)):
            loads.append(pltpu.make_async_copy(root.at[slot], piece.at[side], sems.at[k, side]))
            loads[-1].start()
    for load in loads:
        load.wait()


def order_roots_kernel(table, *refs):
    pieces, out = refs[:-1], refs[-1]
    chips = len(pieces)
    for k, piece in enumerate(pieces):
        out[lax.rem(table[WHERE, 1] + chips - k, chips)] = piece[...]


def merge_roots_kernel(table, mine, others, left, right):
    core = table[WHERE, 0]
    for x in range(mine.shape[0]):
        left[2 * x + core] = mine[x, 0]
        right[2 * x + core] = mine[x, 1]
        left[2 * x + 1 - core] = others[x, 0]
        right[2 * x + 1 - core] = others[x, 1]


def pair_sum_kernel(table, own, other, out):
    chips, depth = out.shape[:2]

    def body(i, carry):
        for x in range(chips):
            block = table[ORDER, i * chips + x]
            out[x, i] = own[block] + other[block]
        return carry

    lax.fori_loop(0, depth, body, 0, unroll=8)


def chip_sum_kernel(table, parts, out, total):
    depth = parts.shape[1]
    acc = parts[0].astype(F32)
    for x in range(1, parts.shape[0]):
        acc = acc + parts[x].astype(F32)
    total[0:depth] = acc.astype(BF16)
    total[depth] = jnp.zeros(total.shape[1:], BF16)

    def body(o, carry):
        out[o] = total[table[PLACE, o]]
        return carry

    lax.fori_loop(0, out.shape[0], body, 0, unroll=8)


def near_kernel(table, own, right, partial, grad_sq):
    core = table[WHERE, 0]
    half = own.shape[1]
    groups = right.shape[0] // 2
    grad = own[...]
    grad_sq[...] = jnp.full(grad_sq.shape, jnp.sum(jnp.square(grad.astype(F32))), F32)
    upper = right[pl.ds(core * groups, groups)].reshape(half, 2 * half)
    partial[...] = dot(grad, upper, ((1,), (0,)))


def direction_kernel(table, other, partial, left, right, grad_sq_near, out):
    core = table[WHERE, 0]
    half = other.shape[1]
    groups = right.shape[0] // 2
    size = 2 * half
    grad = other[...]
    grad_sq = grad_sq_near[0:1, 0:1] + jnp.full((1, 1), jnp.sum(jnp.square(grad.astype(F32))), F32)
    left_mat = left[...].reshape(size, size)

    def columns(h):
        cols = pl.ds(pl.multiple_of(h * half, 128), half)
        lower = right[pl.ds((1 - core) * groups, groups), :, cols].reshape(half, half)
        shaped = partial[:, cols] + dot(grad, lower, ((1,), (0,)))
        return dot(left_mat, shaped.astype(BF16), ((1,), (0,)))

    dir_sq = jnp.sum(jnp.square(columns(1 - core)))
    near = columns(core)
    dir_sq = jnp.full((1, 1), dir_sq + jnp.sum(jnp.square(near)), F32)
    ratio = jnp.sqrt(grad_sq) / jnp.sqrt(dir_sq + NORM_EPS)
    out[...] = (-near * ratio).astype(BF16)


def terms_kernel(table, own, other, *refs):
    pieces, grad = refs[:-1], refs[-1]
    core, x = table[WHERE, 0], table[WHERE, 1]
    chips = len(pieces)
    half = own.shape[1]
    rows = pieces[0].shape[1]
    grad[:, pl.ds(pl.multiple_of(core * half, 128), half)] = own[...]
    grad[:, pl.ds(pl.multiple_of((1 - core) * half, 128), half)] = other[...]
    whole = grad[...]
    for k, piece in enumerate(pieces):
        chip = lax.rem(x + k, chips)
        some = grad[pl.ds(pl.multiple_of((2 * chip + core) * rows, 16), rows)]
        piece[0] = dot(some, whole, ((1,), (1,))).astype(BF16)
        cols = grad[:, pl.ds(pl.multiple_of(chip * 2 * rows, 128), 2 * rows)]
        both = dot(cols, whole, ((0,), (0,)))
        piece[1] = jnp.where(core == 0, both[:rows], both[rows:]).astype(BF16)


def stats_kernel(table, *refs):
    pieces = refs[:-8]
    left_hbm, right_hbm, left_new_hbm, right_new_hbm, stats, results, sems, out_sems = refs[-8:]
    chips = len(pieces)
    capacity = left_hbm.shape[0]
    loads = []
    for j in range(capacity):
        for side, source in enumerate((left_hbm, right_hbm)):
            loads.append(pltpu.make_async_copy(source.at[j], stats.at[j, side], sems.at[j, side]))
            loads[-1].start()
    stores = []
    for j in range(capacity):
        full = table[FULL, j] > 0
        k = lax.rem(table[WHERE, 1] + chips - table[CHIP, j], chips)
        loads[2 * j].wait()
        loads[2 * j + 1].wait()
        for other, piece in enumerate(pieces):

            @pl.when(jnp.logical_and(full, k == other))
            def _():
                results[j] = STAT_DECAY * stats[j] + (1.0 - STAT_DECAY) * piece[...].astype(F32)

        @pl.when(jnp.logical_not(full))
        def _():
            results[j] = STAT_DECAY * stats[j]

        for side, target in enumerate((left_new_hbm, right_new_hbm)):
            stores.append(pltpu.make_async_copy(results.at[j, side], target.at[j], out_sems.at[j, side]))
            stores[-1].start()
    for store in stores:
        store.wait()


def compact_kernel(table, rows, out):
    def body(i, carry):
        block = rows[table[OWNER, i]]
        for x in range(out.shape[0]):
            out[x, i] = block
        return carry

    lax.fori_loop(0, out.shape[1], body, 0, unroll=8)


def place_half(core, table, rows, out_hbm, ordered, sems):
    steps = sems.shape[0]
    step = rows.shape[0] // steps
    width = rows.shape[2]
    cols = pl.ds(pl.multiple_of(core * width, 128), width)
    stores = []
    for i in range(steps):

        def body(b, carry):
            ordered[i * step + b] = rows[table[SOURCE, i * step + b]]
            return carry

        lax.fori_loop(0, step, body, 0, unroll=8)
        part = pl.ds(i * step, step)
        stores.append(pltpu.make_async_copy(ordered.at[part], out_hbm.at[part, :, cols], sems.at[i]))
        stores[-1].start()
    for store in stores:
        store.wait()


def place_near_kernel(table, rows, out_hbm, ordered, sems):
    place_half(table[WHERE, 0], table, rows, out_hbm, ordered, sems)


def place_far_kernel(table, rows, begun, out_hbm, ordered, sems):
    del begun
    place_half(1 - table[WHERE, 0], table, rows, out_hbm, ordered, sems)


def call(kernel, out_shape, in_specs, scratch=(), out_specs=None, cost=None, aliases=None):
    if out_specs is None:
        out_specs = [VMEM_SPEC] * len(out_shape) if isinstance(out_shape, list) else VMEM_SPEC
    if cost is not None:
        cost = pl.CostEstimate(flops=cost[0], bytes_accessed=cost[1], transcendentals=0)
    return pl.pallas_call(
        kernel,
        out_shape=out_shape,
        in_specs=in_specs,
        out_specs=out_specs,
        scratch_shapes=list(scratch),
        input_output_aliases=aliases or {},
        compiler_params=PARAMS,
        cost_estimate=cost,
    )


def exchange(value, axis):
    return lax.all_to_all(value, axis, 0, 0, tiled=True)


def in_hbm(value):
    return pltpu.with_memory_space_constraint(value, pltpu.HBM)


def turn(value, k):
    chips = lax.axis_size("x")
    return lax.ppermute(value, "x", [(i, (i + k) % chips) for i in range(chips)]) if k else value


def swap_cores(value):
    return lax.ppermute(value, "core", [(0, 1), (1, 0)])


def local(grads, block_slot, left_stat, right_stat, left_root, right_root):
    grads = grads[0]
    chips = lax.axis_size("x")
    x = lax.axis_index("x")
    core = lax.axis_index("core")
    owners = lax.axis_size("y") * lax.axis_size("z")
    me = lax.axis_index("y") * lax.axis_size("z") + lax.axis_index("z")
    capacity, stat_rows, _ = left_stat.shape
    blocks, shard_rows, width = grads.shape
    half = width // 2
    depth = blocks // chips

    piece = jax.ShapeDtypeStruct((2, stat_rows, width), BF16)
    groups = width // stat_rows
    half_rows = jax.ShapeDtypeStruct((blocks, shard_rows, half), BF16)
    grads = in_hbm(grads)

    sent = call(send_kernel, half_rows, [SMEM_SPEC, HBM_SPEC], [pltpu.SemaphoreType.DMA])(core.reshape(1), grads)
    sent, late_grads = lax.optimization_barrier((sent, grads))
    other = swap_cores(sent)
    kept, table = call(
        functools.partial(keep_kernel, chips, capacity),
        [half_rows, jax.ShapeDtypeStruct((8, blocks), jnp.int32)],
        [SMEM_SPEC] * 3 + [HBM_SPEC] * 2,
        [pltpu.VMEM((1, blocks), jnp.int32), pltpu.SemaphoreType.DMA((2,))],
        cost=(0, 4_000_000),
    )(core.reshape(1), x.reshape(1), me.reshape(1), in_hbm(block_slot.reshape(1, blocks)), in_hbm(late_grads))

    parts = call(
        pair_sum_kernel,
        jax.ShapeDtypeStruct((chips, depth, shard_rows, half), BF16),
        [SMEM_SPEC, VMEM_SPEC, VMEM_SPEC],
    )(table, kept, other)
    parts = exchange(parts, "x")
    outgoing = call(
        chip_sum_kernel,
        jax.ShapeDtypeStruct((owners, shard_rows, half), BF16),
        [SMEM_SPEC, VMEM_SPEC],
        [pltpu.VMEM((depth + 1, shard_rows, half), BF16)],
    )(table, parts)

    outgoing, late_table = lax.optimization_barrier((outgoing, table))
    own = exchange(outgoing, ("y", "z"))
    pieces = call(
        select_roots_kernel,
        [piece] * chips,
        [SMEM_SPEC, HBM_SPEC, HBM_SPEC],
        [pltpu.SemaphoreType.DMA((chips, 2))],
        cost=(0, 2_000_000),
    )(late_table, in_hbm(left_root), in_hbm(right_root))
    pieces = [turn(value, k) for k, value in enumerate(pieces)]
    mine = call(
        order_roots_kernel,
        jax.ShapeDtypeStruct((chips, 2, stat_rows, width), BF16),
        [SMEM_SPEC] + [VMEM_SPEC] * chips,
        cost=(0, 1_000_000),
    )(late_table, *pieces)
    others = swap_cores(mine)
    left, right = call(
        merge_roots_kernel,
        [jax.ShapeDtypeStruct((groups, stat_rows, width), BF16)] * 2,
        [SMEM_SPEC, VMEM_SPEC, VMEM_SPEC],
        cost=(0, 2_000_000),
    )(late_table, mine, others)
    own, left, right = lax.optimization_barrier((own, left, right))

    own = own.reshape(width, half)
    far = swap_cores(own)
    partial, grad_sq = call(
        near_kernel,
        [jax.ShapeDtypeStruct((width, width), F32), jax.ShapeDtypeStruct((8, 128), F32)],
        [SMEM_SPEC, VMEM_SPEC, VMEM_SPEC],
        cost=(270_000_000, 4_000_000),
    )(table, own, right)
    update = call(
        direction_kernel,
        jax.ShapeDtypeStruct((width, half), BF16),
        [SMEM_SPEC] + [VMEM_SPEC] * 5,
    )(table, far, partial, left, right, grad_sq)

    update, own, far = lax.optimization_barrier((update, own, far))
    rows = exchange(update.reshape(owners, shard_rows, half), ("y", "z"))
    pieces = call(
        terms_kernel,
        [piece] * chips,
        [SMEM_SPEC, VMEM_SPEC, VMEM_SPEC],
        [pltpu.VMEM((width, width), BF16)],
        cost=(800_000_000, 2_000_000),
    )(table, own, far)
    pieces = [turn(value, k) for k, value in enumerate(pieces)]
    stat = jax.ShapeDtypeStruct(left_stat.shape, F32)
    both_stats = (capacity, 2, stat_rows, width)
    left_new, right_new = call(
        stats_kernel,
        [stat, stat],
        [SMEM_SPEC] + [VMEM_SPEC] * chips + [HBM_SPEC] * 2,
        [
            pltpu.VMEM(both_stats, F32),
            pltpu.VMEM(both_stats, F32),
            pltpu.SemaphoreType.DMA((capacity, 2)),
            pltpu.SemaphoreType.DMA((capacity, 2)),
        ],
        [HBM_SPEC, HBM_SPEC],
        cost=(10_000_000, 5_000_000),
    )(table, *pieces, in_hbm(left_stat), in_hbm(right_stat))
    rows, left_new, right_new = lax.optimization_barrier((rows, left_new, right_new))

    packed = call(
        compact_kernel,
        jax.ShapeDtypeStruct((chips, depth, shard_rows, half), BF16),
        [SMEM_SPEC, VMEM_SPEC],
    )(table, rows)
    near = exchange(packed, "x").reshape(blocks, shard_rows, half)
    beyond = swap_cores(near)
    whole_rows = jax.ShapeDtypeStruct((blocks, shard_rows, width), BF16)
    scratch = [pltpu.VMEM((blocks, shard_rows, half), BF16), pltpu.SemaphoreType.DMA((4,))]
    begun = call(
        place_near_kernel, whole_rows, [SMEM_SPEC, VMEM_SPEC], scratch, HBM_SPEC, cost=(0, 4_000_000)
    )(table, near)
    result = call(
        place_far_kernel, whole_rows, [SMEM_SPEC, VMEM_SPEC, HBM_SPEC], scratch, HBM_SPEC, aliases={2: 0}
    )(table, beyond, begun)
    return (result, left_new, right_new)


def solution(mesh):
    fine = Mesh(mesh.devices.reshape(4, 2, 4, 16), ("x", "core", "y", "z"))
    replica, shard = ("x", "core"), ("y", "z")
    in_specs = (
        P(replica, None, shard, None),
        P(),
        P(shard, replica, None),
        P(shard, replica, None),
        P(shard, replica, None),
        P(shard, replica, None),
    )
    out_specs = (P(None, shard, None), P(shard, replica, None), P(shard, replica, None))
    return jax.shard_map(local, mesh=fine, in_specs=in_specs, out_specs=out_specs, check_vma=False)
```

```python
import functools

import jax
import jax.numpy as jnp
from jax import lax
from jax.experimental import pallas as pl
from jax.experimental.pallas import tpu as pltpu
from jax.sharding import Mesh, PartitionSpec as P

STAT_DECAY = 0.9
NORM_EPS = 1e-12
F32 = jnp.float32
BF16 = jnp.bfloat16
VMEM_SPEC = pl.BlockSpec(memory_space=pltpu.VMEM)
HBM_SPEC = pl.BlockSpec(memory_space=pltpu.HBM)
SMEM_SPEC = pl.BlockSpec(memory_space=pltpu.SMEM)
PARAMS = pltpu.CompilerParams(vmem_limit_bytes=32 * 1024 * 1024)


def dot(a, b, dims):
    return lax.dot_general(a, b, (dims, ((), ())), preferred_element_type=F32)


ORDER, SOURCE, PLACE, OWNER, SLOT, FULL, CHIP, WHERE = range(8)


def fill_table(slots, core, x, me, capacity, chips, table):
    blocks = slots.shape[1]
    square = (blocks, blocks)
    cap_bits, chip_bits = capacity.bit_length() - 1, chips.bit_length() - 1
    depth = blocks // chips
    lane = lax.broadcasted_iota(jnp.int32, square, 1)
    sublane = lax.broadcasted_iota(jnp.int32, square, 0)
    across = jnp.broadcast_to(slots[...], square)
    slot = across.T

    def total(mask, value):
        return jnp.sum(jnp.where(mask, value, 0), axis=0, keepdims=True)

    rank_row = total(slot < across, 1)
    rank = jnp.broadcast_to(rank_row, square).T
    chip = rank & (chips - 1)
    spot = rank >> chip_bits
    owner = slot >> cap_bits
    local_slot = slot == me * capacity + lane
    table[pl.ds(ORDER, 1)] = total(rank == lane, sublane)
    table[pl.ds(SOURCE, 1)] = (rank_row & (chips - 1)) * depth + (rank_row >> chip_bits)
    table[pl.ds(PLACE, 1)] = total((chip == x) & (owner == lane), spot - depth) + depth
    table[pl.ds(OWNER, 1)] = total((chip == x) & (spot == lane), owner)
    table[pl.ds(SLOT, 1)] = total((owner == me) & (chip == lane), slot & (capacity - 1))
    table[pl.ds(FULL, 1)] = total(local_slot, 1)
    table[pl.ds(CHIP, 1)] = total(local_slot, chip)
    row = lax.broadcasted_iota(jnp.int32, (1, blocks), 1)
    table[pl.ds(WHERE, 1)] = jnp.where(row == 0, core, x)


def send_kernel(core_ref, grads, left_root, right_root, sent, sems):
    width = sent.shape[2]
    groups = grads.shape[0]
    capacity = left_root.shape[0]
    far = pl.ds(pl.multiple_of((1 - core_ref[0]) * width, 128), width)
    loads = [pltpu.make_async_copy(grads.at[:, :, far], sent.at[pl.ds(0, groups)], sems.at[0])]
    for i in range(4):
        root = (left_root, right_root)[i // 2].at[:, :, pl.ds(i % 2 * width, width)]
        loads.append(pltpu.make_async_copy(root, sent.at[pl.ds(groups + i * capacity, capacity)], sems.at[i + 1]))
    for load in loads:
        load.start()
    for load in loads:
        load.wait()


def keep_kernel(chips, capacity, core_ref, x_ref, me_ref, slots_hbm, grads, kept, table, slots, sems):
    core = core_ref[0]
    width = kept.shape[2]
    near = pl.ds(pl.multiple_of(core * width, 128), width)
    slots_load = pltpu.make_async_copy(slots_hbm, slots, sems.at[0])
    load = pltpu.make_async_copy(grads.at[:, :, near], kept, sems.at[1])
    slots_load.start()
    load.start()
    slots_load.wait()
    fill_table(slots, core, x_ref[0], me_ref[0], capacity, chips, table)
    load.wait()


def select_roots_kernel(groups, table, other, left_root, right_root, beside, across, mine, sems):
    core, x = table[WHERE, 0], table[WHERE, 1]
    capacity = left_root.shape[0]
    width = other.shape[2]
    loads = []
    for i, (chip, out) in enumerate(((lax.rem(x + 1 + 2 * core, 4), beside), (x, mine), (lax.rem(x + 2, 4), across))):
        slot = table[SLOT, chip]
        target = across if i == 2 else out.at[core]
        for side, root in enumerate((left_root, right_root)):
            loads.append(pltpu.make_async_copy(root.at[slot], target.at[side], sems.at[i, side]))
            loads[-1].start()
    for chip, out in ((lax.rem(x + 1 + 2 * core, 4), beside), (x, mine)):
        slot = table[SLOT, chip]
        for i in range(4):
            out[1 - core, i // 2, :, i % 2 * width : (i % 2 + 1) * width] = other[groups + i * capacity + slot]
    for load in loads:
        load.wait()


def stack_kernel(beside, across, out):
    out[0:2] = beside[...]
    out[2] = across[...]


def merge_roots_kernel(table, mine, beside, across, others, left, right):
    core, x = table[WHERE, 0], table[WHERE, 1]
    near, far, opposite = lax.rem(x + 3 - 2 * core, 4), lax.rem(x + 1 + 2 * core, 4), lax.rem(x + 2, 4)
    for side, out in enumerate((left, right)):
        for parity in range(2):
            out[2 * x + parity] = mine[parity, side]
            out[2 * near + parity] = beside[parity, side]
            out[2 * far + parity] = others[parity, side]
        out[2 * opposite + core] = across[side]
        out[2 * opposite + 1 - core] = others[2, side]


def pair_sum_kernel(table, own, other, out):
    chips, depth = out.shape[:2]

    def body(i, carry):
        for x in range(chips):
            block = table[ORDER, i * chips + x]
            out[x, i] = own[block] + other[block]
        return carry

    lax.fori_loop(0, depth, body, 0, unroll=8)


def store_in_steps(source, target, sems, dim, fill):
    steps = sems.shape[0]
    count = source.shape[dim] // steps
    stores = []
    for i in range(steps):
        fill(i * count, count)
        part = (slice(None),) * dim + (pl.ds(i * count, count),)
        stores.append(pltpu.make_async_copy(source.at[part], target.at[part], sems.at[i]))
        stores[-1].start()
    for store in stores:
        store.wait()


def chip_sum_kernel(table, parts, out, total):
    depth = parts.shape[1]
    acc = parts[0].astype(F32)
    for x in range(1, parts.shape[0]):
        acc = acc + parts[x].astype(F32)
    total[0:depth] = acc.astype(BF16)
    total[depth] = jnp.zeros(total.shape[1:], BF16)

    def body(o, carry):
        out[o] = total[table[PLACE, o]]
        return carry

    lax.fori_loop(0, out.shape[0], body, 0, unroll=8)


def near_kernel(table, own, right, partial, grad_sq):
    core = table[WHERE, 0]
    half = own.shape[1]
    groups = right.shape[0] // 2
    grad = own[...]
    grad_sq[...] = jnp.full(grad_sq.shape, jnp.sum(jnp.square(grad.astype(F32))), F32)
    upper = right[pl.ds(core * groups, groups)].reshape(half, 2 * half)
    partial[...] = dot(grad, upper, ((1,), (0,)))


def direction_kernel(table, other, partial, left, right, grad_sq_near, out):
    core = table[WHERE, 0]
    half = other.shape[1]
    groups = right.shape[0] // 2
    size = 2 * half
    grad = other[...]
    grad_sq = grad_sq_near[0:1, 0:1] + jnp.full((1, 1), jnp.sum(jnp.square(grad.astype(F32))), F32)
    left_mat = left[...].reshape(size, size)

    def columns(h):
        cols = pl.ds(pl.multiple_of(h * half, 128), half)
        lower = right[pl.ds((1 - core) * groups, groups), :, cols].reshape(half, half)
        shaped = partial[:, cols] + dot(grad, lower, ((1,), (0,)))
        return dot(left_mat, shaped.astype(BF16), ((1,), (0,)))

    dir_sq = jnp.sum(jnp.square(columns(1 - core)))
    near = columns(core)
    dir_sq = jnp.full((1, 1), dir_sq + jnp.sum(jnp.square(near)), F32)
    ratio = jnp.sqrt(grad_sq) / jnp.sqrt(dir_sq + NORM_EPS)
    out[...] = (-near * ratio).astype(BF16)


def terms_kernel(table, own, other, beside, across, mine, grad):
    core, x = table[WHERE, 0], table[WHERE, 1]
    half = own.shape[1]
    rows = mine.shape[1]
    grad[:, pl.ds(pl.multiple_of(core * half, 128), half)] = own[...]
    grad[:, pl.ds(pl.multiple_of((1 - core) * half, 128), half)] = other[...]
    whole = grad[...]

    def of_chip(chip):
        at = pl.ds(pl.multiple_of(chip * 2 * rows, 128), 2 * rows)
        return dot(grad[at], whole, ((1,), (1,))), dot(grad[:, at], whole, ((0,), (0,)))

    for side, term in enumerate(of_chip(lax.rem(x + 1 + 2 * core, 4))):
        for parity in range(2):
            beside[parity, side] = term[parity * rows : (parity + 1) * rows].astype(BF16)
    for chip, out in ((lax.rem(x + 2, 4), across), (x, mine)):
        for side, term in enumerate(of_chip(chip)):
            out[side] = jnp.where(core == 0, term[:rows], term[rows:]).astype(BF16)


def stats_kernel(table, mine, across, beside, passed, left, right, left_hbm, right_hbm, left_out, right_out, sems):
    core, x = table[WHERE, 0], table[WHERE, 1]
    stores = []
    for j in range(left.shape[0]):
        full = table[FULL, j] > 0
        way = lax.rem(table[CHIP, j] + 4 - x, 4)

        def add(here, term):
            @pl.when(jnp.logical_and(full, here))
            def _():
                left_out[j] = STAT_DECAY * left[j] + (1.0 - STAT_DECAY) * term(0).astype(F32)
                right_out[j] = STAT_DECAY * right[j] + (1.0 - STAT_DECAY) * term(1).astype(F32)

        add(way == 0, lambda side: mine[side])
        add(way == 2, lambda side: across[side])
        add(way == 3 - 2 * core, lambda side: beside[core, side])
        add(way == 1 + 2 * core, lambda side: passed[side])

        @pl.when(jnp.logical_not(full))
        def _():
            left_out[j] = STAT_DECAY * left[j]
            right_out[j] = STAT_DECAY * right[j]

        for side, (result, target) in enumerate(((left_out, left_hbm), (right_out, right_hbm))):
            stores.append(pltpu.make_async_copy(result.at[j], target.at[j], sems.at[j, side]))
            stores[-1].start()
    for store in stores:
        store.wait()


def compact_kernel(table, rows, out):
    def body(i, carry):
        block = rows[table[OWNER, i]]
        for x in range(out.shape[0]):
            out[x, i] = block
        return carry

    lax.fori_loop(0, out.shape[1], body, 0, unroll=8)


def place_half(core, table, rows, out_hbm, ordered, sems):
    width = rows.shape[2]
    cols = pl.ds(pl.multiple_of(core * width, 128), width)

    def fill(first, count):
        def body(b, carry):
            ordered[first + b] = rows[table[SOURCE, first + b]]
            return carry

        lax.fori_loop(0, count, body, 0, unroll=8)

    store_in_steps(ordered, out_hbm.at[:, :, cols], sems, 0, fill)


def place_near_kernel(table, rows, out_hbm, ordered, sems):
    place_half(table[WHERE, 0], table, rows, out_hbm, ordered, sems)


def place_far_kernel(table, rows, begun, out_hbm, ordered, sems):
    del begun
    place_half(1 - table[WHERE, 0], table, rows, out_hbm, ordered, sems)


def call(kernel, out_shape, in_specs, scratch=(), out_specs=None, cost=None, aliases=None):
    if out_specs is None:
        out_specs = [VMEM_SPEC] * len(out_shape) if isinstance(out_shape, list) else VMEM_SPEC
    if cost is not None:
        cost = pl.CostEstimate(flops=cost[0], bytes_accessed=cost[1], transcendentals=0)
    return pl.pallas_call(
        kernel,
        out_shape=out_shape,
        in_specs=in_specs,
        out_specs=out_specs,
        scratch_shapes=list(scratch),
        input_output_aliases=aliases or {},
        compiler_params=PARAMS,
        cost_estimate=cost,
    )


def exchange(value, axis):
    return lax.all_to_all(value, axis, 0, 0, tiled=True)


def in_hbm(value):
    return pltpu.with_memory_space_constraint(value, pltpu.HBM)


def turn(value, k):
    chips = lax.axis_size("x")
    return lax.ppermute(value, "x", [(i, (i + k) % chips) for i in range(chips)]) if k else value


def swap_cores(value):
    return lax.ppermute(value, "core", [(0, 1), (1, 0)])


def local(grads, block_slot, left_stat, right_stat, left_root, right_root):
    grads = grads[0]
    chips = lax.axis_size("x")
    x = lax.axis_index("x")
    core = lax.axis_index("core")
    owners = lax.axis_size("y") * lax.axis_size("z")
    me = lax.axis_index("y") * lax.axis_size("z") + lax.axis_index("z")
    capacity, stat_rows, _ = left_stat.shape
    blocks, shard_rows, width = grads.shape
    half = width // 2
    depth = blocks // chips

    piece = jax.ShapeDtypeStruct((2, stat_rows, width), BF16)
    groups = width // stat_rows
    grads = in_hbm(grads.reshape(-1, stat_rows, width))
    left_root, right_root = in_hbm(left_root), in_hbm(right_root)
    grad_groups = grads.shape[0]

    sent = call(
        send_kernel,
        jax.ShapeDtypeStruct((grad_groups + 4 * capacity, stat_rows, half), BF16),
        [SMEM_SPEC] + [HBM_SPEC] * 3,
        [pltpu.SemaphoreType.DMA((5,))],
    )(core.reshape(1), grads, left_root, right_root)
    sent, late_grads = lax.optimization_barrier((sent, grads))
    other = swap_cores(sent)
    kept, table = call(
        functools.partial(keep_kernel, chips, capacity),
        [jax.ShapeDtypeStruct((grad_groups, stat_rows, half), BF16), jax.ShapeDtypeStruct((8, blocks), jnp.int32)],
        [SMEM_SPEC] * 3 + [HBM_SPEC] * 2,
        [pltpu.VMEM((1, blocks), jnp.int32), pltpu.SemaphoreType.DMA((2,))],
        cost=(0, 4_000_000),
    )(core.reshape(1), x.reshape(1), me.reshape(1), in_hbm(block_slot.reshape(1, blocks)), in_hbm(late_grads))

    parts = call(
        pair_sum_kernel,
        jax.ShapeDtypeStruct((chips, depth, shard_rows, half), BF16),
        [SMEM_SPEC, VMEM_SPEC, VMEM_SPEC],
    )(table, kept.reshape(-1, shard_rows, half), other.reshape(-1, shard_rows, half))
    parts = exchange(parts, "x")
    outgoing = call(
        chip_sum_kernel,
        jax.ShapeDtypeStruct((owners, shard_rows, half), BF16),
        [SMEM_SPEC, VMEM_SPEC],
        [pltpu.VMEM((depth + 1, shard_rows, half), BF16)],
    )(table, parts)

    outgoing, late_other = lax.optimization_barrier((outgoing, other))
    own = exchange(outgoing, ("y", "z"))
    both = jax.ShapeDtypeStruct((2, 2, stat_rows, width), BF16)
    beside, across, mine = call(
        functools.partial(select_roots_kernel, grad_groups),
        [both, piece, both],
        [SMEM_SPEC, VMEM_SPEC, HBM_SPEC, HBM_SPEC],
        [pltpu.SemaphoreType.DMA((3, 2))],
        cost=(0, 2_000_000),
    )(table, late_other, left_root, right_root)
    ways = [(2 * i, 2 * ((i + 1) % chips)) for i in range(chips)]
    ways += [(2 * i + 1, 2 * ((i - 1) % chips) + 1) for i in range(chips)]
    beside, across = lax.ppermute(beside, ("x", "core"), ways), turn(across, 2)
    stacked = call(
        stack_kernel,
        jax.ShapeDtypeStruct((3, 2, stat_rows, width), BF16),
        [VMEM_SPEC, VMEM_SPEC],
        cost=(0, 1_000_000),
    )(beside, across)
    others = swap_cores(stacked)
    left, right = call(
        merge_roots_kernel,
        [jax.ShapeDtypeStruct((groups, stat_rows, width), BF16)] * 2,
        [SMEM_SPEC] + [VMEM_SPEC] * 4,
        cost=(0, 2_000_000),
    )(table, mine, beside, across, others)

    own = own.reshape(width, half)
    far = swap_cores(own)
    partial, grad_sq = call(
        near_kernel,
        [jax.ShapeDtypeStruct((width, width), F32), jax.ShapeDtypeStruct((8, 128), F32)],
        [SMEM_SPEC, VMEM_SPEC, VMEM_SPEC],
        cost=(270_000_000, 4_000_000),
    )(table, own, right)
    update = call(
        direction_kernel,
        jax.ShapeDtypeStruct((width, half), BF16),
        [SMEM_SPEC] + [VMEM_SPEC] * 5,
    )(table, far, partial, left, right, grad_sq)

    update, own, far = lax.optimization_barrier((update, own, far))
    rows = exchange(update.reshape(owners, shard_rows, half), ("y", "z"))
    beside, across, mine = call(
        terms_kernel,
        [both, piece, piece],
        [SMEM_SPEC, VMEM_SPEC, VMEM_SPEC],
        [pltpu.VMEM((width, width), BF16)],
        cost=(800_000_000, 2_000_000),
    )(table, own, far)
    across = turn(across, 2)
    beside = lax.ppermute(beside, ("x", "core"), ways)
    packed = call(
        compact_kernel,
        jax.ShapeDtypeStruct((chips, depth, shard_rows, half), BF16),
        [SMEM_SPEC, VMEM_SPEC],
    )(table, rows)
    packed, beside, across = lax.optimization_barrier((packed, beside, across))
    near = exchange(packed, "x").reshape(blocks, shard_rows, half)
    passed = swap_cores(lax.dynamic_index_in_dim(beside, 1 - core, keepdims=False))
    stat = jax.ShapeDtypeStruct(left_stat.shape, F32)
    left_new, right_new = call(
        stats_kernel,
        [stat, stat],
        [SMEM_SPEC] + [VMEM_SPEC] * 6,
        [
            pltpu.VMEM(left_stat.shape, F32),
            pltpu.VMEM(right_stat.shape, F32),
            pltpu.SemaphoreType.DMA((capacity, 2)),
        ],
        [HBM_SPEC, HBM_SPEC],
        cost=(10_000_000, 5_000_000),
    )(table, mine, across, beside, passed, left_stat, right_stat)
    near, left_new, right_new = lax.optimization_barrier((near, left_new, right_new))
    beyond = swap_cores(near)
    whole_rows = jax.ShapeDtypeStruct((blocks, shard_rows, width), BF16)
    scratch = [pltpu.VMEM((blocks, shard_rows, half), BF16), pltpu.SemaphoreType.DMA((4,))]
    begun = call(
        place_near_kernel, whole_rows, [SMEM_SPEC, VMEM_SPEC], scratch, HBM_SPEC, cost=(0, 4_000_000)
    )(table, near)
    result = call(
        place_far_kernel, whole_rows, [SMEM_SPEC, VMEM_SPEC, HBM_SPEC], scratch, HBM_SPEC, aliases={2: 0}
    )(table, beyond, begun)
    return (result, left_new, right_new)


def solution(mesh):
    fine = Mesh(mesh.devices.reshape(4, 2, 4, 16), ("x", "core", "y", "z"))
    replica, shard = ("x", "core"), ("y", "z")
    in_specs = (
        P(replica, None, shard, None),
        P(),
        P(shard, replica, None),
        P(shard, replica, None),
        P(shard, replica, None),
        P(shard, replica, None),
    )
    out_specs = (P(None, shard, None), P(shard, replica, None), P(shard, replica, None))
    return jax.shard_map(local, mesh=fine, in_specs=in_specs, out_specs=out_specs, check_vma=False)
```

```python
import functools

import jax
import jax.numpy as jnp
from jax import lax
from jax.experimental import pallas as pl
from jax.experimental.pallas import tpu as pltpu
from jax.sharding import Mesh, PartitionSpec as P

STAT_DECAY = 0.9
NORM_EPS = 1e-12
F32 = jnp.float32
BF16 = jnp.bfloat16
VMEM_SPEC = pl.BlockSpec(memory_space=pltpu.VMEM)
HBM_SPEC = pl.BlockSpec(memory_space=pltpu.HBM)
SMEM_SPEC = pl.BlockSpec(memory_space=pltpu.SMEM)
PARAMS = pltpu.CompilerParams(vmem_limit_bytes=32 * 1024 * 1024)


def dot(a, b, dims):
    return lax.dot_general(a, b, (dims, ((), ())), preferred_element_type=F32)


ORDER, SOURCE, PLACE, OWNER, SLOT, FULL, CHIP, WHERE = range(8)


def fill_table(slots, core, x, me, capacity, chips, first, first_done, table):
    blocks = slots.shape[1]
    square = (blocks, blocks)
    cap_bits, chip_bits = capacity.bit_length() - 1, chips.bit_length() - 1
    depth = blocks // chips
    lane = lax.broadcasted_iota(jnp.int32, square, 1)
    sublane = lax.broadcasted_iota(jnp.int32, square, 0)
    across = jnp.broadcast_to(slots[...], square)
    slot = across.T

    def total(mask, value):
        return jnp.sum(jnp.where(mask, value, 0), axis=0, keepdims=True)

    rank_row = total(slot < across, 1)
    rank = jnp.broadcast_to(rank_row, square).T
    chip = rank & (chips - 1)
    spot = rank >> chip_bits
    owner = slot >> cap_bits
    first[...] = total((owner == me) & (chip == lane), slot & (capacity - 1))
    first_done()
    local_slot = slot == me * capacity + lane
    table[pl.ds(ORDER, 1)] = total(rank == lane, sublane)
    table[pl.ds(SOURCE, 1)] = (rank_row & (chips - 1)) * depth + (rank_row >> chip_bits)
    table[pl.ds(PLACE, 1)] = total((chip == x) & (owner == lane), spot - depth) + depth
    table[pl.ds(OWNER, 1)] = total((chip == x) & (spot == lane), owner)
    table[pl.ds(SLOT, 1)] = first[...]
    table[pl.ds(FULL, 1)] = total(local_slot, 1)
    table[pl.ds(CHIP, 1)] = total(local_slot, chip)
    row = lax.broadcasted_iota(jnp.int32, (1, blocks), 1)
    table[pl.ds(WHERE, 1)] = jnp.where(row == 0, core, x)


def send_kernel(core_ref, grads, left_root, right_root, sent, sems):
    width = sent.shape[2]
    groups = grads.shape[0]
    capacity = left_root.shape[0]
    far = pl.ds(pl.multiple_of((1 - core_ref[0]) * width, 128), width)
    loads = [pltpu.make_async_copy(grads.at[:, :, far], sent.at[pl.ds(0, groups)], sems.at[0])]
    for i in range(4):
        root = (left_root, right_root)[i // 2].at[:, :, pl.ds(i % 2 * width, width)]
        loads.append(pltpu.make_async_copy(root, sent.at[pl.ds(groups + i * capacity, capacity)], sems.at[i + 1]))
    for load in loads:
        load.start()
    for load in loads:
        load.wait()


def keep_kernel(
    core_ref, x_ref, me_ref, slots_hbm, grads, left_root, right_root, kept, table, beside, mine, across, slots, first, scalars, sems, root_sems
):
    core, x = core_ref[0], x_ref[0]
    width = kept.shape[2]
    near = pl.ds(pl.multiple_of(core * width, 128), width)
    slots_load = pltpu.make_async_copy(slots_hbm, slots, sems.at[0])
    load = pltpu.make_async_copy(grads.at[:, :, near], kept, sems.at[1])
    first_load = pltpu.make_async_copy(first, scalars, sems.at[2])
    slots_load.start()
    load.start()
    slots_load.wait()
    fill_table(slots, core, x, me_ref[0], left_root.shape[0], 4, first, first_load.start, table)
    first_load.wait()
    loads = [load]
    for i, (chip, out) in enumerate(((x + 1 + 2 * core, beside), (x, mine), (x + 2, across))):
        slot = scalars[0, lax.rem(chip, 4)]
        for side, root in enumerate((left_root, right_root)):
            loads.append(pltpu.make_async_copy(root.at[slot], out.at[side], root_sems.at[i, side]))
            loads[-1].start()
    for load in loads:
        load.wait()


def from_other(groups, capacity, other, slot, side, out):
    width = other.shape[2]
    for h in range(2):
        out[:, h * width : (h + 1) * width] = other[groups + (2 * side + h) * capacity + slot]


def pair_roots_kernel(groups, capacity, table, other, beside, out):
    core, x = table[WHERE, 0], table[WHERE, 1]
    slot = table[SLOT, lax.rem(x + 1 + 2 * core, 4)]
    out[core] = beside[...]
    for side in range(2):
        from_other(groups, capacity, other, slot, side, out.at[1 - core, side])


def stack_kernel(beside, across, out):
    out[0:2] = beside[...]
    out[2] = across[...]


def merge_roots_kernel(groups, capacity, table, other, mine, beside, across, others, left, right):
    core, x = table[WHERE, 0], table[WHERE, 1]
    near, far, opposite = lax.rem(x + 3 - 2 * core, 4), lax.rem(x + 1 + 2 * core, 4), lax.rem(x + 2, 4)
    for side, out in enumerate((left, right)):
        out[2 * x + core] = mine[side]
        from_other(groups, capacity, other, table[SLOT, x], side, out.at[2 * x + 1 - core])
        for parity in range(2):
            out[2 * near + parity] = beside[parity, side]
            out[2 * far + parity] = others[parity, side]
        out[2 * opposite + core] = across[side]
        out[2 * opposite + 1 - core] = others[2, side]


def pair_sum_kernel(table, own, other, out):
    chips, depth = out.shape[:2]

    def body(i, carry):
        for x in range(chips):
            block = table[ORDER, i * chips + x]
            out[x, i] = own[block] + other[block]
        return carry

    lax.fori_loop(0, depth, body, 0, unroll=8)


def store_in_steps(source, target, sems, dim, fill):
    steps = sems.shape[0]
    count = source.shape[dim] // steps
    stores = []
    for i in range(steps):
        fill(i * count, count)
        part = (slice(None),) * dim + (pl.ds(i * count, count),)
        stores.append(pltpu.make_async_copy(source.at[part], target.at[part], sems.at[i]))
        stores[-1].start()
    for store in stores:
        store.wait()


def chip_sum_kernel(table, parts, out, total, place, sem):
    depth = parts.shape[1]
    load = pltpu.make_async_copy(table, place, sem)
    load.start()
    acc = parts[0].astype(F32)
    for x in range(1, parts.shape[0]):
        acc = acc + parts[x].astype(F32)
    total[0:depth] = acc.astype(BF16)
    total[depth] = jnp.zeros(total.shape[1:], BF16)
    load.wait()

    def body(o, carry):
        out[o] = total[place[PLACE, o]]
        return carry

    lax.fori_loop(0, out.shape[0], body, 0, unroll=8)


def near_kernel(table, own, right, partial, grad_sq):
    core = table[WHERE, 0]
    half = own.shape[1]
    groups = right.shape[0] // 2
    grad = own[...]
    grad_sq[...] = jnp.full(grad_sq.shape, jnp.sum(jnp.square(grad.astype(F32))), F32)
    upper = right[pl.ds(core * groups, groups)].reshape(half, 2 * half)
    partial[...] = dot(grad, upper, ((1,), (0,)))


def direction_kernel(table, other, partial, left, right, grad_sq_near, out):
    core = table[WHERE, 0]
    half = other.shape[1]
    groups = right.shape[0] // 2
    size = 2 * half
    grad = other[...]
    grad_sq = grad_sq_near[0:1, 0:1] + jnp.full((1, 1), jnp.sum(jnp.square(grad.astype(F32))), F32)
    left_mat = left[...].reshape(size, size)

    def columns(h):
        cols = pl.ds(pl.multiple_of(h * half, 128), half)
        lower = right[pl.ds((1 - core) * groups, groups), :, cols].reshape(half, half)
        shaped = partial[:, cols] + dot(grad, lower, ((1,), (0,)))
        return dot(left_mat, shaped.astype(BF16), ((1,), (0,)))

    dir_sq = jnp.sum(jnp.square(columns(1 - core)))
    near = columns(core)
    dir_sq = jnp.full((1, 1), dir_sq + jnp.sum(jnp.square(near)), F32)
    ratio = jnp.sqrt(grad_sq) / jnp.sqrt(dir_sq + NORM_EPS)
    out[...] = (-near * ratio).astype(BF16)


def terms_kernel(table, own, other, beside, across, mine, grad):
    core, x = table[WHERE, 0], table[WHERE, 1]
    half = own.shape[1]
    rows = mine.shape[1]
    grad[:, pl.ds(pl.multiple_of(core * half, 128), half)] = own[...]
    grad[:, pl.ds(pl.multiple_of((1 - core) * half, 128), half)] = other[...]
    whole = grad[...]

    def of_chip(chip):
        at = pl.ds(pl.multiple_of(chip * 2 * rows, 128), 2 * rows)
        return dot(grad[at], whole, ((1,), (1,))), dot(grad[:, at], whole, ((0,), (0,)))

    for side, term in enumerate(of_chip(lax.rem(x + 1 + 2 * core, 4))):
        for parity in range(2):
            beside[parity, side] = term[parity * rows : (parity + 1) * rows].astype(BF16)
    for chip, out in ((lax.rem(x + 2, 4), across), (x, mine)):
        for side, term in enumerate(of_chip(chip)):
            out[side] = jnp.where(core == 0, term[:rows], term[rows:]).astype(BF16)


def stats_kernel(table, mine, across, beside, passed, left, right, left_hbm, right_hbm, left_out, right_out, sems):
    core, x = table[WHERE, 0], table[WHERE, 1]
    stores = []
    for j in range(left.shape[0]):
        full = table[FULL, j] > 0
        way = lax.rem(table[CHIP, j] + 4 - x, 4)

        def add(here, term):
            @pl.when(jnp.logical_and(full, here))
            def _():
                left_out[j] = STAT_DECAY * left[j] + (1.0 - STAT_DECAY) * term(0).astype(F32)
                right_out[j] = STAT_DECAY * right[j] + (1.0 - STAT_DECAY) * term(1).astype(F32)

        add(way == 0, lambda side: mine[side])
        add(way == 2, lambda side: across[side])
        add(way == 3 - 2 * core, lambda side: beside[core, side])
        add(way == 1 + 2 * core, lambda side: passed[side])

        @pl.when(jnp.logical_not(full))
        def _():
            left_out[j] = STAT_DECAY * left[j]
            right_out[j] = STAT_DECAY * right[j]

        for side, (result, target) in enumerate(((left_out, left_hbm), (right_out, right_hbm))):
            stores.append(pltpu.make_async_copy(result.at[j], target.at[j], sems.at[j, side]))
            stores[-1].start()
    for store in stores:
        store.wait()


def compact_kernel(table, rows, out):
    def body(i, carry):
        block = rows[table[OWNER, i]]
        for x in range(out.shape[0]):
            out[x, i] = block
        return carry

    lax.fori_loop(0, out.shape[1], body, 0, unroll=8)


def place_half(core, table, rows, out_hbm, ordered, sems):
    width = rows.shape[2]
    cols = pl.ds(pl.multiple_of(core * width, 128), width)

    def fill(first, count):
        def body(b, carry):
            ordered[first + b] = rows[table[SOURCE, first + b]]
            return carry

        lax.fori_loop(0, count, body, 0, unroll=8)

    store_in_steps(ordered, out_hbm.at[:, :, cols], sems, 0, fill)


def place_near_kernel(table, rows, out_hbm, ordered, sems):
    place_half(table[WHERE, 0], table, rows, out_hbm, ordered, sems)


def place_far_kernel(table, rows, begun, out_hbm, ordered, sems):
    del begun
    place_half(1 - table[WHERE, 0], table, rows, out_hbm, ordered, sems)


def call(kernel, out_shape, in_specs, scratch=(), out_specs=None, cost=None, aliases=None):
    if out_specs is None:
        out_specs = [VMEM_SPEC] * len(out_shape) if isinstance(out_shape, list) else VMEM_SPEC
    if cost is not None:
        cost = pl.CostEstimate(flops=cost[0], bytes_accessed=cost[1], transcendentals=0)
    return pl.pallas_call(
        kernel,
        out_shape=out_shape,
        in_specs=in_specs,
        out_specs=out_specs,
        scratch_shapes=list(scratch),
        input_output_aliases=aliases or {},
        compiler_params=PARAMS,
        cost_estimate=cost,
    )


def exchange(value, axis):
    return lax.all_to_all(value, axis, 0, 0, tiled=True)


def in_hbm(value):
    return pltpu.with_memory_space_constraint(value, pltpu.HBM)


def turn(value, k):
    chips = lax.axis_size("x")
    return lax.ppermute(value, "x", [(i, (i + k) % chips) for i in range(chips)]) if k else value


def swap_cores(value):
    return lax.ppermute(value, "core", [(0, 1), (1, 0)])


def local(grads, block_slot, left_stat, right_stat, left_root, right_root):
    grads = grads[0]
    chips = lax.axis_size("x")
    x = lax.axis_index("x")
    core = lax.axis_index("core")
    owners = lax.axis_size("y") * lax.axis_size("z")
    me = lax.axis_index("y") * lax.axis_size("z") + lax.axis_index("z")
    capacity, stat_rows, _ = left_stat.shape
    blocks, shard_rows, width = grads.shape
    half = width // 2
    depth = blocks // chips

    piece = jax.ShapeDtypeStruct((2, stat_rows, width), BF16)
    groups = width // stat_rows
    grads = in_hbm(grads.reshape(-1, stat_rows, width))
    left_root, right_root = in_hbm(left_root), in_hbm(right_root)
    grad_groups = grads.shape[0]

    sent = call(
        send_kernel,
        jax.ShapeDtypeStruct((grad_groups + 4 * capacity, stat_rows, half), BF16),
        [SMEM_SPEC] + [HBM_SPEC] * 3,
        [pltpu.SemaphoreType.DMA((5,))],
    )(core.reshape(1), grads, left_root, right_root)
    sent, late_grads = lax.optimization_barrier((sent, grads))
    other = swap_cores(sent)
    kept, table, beside, mine, across = call(
        keep_kernel,
        [jax.ShapeDtypeStruct((grad_groups, stat_rows, half), BF16), jax.ShapeDtypeStruct((8, blocks), jnp.int32)]
        + [piece] * 3,
        [SMEM_SPEC] * 3 + [HBM_SPEC] * 4,
        [
            pltpu.VMEM((1, blocks), jnp.int32),
            pltpu.VMEM((1, blocks), jnp.int32),
            pltpu.SMEM((1, blocks), jnp.int32),
            pltpu.SemaphoreType.DMA((3,)),
            pltpu.SemaphoreType.DMA((3, 2)),
        ],
        cost=(0, 4_000_000),
    )(
        core.reshape(1),
        x.reshape(1),
        me.reshape(1),
        in_hbm(block_slot.reshape(1, blocks)),
        in_hbm(late_grads),
        left_root,
        right_root,
    )

    parts = call(
        pair_sum_kernel,
        jax.ShapeDtypeStruct((chips, depth, shard_rows, half), BF16),
        [SMEM_SPEC, VMEM_SPEC, VMEM_SPEC],
    )(table, kept.reshape(-1, shard_rows, half), other.reshape(-1, shard_rows, half))
    parts = exchange(parts, "x")
    outgoing = call(
        chip_sum_kernel,
        jax.ShapeDtypeStruct((owners, shard_rows, half), BF16),
        [VMEM_SPEC, VMEM_SPEC],
        [
            pltpu.VMEM((depth + 1, shard_rows, half), BF16),
            pltpu.SMEM((8, blocks), jnp.int32),
            pltpu.SemaphoreType.DMA,
        ],
    )(table, parts)

    outgoing, late_other, beside, across = lax.optimization_barrier((outgoing, other, beside, across))
    own = exchange(outgoing, ("y", "z"))
    both = jax.ShapeDtypeStruct((2, 2, stat_rows, width), BF16)
    beside = call(
        functools.partial(pair_roots_kernel, grad_groups, capacity),
        both,
        [SMEM_SPEC, VMEM_SPEC, VMEM_SPEC],
        cost=(0, 1_000_000),
    )(table, late_other, beside)
    ways = [(2 * i, 2 * ((i + 1) % chips)) for i in range(chips)]
    ways += [(2 * i + 1, 2 * ((i - 1) % chips) + 1) for i in range(chips)]
    beside, across = lax.ppermute(beside, ("x", "core"), ways), turn(across, 2)
    stacked = call(
        stack_kernel,
        jax.ShapeDtypeStruct((3, 2, stat_rows, width), BF16),
        [VMEM_SPEC, VMEM_SPEC],
        cost=(0, 1_000_000),
    )(beside, across)
    others = swap_cores(stacked)
    left, right = call(
        functools.partial(merge_roots_kernel, grad_groups, capacity),
        [jax.ShapeDtypeStruct((groups, stat_rows, width), BF16)] * 2,
        [SMEM_SPEC] + [VMEM_SPEC] * 5,
        cost=(0, 2_000_000),
    )(table, late_other, mine, beside, across, others)

    own = own.reshape(width, half)
    far = swap_cores(own)
    partial, grad_sq = call(
        near_kernel,
        [jax.ShapeDtypeStruct((width, width), F32), jax.ShapeDtypeStruct((8, 128), F32)],
        [SMEM_SPEC, VMEM_SPEC, VMEM_SPEC],
        cost=(270_000_000, 4_000_000),
    )(table, own, right)
    update = call(
        direction_kernel,
        jax.ShapeDtypeStruct((width, half), BF16),
        [SMEM_SPEC] + [VMEM_SPEC] * 5,
    )(table, far, partial, left, right, grad_sq)

    update, own, far = lax.optimization_barrier((update, own, far))
    rows = exchange(update.reshape(owners, shard_rows, half), ("y", "z"))
    beside, across, mine = call(
        terms_kernel,
        [both, piece, piece],
        [SMEM_SPEC, VMEM_SPEC, VMEM_SPEC],
        [pltpu.VMEM((width, width), BF16)],
        cost=(800_000_000, 2_000_000),
    )(table, own, far)
    across = turn(across, 2)
    beside = lax.ppermute(beside, ("x", "core"), ways)
    packed = call(
        compact_kernel,
        jax.ShapeDtypeStruct((chips, depth, shard_rows, half), BF16),
        [SMEM_SPEC, VMEM_SPEC],
    )(table, rows)
    packed, beside, across = lax.optimization_barrier((packed, beside, across))
    near = exchange(packed, "x").reshape(blocks, shard_rows, half)
    passed = swap_cores(lax.dynamic_index_in_dim(beside, 1 - core, keepdims=False))
    stat = jax.ShapeDtypeStruct(left_stat.shape, F32)
    left_new, right_new = call(
        stats_kernel,
        [stat, stat],
        [SMEM_SPEC] + [VMEM_SPEC] * 6,
        [
            pltpu.VMEM(left_stat.shape, F32),
            pltpu.VMEM(right_stat.shape, F32),
            pltpu.SemaphoreType.DMA((capacity, 2)),
        ],
        [HBM_SPEC, HBM_SPEC],
        cost=(10_000_000, 5_000_000),
    )(table, mine, across, beside, passed, left_stat, right_stat)
    near, left_new, right_new = lax.optimization_barrier((near, left_new, right_new))
    beyond = swap_cores(near)
    whole_rows = jax.ShapeDtypeStruct((blocks, shard_rows, width), BF16)
    scratch = [pltpu.VMEM((blocks, shard_rows, half), BF16), pltpu.SemaphoreType.DMA((4,))]
    begun = call(
        place_near_kernel, whole_rows, [SMEM_SPEC, VMEM_SPEC], scratch, HBM_SPEC, cost=(0, 4_000_000)
    )(table, near)
    result = call(
        place_far_kernel, whole_rows, [SMEM_SPEC, VMEM_SPEC, HBM_SPEC], scratch, HBM_SPEC, aliases={2: 0}
    )(table, beyond, begun)
    return (result, left_new, right_new)


def solution(mesh):
    fine = Mesh(mesh.devices.reshape(4, 2, 4, 16), ("x", "core", "y", "z"))
    replica, shard = ("x", "core"), ("y", "z")
    in_specs = (
        P(replica, None, shard, None),
        P(),
        P(shard, replica, None),
        P(shard, replica, None),
        P(shard, replica, None),
        P(shard, replica, None),
    )
    out_specs = (P(None, shard, None), P(shard, replica, None), P(shard, replica, None))
    return jax.shard_map(local, mesh=fine, in_specs=in_specs, out_specs=out_specs, check_vma=False)
```

```python
import functools

import jax
import jax.numpy as jnp
from jax import lax
from jax.experimental import pallas as pl
from jax.experimental.pallas import tpu as pltpu
from jax.sharding import Mesh, PartitionSpec as P

STAT_DECAY = 0.9
NORM_EPS = 1e-12
F32 = jnp.float32
BF16 = jnp.bfloat16
VMEM_SPEC = pl.BlockSpec(memory_space=pltpu.VMEM)
HBM_SPEC = pl.BlockSpec(memory_space=pltpu.HBM)
SMEM_SPEC = pl.BlockSpec(memory_space=pltpu.SMEM)
PARAMS = pltpu.CompilerParams(vmem_limit_bytes=32 * 1024 * 1024)


def dot(a, b, dims):
    return lax.dot_general(a, b, (dims, ((), ())), preferred_element_type=F32)


ORDER, SOURCE, PLACE, OWNER, SLOT, FULL, CHIP, WHERE = range(8)


def fill_table(slots, core, x, me, capacity, chips, first, first_done, table):
    blocks = slots.shape[1]
    square = (blocks, blocks)
    cap_bits, chip_bits = capacity.bit_length() - 1, chips.bit_length() - 1
    depth = blocks // chips
    lane = lax.broadcasted_iota(jnp.int32, square, 1)
    sublane = lax.broadcasted_iota(jnp.int32, square, 0)
    across = jnp.broadcast_to(slots[...], square)
    slot = across.T

    def total(mask, value):
        return jnp.sum(jnp.where(mask, value, 0), axis=0, keepdims=True)

    rank_row = total(slot < across, 1)
    rank = jnp.broadcast_to(rank_row, square).T
    chip = rank & (chips - 1)
    spot = rank >> chip_bits
    owner = slot >> cap_bits
    first[...] = total((owner == me) & (chip == lane), slot & (capacity - 1))
    first_done()
    local_slot = slot == me * capacity + lane
    table[pl.ds(ORDER, 1)] = total(rank == lane, sublane)
    table[pl.ds(SOURCE, 1)] = (rank_row & (chips - 1)) * depth + (rank_row >> chip_bits)
    table[pl.ds(PLACE, 1)] = total((chip == x) & (owner == lane), spot - depth) + depth
    table[pl.ds(OWNER, 1)] = total((chip == x) & (spot == lane), owner)
    table[pl.ds(SLOT, 1)] = first[...]
    table[pl.ds(FULL, 1)] = total(local_slot, 1)
    table[pl.ds(CHIP, 1)] = total(local_slot, chip)
    row = lax.broadcasted_iota(jnp.int32, (1, blocks), 1)
    table[pl.ds(WHERE, 1)] = jnp.where(row == 0, core, x)


def send_kernel(core_ref, grads, left_root, right_root, sent, sems):
    width = sent.shape[2]
    groups = grads.shape[0]
    capacity = left_root.shape[0]
    far = pl.ds(pl.multiple_of((1 - core_ref[0]) * width, 128), width)
    loads = [pltpu.make_async_copy(grads.at[:, :, far], sent.at[pl.ds(0, groups)], sems.at[0])]
    for i in range(4):
        root = (left_root, right_root)[i // 2].at[:, :, pl.ds(i % 2 * width, width)]
        loads.append(pltpu.make_async_copy(root, sent.at[pl.ds(groups + i * capacity, capacity)], sems.at[i + 1]))
    for load in loads:
        load.start()
    for load in loads:
        load.wait()


def keep_kernel(
    core_ref, x_ref, me_ref, slots_hbm, grads, left_root, right_root, kept, table, beside, mine, across, slots, first, scalars, sems, root_sems
):
    core, x = core_ref[0], x_ref[0]
    width = kept.shape[2]
    near = pl.ds(pl.multiple_of(core * width, 128), width)
    slots_load = pltpu.make_async_copy(slots_hbm, slots, sems.at[0])
    load = pltpu.make_async_copy(grads.at[:, :, near], kept, sems.at[1])
    first_load = pltpu.make_async_copy(first, scalars, sems.at[2])
    slots_load.start()
    load.start()
    slots_load.wait()
    fill_table(slots, core, x, me_ref[0], left_root.shape[0], 4, first, first_load.start, table)
    first_load.wait()
    loads = [load]
    for i, (chip, out) in enumerate(((x + 1 + 2 * core, beside), (x, mine), (x + 2, across))):
        slot = scalars[0, lax.rem(chip, 4)]
        for side, root in enumerate((left_root, right_root)):
            loads.append(pltpu.make_async_copy(root.at[slot], out.at[side], root_sems.at[i, side]))
            loads[-1].start()
    for load in loads:
        load.wait()


def from_other(groups, capacity, other, slot, side, out):
    width = other.shape[2]
    for h in range(2):
        out[:, h * width : (h + 1) * width] = other[groups + (2 * side + h) * capacity + slot]


def pair_roots_kernel(groups, capacity, table, other, beside, out):
    core, x = table[WHERE, 0], table[WHERE, 1]
    slot = table[SLOT, lax.rem(x + 1 + 2 * core, 4)]
    out[core] = beside[...]
    for side in range(2):
        from_other(groups, capacity, other, slot, side, out.at[1 - core, side])


def stack_kernel(beside, across, out):
    out[0:2] = beside[...]
    out[2] = across[...]


def merge_roots_kernel(groups, capacity, table, other, mine, beside, across, others, left, right):
    core, x = table[WHERE, 0], table[WHERE, 1]
    near, far, opposite = lax.rem(x + 3 - 2 * core, 4), lax.rem(x + 1 + 2 * core, 4), lax.rem(x + 2, 4)
    for side, out in enumerate((left, right)):
        out[2 * x + core] = mine[side]
        from_other(groups, capacity, other, table[SLOT, x], side, out.at[2 * x + 1 - core])
        for parity in range(2):
            out[2 * near + parity] = beside[parity, side]
            out[2 * far + parity] = others[parity, side]
        out[2 * opposite + core] = across[side]
        out[2 * opposite + 1 - core] = others[2, side]


def pair_sum_kernel(table, own, other, out):
    chips, depth = out.shape[:2]

    def body(i, carry):
        for x in range(chips):
            block = table[ORDER, i * chips + x]
            out[x, i] = own[block] + other[block]
        return carry

    lax.fori_loop(0, depth, body, 0, unroll=8)


def store_in_steps(source, target, sems, dim, fill):
    steps = sems.shape[0]
    count = source.shape[dim] // steps
    stores = []
    for i in range(steps):
        fill(i * count, count)
        part = (slice(None),) * dim + (pl.ds(i * count, count),)
        stores.append(pltpu.make_async_copy(source.at[part], target.at[part], sems.at[i]))
        stores[-1].start()
    for store in stores:
        store.wait()


def chip_sum_kernel(table, parts, out, total, place, sem):
    depth = parts.shape[1]
    load = pltpu.make_async_copy(table, place, sem)
    load.start()
    acc = parts[0].astype(F32)
    for x in range(1, parts.shape[0]):
        acc = acc + parts[x].astype(F32)
    total[0:depth] = acc.astype(BF16)
    total[depth] = jnp.zeros(total.shape[1:], BF16)
    load.wait()

    def body(o, carry):
        out[o] = total[place[PLACE, o]]
        return carry

    lax.fori_loop(0, out.shape[0], body, 0, unroll=8)


def near_kernel(table, own, right, partial, grad_sq):
    core = table[WHERE, 0]
    half = own.shape[1]
    groups = right.shape[0] // 2
    grad = own[...]
    grad_sq[...] = jnp.full(grad_sq.shape, jnp.sum(jnp.square(grad.astype(F32))), F32)
    upper = right[pl.ds(core * groups, groups)].reshape(half, 2 * half)
    partial[...] = dot(grad, upper, ((1,), (0,)))


def direction_kernel(table, other, partial, left, right, grad_sq_near, out):
    core = table[WHERE, 0]
    half = other.shape[1]
    groups = right.shape[0] // 2
    size = 2 * half
    grad = other[...]
    grad_sq = grad_sq_near[0:1, 0:1] + jnp.full((1, 1), jnp.sum(jnp.square(grad.astype(F32))), F32)
    left_mat = left[...].reshape(size, size)

    def columns(h):
        cols = pl.ds(pl.multiple_of(h * half, 128), half)
        lower = right[pl.ds((1 - core) * groups, groups), :, cols].reshape(half, half)
        shaped = partial[:, cols] + dot(grad, lower, ((1,), (0,)))
        return dot(left_mat, shaped.astype(BF16), ((1,), (0,)))

    dir_sq = jnp.sum(jnp.square(columns(1 - core)))
    near = columns(core)
    dir_sq = jnp.full((1, 1), dir_sq + jnp.sum(jnp.square(near)), F32)
    ratio = jnp.sqrt(grad_sq) / jnp.sqrt(dir_sq + NORM_EPS)
    out[...] = (-near * ratio).astype(BF16)


def terms_kernel(table, own, other, beside, across, mine, grad):
    core, x = table[WHERE, 0], table[WHERE, 1]
    half = own.shape[1]
    rows = mine.shape[1]
    grad[:, pl.ds(pl.multiple_of(core * half, 128), half)] = own[...]
    grad[:, pl.ds(pl.multiple_of((1 - core) * half, 128), half)] = other[...]
    whole = grad[...]

    def of_chip(chip):
        at = pl.ds(pl.multiple_of(chip * 2 * rows, 128), 2 * rows)
        return dot(grad[at], whole, ((1,), (1,))), dot(grad[:, at], whole, ((0,), (0,)))

    for side, term in enumerate(of_chip(lax.rem(x + 1 + 2 * core, 4))):
        for parity in range(2):
            beside[parity, side] = term[parity * rows : (parity + 1) * rows].astype(BF16)
    for chip, out in ((lax.rem(x + 2, 4), across), (x, mine)):
        for side, term in enumerate(of_chip(chip)):
            out[side] = jnp.where(core == 0, term[:rows], term[rows:]).astype(BF16)


def stats_kernel(table, mine, across, beside, passed, left, right, left_hbm, right_hbm, left_out, right_out, sems):
    core, x = table[WHERE, 0], table[WHERE, 1]
    stores = []
    for j in range(left.shape[0]):
        full = table[FULL, j] > 0
        way = lax.rem(table[CHIP, j] + 4 - x, 4)

        def add(here, term):
            @pl.when(jnp.logical_and(full, here))
            def _():
                left_out[j] = STAT_DECAY * left[j] + (1.0 - STAT_DECAY) * term(0).astype(F32)
                right_out[j] = STAT_DECAY * right[j] + (1.0 - STAT_DECAY) * term(1).astype(F32)

        add(way == 0, lambda side: mine[side])
        add(way == 2, lambda side: across[side])
        add(way == 3 - 2 * core, lambda side: beside[core, side])
        add(way == 1 + 2 * core, lambda side: passed[side])

        @pl.when(jnp.logical_not(full))
        def _():
            left_out[j] = STAT_DECAY * left[j]
            right_out[j] = STAT_DECAY * right[j]

        for side, (result, target) in enumerate(((left_out, left_hbm), (right_out, right_hbm))):
            stores.append(pltpu.make_async_copy(result.at[j], target.at[j], sems.at[j, side]))
            stores[-1].start()
    for store in stores:
        store.wait()


def compact_kernel(table, rows, out):
    def body(i, carry):
        block = rows[table[OWNER, i]]
        for x in range(out.shape[0]):
            out[x, i] = block
        return carry

    lax.fori_loop(0, out.shape[1], body, 0, unroll=8)


def place_half(core, table, rows, out_hbm, ordered, sems):
    width = rows.shape[2]
    cols = pl.ds(pl.multiple_of(core * width, 128), width)

    def fill(first, count):
        def body(b, carry):
            ordered[first + b] = rows[table[SOURCE, first + b]]
            return carry

        lax.fori_loop(0, count, body, 0, unroll=8)

    store_in_steps(ordered, out_hbm.at[:, :, cols], sems, 0, fill)


def place_near_kernel(table, rows, out_hbm, ordered, sems):
    place_half(table[WHERE, 0], table, rows, out_hbm, ordered, sems)


def place_far_kernel(table, rows, begun, out_hbm, ordered, sems):
    del begun
    place_half(1 - table[WHERE, 0], table, rows, out_hbm, ordered, sems)


def call(kernel, out_shape, in_specs, scratch=(), out_specs=None, cost=None, aliases=None):
    if out_specs is None:
        out_specs = [VMEM_SPEC] * len(out_shape) if isinstance(out_shape, list) else VMEM_SPEC
    if cost is not None:
        cost = pl.CostEstimate(flops=cost[0], bytes_accessed=cost[1], transcendentals=0)
    return pl.pallas_call(
        kernel,
        out_shape=out_shape,
        in_specs=in_specs,
        out_specs=out_specs,
        scratch_shapes=list(scratch),
        input_output_aliases=aliases or {},
        compiler_params=PARAMS,
        cost_estimate=cost,
    )


def exchange(value, axis):
    return lax.all_to_all(value, axis, 0, 0, tiled=True)


def in_hbm(value):
    return pltpu.with_memory_space_constraint(value, pltpu.HBM)


def turn(value, k):
    chips = lax.axis_size("x")
    return lax.ppermute(value, "x", [(i, (i + k) % chips) for i in range(chips)]) if k else value


def swap_cores(value):
    return lax.ppermute(value, "core", [(0, 1), (1, 0)])


def local(grads, block_slot, left_stat, right_stat, left_root, right_root):
    grads = grads[0]
    chips = lax.axis_size("x")
    x = lax.axis_index("x")
    core = lax.axis_index("core")
    owners = lax.axis_size("y") * lax.axis_size("z")
    me = lax.axis_index("y") * lax.axis_size("z") + lax.axis_index("z")
    capacity, stat_rows, _ = left_stat.shape
    blocks, shard_rows, width = grads.shape
    half = width // 2
    depth = blocks // chips

    piece = jax.ShapeDtypeStruct((2, stat_rows, width), BF16)
    groups = width // stat_rows
    grads = in_hbm(grads.reshape(-1, stat_rows, width))
    left_root, right_root = in_hbm(left_root), in_hbm(right_root)
    grad_groups = grads.shape[0]

    sent = call(
        send_kernel,
        jax.ShapeDtypeStruct((grad_groups + 4 * capacity, stat_rows, half), BF16),
        [SMEM_SPEC] + [HBM_SPEC] * 3,
        [pltpu.SemaphoreType.DMA((5,))],
    )(core.reshape(1), grads, left_root, right_root)
    sent, late_grads = lax.optimization_barrier((sent, grads))
    other = swap_cores(sent)
    kept, table, beside, mine, across = call(
        keep_kernel,
        [jax.ShapeDtypeStruct((grad_groups, stat_rows, half), BF16), jax.ShapeDtypeStruct((8, blocks), jnp.int32)]
        + [piece] * 3,
        [SMEM_SPEC] * 3 + [HBM_SPEC] * 4,
        [
            pltpu.VMEM((1, blocks), jnp.int32),
            pltpu.VMEM((1, blocks), jnp.int32),
            pltpu.SMEM((1, blocks), jnp.int32),
            pltpu.SemaphoreType.DMA((3,)),
            pltpu.SemaphoreType.DMA((3, 2)),
        ],
        cost=(0, 4_000_000),
    )(
        core.reshape(1),
        x.reshape(1),
        me.reshape(1),
        in_hbm(block_slot.reshape(1, blocks)),
        in_hbm(late_grads),
        left_root,
        right_root,
    )

    parts = call(
        pair_sum_kernel,
        jax.ShapeDtypeStruct((chips, depth, shard_rows, half), BF16),
        [SMEM_SPEC, VMEM_SPEC, VMEM_SPEC],
    )(table, kept.reshape(-1, shard_rows, half), other.reshape(-1, shard_rows, half))
    both = jax.ShapeDtypeStruct((2, 2, stat_rows, width), BF16)
    parts, late_table = lax.optimization_barrier((parts, table))
    parts = exchange(parts, "x")
    beside = call(
        functools.partial(pair_roots_kernel, grad_groups, capacity),
        both,
        [SMEM_SPEC, VMEM_SPEC, VMEM_SPEC],
        cost=(0, 1000),
    )(late_table, other, beside)
    parts, beside = lax.optimization_barrier((parts, beside))
    outgoing = call(
        chip_sum_kernel,
        jax.ShapeDtypeStruct((owners, shard_rows, half), BF16),
        [VMEM_SPEC, VMEM_SPEC],
        [
            pltpu.VMEM((depth + 1, shard_rows, half), BF16),
            pltpu.SMEM((8, blocks), jnp.int32),
            pltpu.SemaphoreType.DMA,
        ],
    )(table, parts)

    across = turn(across, 2)
    outgoing, late_other, beside, across = lax.optimization_barrier((outgoing, other, beside, across))
    own = exchange(outgoing, ("y", "z"))
    ways = [(2 * i, 2 * ((i + 1) % chips)) for i in range(chips)]
    ways += [(2 * i + 1, 2 * ((i - 1) % chips) + 1) for i in range(chips)]
    beside = lax.ppermute(beside, ("x", "core"), ways)
    stacked = call(
        stack_kernel,
        jax.ShapeDtypeStruct((3, 2, stat_rows, width), BF16),
        [VMEM_SPEC, VMEM_SPEC],
        cost=(0, 1_000_000),
    )(beside, across)
    others = swap_cores(stacked)
    left, right = call(
        functools.partial(merge_roots_kernel, grad_groups, capacity),
        [jax.ShapeDtypeStruct((groups, stat_rows, width), BF16)] * 2,
        [SMEM_SPEC] + [VMEM_SPEC] * 5,
        cost=(0, 2_000_000),
    )(table, late_other, mine, beside, across, others)

    own = own.reshape(width, half)
    far = swap_cores(own)
    partial, grad_sq = call(
        near_kernel,
        [jax.ShapeDtypeStruct((width, width), F32), jax.ShapeDtypeStruct((8, 128), F32)],
        [SMEM_SPEC, VMEM_SPEC, VMEM_SPEC],
        cost=(270_000_000, 4_000_000),
    )(table, own, right)
    update = call(
        direction_kernel,
        jax.ShapeDtypeStruct((width, half), BF16),
        [SMEM_SPEC] + [VMEM_SPEC] * 5,
    )(table, far, partial, left, right, grad_sq)

    update, own, far = lax.optimization_barrier((update, own, far))
    rows = exchange(update.reshape(owners, shard_rows, half), ("y", "z"))
    beside, across, mine = call(
        terms_kernel,
        [both, piece, piece],
        [SMEM_SPEC, VMEM_SPEC, VMEM_SPEC],
        [pltpu.VMEM((width, width), BF16)],
        cost=(800_000_000, 2_000_000),
    )(table, own, far)
    across = turn(across, 2)
    beside = lax.ppermute(beside, ("x", "core"), ways)
    packed = call(
        compact_kernel,
        jax.ShapeDtypeStruct((chips, depth, shard_rows, half), BF16),
        [SMEM_SPEC, VMEM_SPEC],
    )(table, rows)
    packed, beside, across = lax.optimization_barrier((packed, beside, across))
    near = exchange(packed, "x").reshape(blocks, shard_rows, half)
    passed = swap_cores(lax.dynamic_index_in_dim(beside, 1 - core, keepdims=False))
    stat = jax.ShapeDtypeStruct(left_stat.shape, F32)
    left_new, right_new = call(
        stats_kernel,
        [stat, stat],
        [SMEM_SPEC] + [VMEM_SPEC] * 6,
        [
            pltpu.VMEM(left_stat.shape, F32),
            pltpu.VMEM(right_stat.shape, F32),
            pltpu.SemaphoreType.DMA((capacity, 2)),
        ],
        [HBM_SPEC, HBM_SPEC],
        cost=(10_000_000, 5_000_000),
    )(table, mine, across, beside, passed, left_stat, right_stat)
    near, left_new, right_new = lax.optimization_barrier((near, left_new, right_new))
    beyond = swap_cores(near)
    whole_rows = jax.ShapeDtypeStruct((blocks, shard_rows, width), BF16)
    scratch = [pltpu.VMEM((blocks, shard_rows, half), BF16), pltpu.SemaphoreType.DMA((4,))]
    begun = call(
        place_near_kernel, whole_rows, [SMEM_SPEC, VMEM_SPEC], scratch, HBM_SPEC, cost=(0, 4_000_000)
    )(table, near)
    result = call(
        place_far_kernel, whole_rows, [SMEM_SPEC, VMEM_SPEC, HBM_SPEC], scratch, HBM_SPEC, aliases={2: 0}
    )(table, beyond, begun)
    return (result, left_new, right_new)


def solution(mesh):
    fine = Mesh(mesh.devices.reshape(4, 2, 4, 16), ("x", "core", "y", "z"))
    replica, shard = ("x", "core"), ("y", "z")
    in_specs = (
        P(replica, None, shard, None),
        P(),
        P(shard, replica, None),
        P(shard, replica, None),
        P(shard, replica, None),
        P(shard, replica, None),
    )
    out_specs = (P(None, shard, None), P(shard, replica, None), P(shard, replica, None))
    return jax.shard_map(local, mesh=fine, in_specs=in_specs, out_specs=out_specs, check_vma=False)
```

```python
import functools

import jax
import jax.numpy as jnp
from jax import lax
from jax.experimental import pallas as pl
from jax.experimental.pallas import tpu as pltpu
from jax.sharding import Mesh, PartitionSpec as P

STAT_DECAY = 0.9
NORM_EPS = 1e-12
F32 = jnp.float32
BF16 = jnp.bfloat16
VMEM_SPEC = pl.BlockSpec(memory_space=pltpu.VMEM)
HBM_SPEC = pl.BlockSpec(memory_space=pltpu.HBM)
SMEM_SPEC = pl.BlockSpec(memory_space=pltpu.SMEM)
PARAMS = pltpu.CompilerParams(vmem_limit_bytes=32 * 1024 * 1024)


def dot(a, b, dims):
    return lax.dot_general(a, b, (dims, ((), ())), preferred_element_type=F32)


ORDER, SOURCE, PLACE, OWNER, SLOT, FULL, CHIP, WHERE = range(8)


def fill_table(slots, core, x, me, capacity, chips, first, first_done, table):
    blocks = slots.shape[1]
    square = (blocks, blocks)
    cap_bits, chip_bits = capacity.bit_length() - 1, chips.bit_length() - 1
    depth = blocks // chips
    lane = lax.broadcasted_iota(jnp.int32, square, 1)
    sublane = lax.broadcasted_iota(jnp.int32, square, 0)
    across = jnp.broadcast_to(slots[...], square)
    slot = across.T

    def total(mask, value):
        return jnp.sum(jnp.where(mask, value, 0), axis=0, keepdims=True)

    rank_row = total(slot < across, 1)
    rank = jnp.broadcast_to(rank_row, square).T
    chip = rank & (chips - 1)
    spot = rank >> chip_bits
    owner = slot >> cap_bits
    first[...] = total((owner == me) & (chip == lane), slot & (capacity - 1))
    first_done()
    local_slot = slot == me * capacity + lane
    table[pl.ds(ORDER, 1)] = total(rank == lane, sublane)
    table[pl.ds(SOURCE, 1)] = (rank_row & (chips - 1)) * depth + (rank_row >> chip_bits)
    table[pl.ds(PLACE, 1)] = total((chip == x) & (owner == lane), spot - depth) + depth
    table[pl.ds(OWNER, 1)] = total((chip == x) & (spot == lane), owner)
    table[pl.ds(SLOT, 1)] = first[...]
    table[pl.ds(FULL, 1)] = total(local_slot, 1)
    table[pl.ds(CHIP, 1)] = total(local_slot, chip)
    row = lax.broadcasted_iota(jnp.int32, (1, blocks), 1)
    table[pl.ds(WHERE, 1)] = jnp.where(row == 0, core, x)


def send_kernel(core_ref, grads, left_root, right_root, sent, sems):
    width = sent.shape[2]
    groups = grads.shape[0]
    capacity = left_root.shape[0]
    far = pl.ds(pl.multiple_of((1 - core_ref[0]) * width, 128), width)
    loads = [pltpu.make_async_copy(grads.at[:, :, far], sent.at[pl.ds(0, groups)], sems.at[0])]
    for i in range(4):
        root = (left_root, right_root)[i // 2].at[:, :, pl.ds(i % 2 * width, width)]
        loads.append(pltpu.make_async_copy(root, sent.at[pl.ds(groups + i * capacity, capacity)], sems.at[i + 1]))
    for load in loads:
        load.start()
    for load in loads:
        load.wait()


def keep_kernel(
    core_ref, x_ref, me_ref, slots_hbm, grads, left_root, right_root, kept, table, beside, mine, across, slots, first, scalars, sems, root_sems
):
    core, x = core_ref[0], x_ref[0]
    width = kept.shape[2]
    near = pl.ds(pl.multiple_of(core * width, 128), width)
    slots_load = pltpu.make_async_copy(slots_hbm, slots, sems.at[0])
    load = pltpu.make_async_copy(grads.at[:, :, near], kept, sems.at[1])
    first_load = pltpu.make_async_copy(first, scalars, sems.at[2])
    slots_load.start()
    load.start()
    slots_load.wait()
    fill_table(slots, core, x, me_ref[0], left_root.shape[0], 4, first, first_load.start, table)
    first_load.wait()
    loads = [load]
    for i, (chip, out) in enumerate(((x + 1 + 2 * core, beside), (x, mine), (x + 2, across))):
        slot = scalars[0, lax.rem(chip, 4)]
        for side, root in enumerate((left_root, right_root)):
            loads.append(pltpu.make_async_copy(root.at[slot], out.at[side], root_sems.at[i, side]))
            loads[-1].start()
    for load in loads:
        load.wait()


def from_other(groups, capacity, other, slot, side, out):
    width = other.shape[2]
    for h in range(2):
        out[:, h * width : (h + 1) * width] = other[groups + (2 * side + h) * capacity + slot]


def pair_roots_kernel(groups, capacity, table, other, beside, out):
    core, x = table[WHERE, 0], table[WHERE, 1]
    slot = table[SLOT, lax.rem(x + 1 + 2 * core, 4)]
    out[core] = beside[...]
    for side in range(2):
        from_other(groups, capacity, other, slot, side, out.at[1 - core, side])


def stack_kernel(beside, across, out):
    out[0:2] = beside[...]
    out[2] = across[...]


def merge_roots_kernel(groups, capacity, table, other, mine, beside, across, others, left, right):
    core, x = table[WHERE, 0], table[WHERE, 1]
    near, far, opposite = lax.rem(x + 3 - 2 * core, 4), lax.rem(x + 1 + 2 * core, 4), lax.rem(x + 2, 4)
    for side, out in enumerate((left, right)):
        out[2 * x + core] = mine[side]
        from_other(groups, capacity, other, table[SLOT, x], side, out.at[2 * x + 1 - core])
        for parity in range(2):
            out[2 * near + parity] = beside[parity, side]
            out[2 * far + parity] = others[parity, side]
        out[2 * opposite + core] = across[side]
        out[2 * opposite + 1 - core] = others[2, side]


def pair_sum_kernel(table, own, other, out):
    chips, depth = out.shape[:2]

    def body(i, carry):
        for x in range(chips):
            block = table[ORDER, i * chips + x]
            out[x, i] = own[block] + other[block]
        return carry

    lax.fori_loop(0, depth, body, 0, unroll=8)


def store_in_steps(source, target, sems, dim, fill):
    steps = sems.shape[0]
    count = source.shape[dim] // steps
    stores = []
    for i in range(steps):
        fill(i * count, count)
        part = (slice(None),) * dim + (pl.ds(i * count, count),)
        stores.append(pltpu.make_async_copy(source.at[part], target.at[part], sems.at[i]))
        stores[-1].start()
    for store in stores:
        store.wait()


def chip_sum_kernel(table, parts, out, total, place, sem):
    depth = parts.shape[1]
    load = pltpu.make_async_copy(table, place, sem)
    load.start()
    acc = parts[0].astype(F32)
    for x in range(1, parts.shape[0]):
        acc = acc + parts[x].astype(F32)
    total[0:depth] = acc.astype(BF16)
    total[depth] = jnp.zeros(total.shape[1:], BF16)
    load.wait()

    def body(o, carry):
        out[o] = total[place[PLACE, o]]
        return carry

    lax.fori_loop(0, out.shape[0], body, 0, unroll=8)


def near_kernel(table, own, right, partial, grad_sq):
    core = table[WHERE, 0]
    half = own.shape[1]
    groups = right.shape[0] // 2
    grad = own[...]
    grad_sq[...] = jnp.full(grad_sq.shape, jnp.sum(jnp.square(grad.astype(F32))), F32)
    upper = right[pl.ds(core * groups, groups)].reshape(half, 2 * half)
    partial[...] = dot(grad, upper, ((1,), (0,)))


def direction_kernel(table, other, partial, left, right, grad_sq_near, out):
    core = table[WHERE, 0]
    half = other.shape[1]
    groups = right.shape[0] // 2
    size = 2 * half
    grad = other[...]
    grad_sq = grad_sq_near[0:1, 0:1] + jnp.full((1, 1), jnp.sum(jnp.square(grad.astype(F32))), F32)
    left_mat = left[...].reshape(size, size)

    def columns(h):
        cols = pl.ds(pl.multiple_of(h * half, 128), half)
        lower = right[pl.ds((1 - core) * groups, groups), :, cols].reshape(half, half)
        shaped = partial[:, cols] + dot(grad, lower, ((1,), (0,)))
        return dot(left_mat, shaped.astype(BF16), ((1,), (0,)))

    dir_sq = jnp.sum(jnp.square(columns(1 - core)))
    near = columns(core)
    dir_sq = jnp.full((1, 1), dir_sq + jnp.sum(jnp.square(near)), F32)
    ratio = jnp.sqrt(grad_sq) / jnp.sqrt(dir_sq + NORM_EPS)
    out[...] = (-near * ratio).astype(BF16)


def terms_kernel(table, own, other, beside, across, mine, grad):
    core, x = table[WHERE, 0], table[WHERE, 1]
    half = own.shape[1]
    rows = mine.shape[1]
    grad[:, pl.ds(pl.multiple_of(core * half, 128), half)] = own[...]
    grad[:, pl.ds(pl.multiple_of((1 - core) * half, 128), half)] = other[...]
    whole = grad[...]

    def of_chip(chip):
        at = pl.ds(pl.multiple_of(chip * 2 * rows, 128), 2 * rows)
        return dot(grad[at], whole, ((1,), (1,))), dot(grad[:, at], whole, ((0,), (0,)))

    for side, term in enumerate(of_chip(lax.rem(x + 1 + 2 * core, 4))):
        for parity in range(2):
            beside[parity, side] = term[parity * rows : (parity + 1) * rows].astype(BF16)
    for chip, out in ((lax.rem(x + 2, 4), across), (x, mine)):
        for side, term in enumerate(of_chip(chip)):
            out[side] = jnp.where(core == 0, term[:rows], term[rows:]).astype(BF16)


def stats_kernel(table, mine, across, beside, passed, left, right, left_hbm, right_hbm, left_out, right_out, sems):
    core, x = table[WHERE, 0], table[WHERE, 1]
    stores = []
    for j in range(left.shape[0]):
        full = table[FULL, j] > 0
        way = lax.rem(table[CHIP, j] + 4 - x, 4)

        def add(here, term):
            @pl.when(jnp.logical_and(full, here))
            def _():
                left_out[j] = STAT_DECAY * left[j] + (1.0 - STAT_DECAY) * term(0).astype(F32)
                right_out[j] = STAT_DECAY * right[j] + (1.0 - STAT_DECAY) * term(1).astype(F32)

        add(way == 0, lambda side: mine[side])
        add(way == 2, lambda side: across[side])
        add(way == 3 - 2 * core, lambda side: beside[core, side])
        add(way == 1 + 2 * core, lambda side: passed[side])

        @pl.when(jnp.logical_not(full))
        def _():
            left_out[j] = STAT_DECAY * left[j]
            right_out[j] = STAT_DECAY * right[j]

        for side, (result, target) in enumerate(((left_out, left_hbm), (right_out, right_hbm))):
            stores.append(pltpu.make_async_copy(result.at[j], target.at[j], sems.at[j, side]))
            stores[-1].start()
    for store in stores:
        store.wait()


def compact_kernel(table, rows, out):
    def body(i, carry):
        block = rows[table[OWNER, i]]
        for x in range(out.shape[0]):
            out[x, i] = block
        return carry

    lax.fori_loop(0, out.shape[1], body, 0, unroll=8)


def order_kernel(table, rows, out):
    def body(b, carry):
        out[b] = rows[table[SOURCE, b]]
        return carry

    lax.fori_loop(0, out.shape[0], body, 0, unroll=8)


def place_half(half, rows, out_hbm, sem):
    width = rows.shape[2]
    store = pltpu.make_async_copy(rows, out_hbm.at[:, :, pl.ds(pl.multiple_of(half * width, 128), width)], sem)
    store.start()
    store.wait()


def place_near_kernel(core_ref, rows, out_hbm, sem):
    place_half(core_ref[0], rows, out_hbm, sem)


def place_far_kernel(core_ref, rows, begun, out_hbm, sem):
    del begun
    place_half(1 - core_ref[0], rows, out_hbm, sem)


def call(kernel, out_shape, in_specs, scratch=(), out_specs=None, cost=None, aliases=None):
    if out_specs is None:
        out_specs = [VMEM_SPEC] * len(out_shape) if isinstance(out_shape, list) else VMEM_SPEC
    if cost is not None:
        cost = pl.CostEstimate(flops=cost[0], bytes_accessed=cost[1], transcendentals=0)
    return pl.pallas_call(
        kernel,
        out_shape=out_shape,
        in_specs=in_specs,
        out_specs=out_specs,
        scratch_shapes=list(scratch),
        input_output_aliases=aliases or {},
        compiler_params=PARAMS,
        cost_estimate=cost,
    )


def exchange(value, axis):
    return lax.all_to_all(value, axis, 0, 0, tiled=True)


def in_hbm(value):
    return pltpu.with_memory_space_constraint(value, pltpu.HBM)


def turn(value, k):
    chips = lax.axis_size("x")
    return lax.ppermute(value, "x", [(i, (i + k) % chips) for i in range(chips)]) if k else value


def swap_cores(value):
    return lax.ppermute(value, "core", [(0, 1), (1, 0)])


def local(grads, block_slot, left_stat, right_stat, left_root, right_root):
    grads = grads[0]
    chips = lax.axis_size("x")
    x = lax.axis_index("x")
    core = lax.axis_index("core")
    owners = lax.axis_size("y") * lax.axis_size("z")
    me = lax.axis_index("y") * lax.axis_size("z") + lax.axis_index("z")
    capacity, stat_rows, _ = left_stat.shape
    blocks, shard_rows, width = grads.shape
    half = width // 2
    depth = blocks // chips

    piece = jax.ShapeDtypeStruct((2, stat_rows, width), BF16)
    groups = width // stat_rows
    half_rows = jax.ShapeDtypeStruct((blocks, shard_rows, half), BF16)
    grads = in_hbm(grads.reshape(-1, stat_rows, width))
    left_root, right_root = in_hbm(left_root), in_hbm(right_root)
    grad_groups = grads.shape[0]

    sent = call(
        send_kernel,
        jax.ShapeDtypeStruct((grad_groups + 4 * capacity, stat_rows, half), BF16),
        [SMEM_SPEC] + [HBM_SPEC] * 3,
        [pltpu.SemaphoreType.DMA((5,))],
    )(core.reshape(1), grads, left_root, right_root)
    sent, late_grads = lax.optimization_barrier((sent, grads))
    other = swap_cores(sent)
    kept, table, beside, mine, across = call(
        keep_kernel,
        [jax.ShapeDtypeStruct((grad_groups, stat_rows, half), BF16), jax.ShapeDtypeStruct((8, blocks), jnp.int32)]
        + [piece] * 3,
        [SMEM_SPEC] * 3 + [HBM_SPEC] * 4,
        [
            pltpu.VMEM((1, blocks), jnp.int32),
            pltpu.VMEM((1, blocks), jnp.int32),
            pltpu.SMEM((1, blocks), jnp.int32),
            pltpu.SemaphoreType.DMA((3,)),
            pltpu.SemaphoreType.DMA((3, 2)),
        ],
        cost=(0, 4_000_000),
    )(
        core.reshape(1),
        x.reshape(1),
        me.reshape(1),
        in_hbm(block_slot.reshape(1, blocks)),
        in_hbm(late_grads),
        left_root,
        right_root,
    )

    parts = call(
        pair_sum_kernel,
        jax.ShapeDtypeStruct((chips, depth, shard_rows, half), BF16),
        [SMEM_SPEC, VMEM_SPEC, VMEM_SPEC],
    )(table, kept.reshape(-1, shard_rows, half), other.reshape(-1, shard_rows, half))
    both = jax.ShapeDtypeStruct((2, 2, stat_rows, width), BF16)
    parts, late_table = lax.optimization_barrier((parts, table))
    parts = exchange(parts, "x")
    beside = call(
        functools.partial(pair_roots_kernel, grad_groups, capacity),
        both,
        [SMEM_SPEC, VMEM_SPEC, VMEM_SPEC],
        cost=(0, 1000),
    )(late_table, other, beside)
    ways = [(2 * i, 2 * ((i + 1) % chips)) for i in range(chips)]
    ways += [(2 * i + 1, 2 * ((i - 1) % chips) + 1) for i in range(chips)]
    beside = lax.ppermute(beside, ("x", "core"), ways)
    outgoing = call(
        chip_sum_kernel,
        jax.ShapeDtypeStruct((owners, shard_rows, half), BF16),
        [VMEM_SPEC, VMEM_SPEC],
        [
            pltpu.VMEM((depth + 1, shard_rows, half), BF16),
            pltpu.SMEM((8, blocks), jnp.int32),
            pltpu.SemaphoreType.DMA,
        ],
    )(table, parts)

    outgoing, late_other, beside, across = lax.optimization_barrier((outgoing, other, beside, across))
    own = exchange(outgoing, ("y", "z"))
    across = turn(across, 2)
    stacked = call(
        stack_kernel,
        jax.ShapeDtypeStruct((3, 2, stat_rows, width), BF16),
        [VMEM_SPEC, VMEM_SPEC],
        cost=(0, 1_000_000),
    )(beside, across)
    others = swap_cores(stacked)
    left, right = call(
        functools.partial(merge_roots_kernel, grad_groups, capacity),
        [jax.ShapeDtypeStruct((groups, stat_rows, width), BF16)] * 2,
        [SMEM_SPEC] + [VMEM_SPEC] * 5,
        cost=(0, 2_000_000),
    )(table, late_other, mine, beside, across, others)

    own = own.reshape(width, half)
    far = swap_cores(own)
    partial, grad_sq = call(
        near_kernel,
        [jax.ShapeDtypeStruct((width, width), F32), jax.ShapeDtypeStruct((8, 128), F32)],
        [SMEM_SPEC, VMEM_SPEC, VMEM_SPEC],
        cost=(270_000_000, 4_000_000),
    )(table, own, right)
    update = call(
        direction_kernel,
        jax.ShapeDtypeStruct((width, half), BF16),
        [SMEM_SPEC] + [VMEM_SPEC] * 5,
    )(table, far, partial, left, right, grad_sq)

    update, own, far = lax.optimization_barrier((update, own, far))
    rows = exchange(update.reshape(owners, shard_rows, half), ("y", "z"))
    beside, across, mine = call(
        terms_kernel,
        [both, piece, piece],
        [SMEM_SPEC, VMEM_SPEC, VMEM_SPEC],
        [pltpu.VMEM((width, width), BF16)],
        cost=(800_000_000, 2_000_000),
    )(table, own, far)
    across = turn(across, 2)
    beside = lax.ppermute(beside, ("x", "core"), ways)
    packed = call(
        compact_kernel,
        jax.ShapeDtypeStruct((chips, depth, shard_rows, half), BF16),
        [SMEM_SPEC, VMEM_SPEC],
    )(table, rows)
    packed, beside, across = lax.optimization_barrier((packed, beside, across))
    near = exchange(packed, "x").reshape(blocks, shard_rows, half)
    passed = swap_cores(lax.dynamic_index_in_dim(beside, 1 - core, keepdims=False))
    stat = jax.ShapeDtypeStruct(left_stat.shape, F32)
    left_new, right_new = call(
        stats_kernel,
        [stat, stat],
        [SMEM_SPEC] + [VMEM_SPEC] * 6,
        [
            pltpu.VMEM(left_stat.shape, F32),
            pltpu.VMEM(right_stat.shape, F32),
            pltpu.SemaphoreType.DMA((capacity, 2)),
        ],
        [HBM_SPEC, HBM_SPEC],
        cost=(10_000_000, 5_000_000),
    )(table, mine, across, beside, passed, left_stat, right_stat)
    near, left_new, right_new = lax.optimization_barrier((near, left_new, right_new))
    near = call(order_kernel, half_rows, [SMEM_SPEC, VMEM_SPEC])(table, near)
    beyond = swap_cores(near)
    whole_rows = jax.ShapeDtypeStruct((blocks, shard_rows, width), BF16)
    begun = call(
        place_near_kernel,
        whole_rows,
        [SMEM_SPEC, VMEM_SPEC],
        [pltpu.SemaphoreType.DMA],
        HBM_SPEC,
        cost=(0, 4_000_000),
    )(core.reshape(1), near)
    result = call(
        place_far_kernel,
        whole_rows,
        [SMEM_SPEC, VMEM_SPEC, HBM_SPEC],
        [pltpu.SemaphoreType.DMA],
        HBM_SPEC,
        aliases={2: 0},
    )(core.reshape(1), beyond, begun)
    return (result, left_new, right_new)


def solution(mesh):
    fine = Mesh(mesh.devices.reshape(4, 2, 4, 16), ("x", "core", "y", "z"))
    replica, shard = ("x", "core"), ("y", "z")
    in_specs = (
        P(replica, None, shard, None),
        P(),
        P(shard, replica, None),
        P(shard, replica, None),
        P(shard, replica, None),
        P(shard, replica, None),
    )
    out_specs = (P(None, shard, None), P(shard, replica, None), P(shard, replica, None))
    return jax.shard_map(local, mesh=fine, in_specs=in_specs, out_specs=out_specs, check_vma=False)
```

```python
import functools

import jax
import jax.numpy as jnp
from jax import lax
from jax.experimental import pallas as pl
from jax.experimental.pallas import tpu as pltpu
from jax.sharding import Mesh, PartitionSpec as P

STAT_DECAY = 0.9
NORM_EPS = 1e-12
F32 = jnp.float32
BF16 = jnp.bfloat16
VMEM_SPEC = pl.BlockSpec(memory_space=pltpu.VMEM)
HBM_SPEC = pl.BlockSpec(memory_space=pltpu.HBM)
SMEM_SPEC = pl.BlockSpec(memory_space=pltpu.SMEM)
PARAMS = pltpu.CompilerParams(vmem_limit_bytes=32 * 1024 * 1024)


def dot(a, b, dims):
    return lax.dot_general(a, b, (dims, ((), ())), preferred_element_type=F32)


ORDER, SOURCE, PLACE, OWNER, SLOT, FULL, CHIP, WHERE = range(8)


def fill_table(slots, core, x, me, capacity, chips, first, first_done, table):
    blocks = slots.shape[1]
    square = (blocks, blocks)
    cap_bits, chip_bits = capacity.bit_length() - 1, chips.bit_length() - 1
    depth = blocks // chips
    lane = lax.broadcasted_iota(jnp.int32, square, 1)
    sublane = lax.broadcasted_iota(jnp.int32, square, 0)
    across = jnp.broadcast_to(slots[...], square)
    slot = across.T

    def total(mask, value):
        return jnp.sum(jnp.where(mask, value, 0), axis=0, keepdims=True)

    rank_row = total(slot < across, 1)
    rank = jnp.broadcast_to(rank_row, square).T
    chip = rank & (chips - 1)
    spot = rank >> chip_bits
    owner = slot >> cap_bits
    first[...] = total((owner == me) & (chip == lane), slot & (capacity - 1))
    first_done()
    local_slot = slot == me * capacity + lane
    table[pl.ds(ORDER, 1)] = total(rank == lane, sublane)
    table[pl.ds(SOURCE, 1)] = (rank_row & (chips - 1)) * depth + (rank_row >> chip_bits)
    table[pl.ds(PLACE, 1)] = total((chip == x) & (owner == lane), spot - depth) + depth
    table[pl.ds(OWNER, 1)] = total((chip == x) & (spot == lane), owner)
    table[pl.ds(SLOT, 1)] = first[...]
    table[pl.ds(FULL, 1)] = total(local_slot, 1)
    table[pl.ds(CHIP, 1)] = total(local_slot, chip)
    row = lax.broadcasted_iota(jnp.int32, (1, blocks), 1)
    table[pl.ds(WHERE, 1)] = jnp.where(row == 0, core, x)


def send_kernel(core_ref, grads, left_root, right_root, sent, sems):
    width = sent.shape[2]
    groups = grads.shape[0]
    capacity = left_root.shape[0]
    far = pl.ds(pl.multiple_of((1 - core_ref[0]) * width, 128), width)
    loads = [pltpu.make_async_copy(grads.at[:, :, far], sent.at[pl.ds(0, groups)], sems.at[0])]
    for i in range(4):
        root = (left_root, right_root)[i // 2].at[:, :, pl.ds(i % 2 * width, width)]
        loads.append(pltpu.make_async_copy(root, sent.at[pl.ds(groups + i * capacity, capacity)], sems.at[i + 1]))
    for load in loads:
        load.start()
    for load in loads:
        load.wait()


def keep_kernel(
    core_ref, x_ref, me_ref, slots_hbm, grads, left_root, right_root, kept, table, beside, mine, across, slots, first, scalars, sems, root_sems
):
    core, x = core_ref[0], x_ref[0]
    width = kept.shape[2]
    near = pl.ds(pl.multiple_of(core * width, 128), width)
    slots_load = pltpu.make_async_copy(slots_hbm, slots, sems.at[0])
    load = pltpu.make_async_copy(grads.at[:, :, near], kept, sems.at[1])
    first_load = pltpu.make_async_copy(first, scalars, sems.at[2])
    slots_load.start()
    load.start()
    slots_load.wait()
    fill_table(slots, core, x, me_ref[0], left_root.shape[0], 4, first, first_load.start, table)
    first_load.wait()
    loads = [load]
    for i, (chip, out) in enumerate(((x + 1 + 2 * core, beside), (x, mine), (x + 2, across))):
        slot = scalars[0, lax.rem(chip, 4)]
        for side, root in enumerate((left_root, right_root)):
            loads.append(pltpu.make_async_copy(root.at[slot], out.at[side], root_sems.at[i, side]))
            loads[-1].start()
    for load in loads:
        load.wait()


def from_other(groups, capacity, other, slot, side, out):
    width = other.shape[2]
    for h in range(2):
        out[:, h * width : (h + 1) * width] = other[groups + (2 * side + h) * capacity + slot]


def pair_roots_kernel(groups, capacity, table, other, beside, out):
    core, x = table[WHERE, 0], table[WHERE, 1]
    slot = table[SLOT, lax.rem(x + 1 + 2 * core, 4)]
    out[core] = beside[...]
    for side in range(2):
        from_other(groups, capacity, other, slot, side, out.at[1 - core, side])


def stack_kernel(beside, across, out):
    out[0:2] = beside[...]
    out[2] = across[...]


def merge_roots_kernel(groups, capacity, table, other, mine, beside, across, others, left, right):
    core, x = table[WHERE, 0], table[WHERE, 1]
    near, far, opposite = lax.rem(x + 3 - 2 * core, 4), lax.rem(x + 1 + 2 * core, 4), lax.rem(x + 2, 4)
    for side, out in enumerate((left, right)):
        out[2 * x + core] = mine[side]
        from_other(groups, capacity, other, table[SLOT, x], side, out.at[2 * x + 1 - core])
        for parity in range(2):
            out[2 * near + parity] = beside[parity, side]
            out[2 * far + parity] = others[parity, side]
        out[2 * opposite + core] = across[side]
        out[2 * opposite + 1 - core] = others[2, side]


def pair_sum_kernel(table, own, other, out):
    chips, depth = out.shape[:2]

    def body(i, carry):
        for x in range(chips):
            block = table[ORDER, i * chips + x]
            out[x, i] = own[block] + other[block]
        return carry

    lax.fori_loop(0, depth, body, 0, unroll=8)


def store_in_steps(source, target, sems, dim, fill):
    steps = sems.shape[0]
    count = source.shape[dim] // steps
    stores = []
    for i in range(steps):
        fill(i * count, count)
        part = (slice(None),) * dim + (pl.ds(i * count, count),)
        stores.append(pltpu.make_async_copy(source.at[part], target.at[part], sems.at[i]))
        stores[-1].start()
    for store in stores:
        store.wait()


def chip_sum_kernel(table, parts, out, total, place, sem):
    depth = parts.shape[1]
    load = pltpu.make_async_copy(table, place, sem)
    load.start()
    acc = parts[0].astype(F32)
    for x in range(1, parts.shape[0]):
        acc = acc + parts[x].astype(F32)
    total[0:depth] = acc.astype(BF16)
    total[depth] = jnp.zeros(total.shape[1:], BF16)
    load.wait()

    def body(o, carry):
        out[o] = total[place[PLACE, o]]
        return carry

    lax.fori_loop(0, out.shape[0], body, 0, unroll=8)


def near_kernel(table, own, right, partial, grad_sq):
    core = table[WHERE, 0]
    half = own.shape[1]
    groups = right.shape[0] // 2
    grad = own[...]
    grad_sq[...] = jnp.full(grad_sq.shape, jnp.sum(jnp.square(grad.astype(F32))), F32)
    upper = right[pl.ds(core * groups, groups)].reshape(half, 2 * half)
    partial[...] = dot(grad, upper, ((1,), (0,)))


def direction_kernel(table, other, partial, left, right, grad_sq_near, out):
    core = table[WHERE, 0]
    half = other.shape[1]
    groups = right.shape[0] // 2
    size = 2 * half
    grad = other[...]
    grad_sq = grad_sq_near[0:1, 0:1] + jnp.full((1, 1), jnp.sum(jnp.square(grad.astype(F32))), F32)
    left_mat = left[...].reshape(size, size)

    def columns(h):
        cols = pl.ds(pl.multiple_of(h * half, 128), half)
        lower = right[pl.ds((1 - core) * groups, groups), :, cols].reshape(half, half)
        shaped = partial[:, cols] + dot(grad, lower, ((1,), (0,)))
        return dot(left_mat, shaped.astype(BF16), ((1,), (0,)))

    dir_sq = jnp.sum(jnp.square(columns(1 - core)))
    near = columns(core)
    dir_sq = jnp.full((1, 1), dir_sq + jnp.sum(jnp.square(near)), F32)
    ratio = jnp.sqrt(grad_sq) / jnp.sqrt(dir_sq + NORM_EPS)
    out[...] = (-near * ratio).astype(BF16)


def terms_kernel(table, own, other, beside, across, mine, grad):
    core, x = table[WHERE, 0], table[WHERE, 1]
    half = own.shape[1]
    rows = mine.shape[1]
    grad[:, pl.ds(pl.multiple_of(core * half, 128), half)] = own[...]
    grad[:, pl.ds(pl.multiple_of((1 - core) * half, 128), half)] = other[...]
    whole = grad[...]

    def of_chip(chip):
        at = pl.ds(pl.multiple_of(chip * 2 * rows, 128), 2 * rows)
        return dot(grad[at], whole, ((1,), (1,))), dot(grad[:, at], whole, ((0,), (0,)))

    for side, term in enumerate(of_chip(lax.rem(x + 1 + 2 * core, 4))):
        for parity in range(2):
            beside[parity, side] = term[parity * rows : (parity + 1) * rows].astype(BF16)
    for chip, out in ((lax.rem(x + 2, 4), across), (x, mine)):
        for side, term in enumerate(of_chip(chip)):
            out[side] = jnp.where(core == 0, term[:rows], term[rows:]).astype(BF16)


def stats_kernel(table, mine, across, beside, passed, left, right, left_hbm, right_hbm, left_out, right_out, sems):
    core, x = table[WHERE, 0], table[WHERE, 1]
    stores = []
    for j in range(left.shape[0]):
        full = table[FULL, j] > 0
        way = lax.rem(table[CHIP, j] + 4 - x, 4)

        def add(here, term):
            @pl.when(jnp.logical_and(full, here))
            def _():
                left_out[j] = STAT_DECAY * left[j] + (1.0 - STAT_DECAY) * term(0).astype(F32)
                right_out[j] = STAT_DECAY * right[j] + (1.0 - STAT_DECAY) * term(1).astype(F32)

        add(way == 0, lambda side: mine[side])
        add(way == 2, lambda side: across[side])
        add(way == 3 - 2 * core, lambda side: beside[core, side])
        add(way == 1 + 2 * core, lambda side: passed[side])

        @pl.when(jnp.logical_not(full))
        def _():
            left_out[j] = STAT_DECAY * left[j]
            right_out[j] = STAT_DECAY * right[j]

        for side, (result, target) in enumerate(((left_out, left_hbm), (right_out, right_hbm))):
            stores.append(pltpu.make_async_copy(result.at[j], target.at[j], sems.at[j, side]))
            stores[-1].start()
    for store in stores:
        store.wait()


def compact_kernel(table, rows, out):
    def body(i, carry):
        block = rows[table[OWNER, i]]
        for x in range(out.shape[0]):
            out[x, i] = block
        return carry

    lax.fori_loop(0, out.shape[1], body, 0, unroll=8)


def order_kernel(table, rows, out):
    def body(b, carry):
        out[b] = rows[table[SOURCE, b]]
        return carry

    lax.fori_loop(0, out.shape[0], body, 0, unroll=8)


def place_half(half, rows, out_hbm, sem):
    width = rows.shape[2]
    store = pltpu.make_async_copy(rows, out_hbm.at[:, :, pl.ds(pl.multiple_of(half * width, 128), width)], sem)
    store.start()
    store.wait()


def place_near_kernel(core_ref, rows, out_hbm, sem):
    place_half(core_ref[0], rows, out_hbm, sem)


def place_far_kernel(core_ref, rows, begun, out_hbm, sem):
    del begun
    place_half(1 - core_ref[0], rows, out_hbm, sem)


def call(kernel, out_shape, in_specs, scratch=(), out_specs=None, cost=None, aliases=None):
    if out_specs is None:
        out_specs = [VMEM_SPEC] * len(out_shape) if isinstance(out_shape, list) else VMEM_SPEC
    if cost is not None:
        cost = pl.CostEstimate(flops=cost[0], bytes_accessed=cost[1], transcendentals=0)
    return pl.pallas_call(
        kernel,
        out_shape=out_shape,
        in_specs=in_specs,
        out_specs=out_specs,
        scratch_shapes=list(scratch),
        input_output_aliases=aliases or {},
        compiler_params=PARAMS,
        cost_estimate=cost,
    )


def exchange(value, axis):
    return lax.all_to_all(value, axis, 0, 0, tiled=True)


def in_hbm(value):
    return pltpu.with_memory_space_constraint(value, pltpu.HBM)


def turn(value, k):
    chips = lax.axis_size("x")
    return lax.ppermute(value, "x", [(i, (i + k) % chips) for i in range(chips)]) if k else value


def swap_cores(value):
    return lax.ppermute(value, "core", [(0, 1), (1, 0)])


def local(grads, block_slot, left_stat, right_stat, left_root, right_root):
    grads = grads[0]
    chips = lax.axis_size("x")
    x = lax.axis_index("x")
    core = lax.axis_index("core")
    owners = lax.axis_size("y") * lax.axis_size("z")
    me = lax.axis_index("y") * lax.axis_size("z") + lax.axis_index("z")
    capacity, stat_rows, _ = left_stat.shape
    blocks, shard_rows, width = grads.shape
    half = width // 2
    depth = blocks // chips

    piece = jax.ShapeDtypeStruct((2, stat_rows, width), BF16)
    groups = width // stat_rows
    half_rows = jax.ShapeDtypeStruct((blocks, shard_rows, half), BF16)
    grads = in_hbm(grads.reshape(-1, stat_rows, width))
    left_root, right_root = in_hbm(left_root), in_hbm(right_root)
    grad_groups = grads.shape[0]

    sent = call(
        send_kernel,
        jax.ShapeDtypeStruct((grad_groups + 4 * capacity, stat_rows, half), BF16),
        [SMEM_SPEC] + [HBM_SPEC] * 3,
        [pltpu.SemaphoreType.DMA((5,))],
    )(core.reshape(1), grads, left_root, right_root)
    sent, late_grads = lax.optimization_barrier((sent, grads))
    other = swap_cores(sent)
    kept, table, beside, mine, across = call(
        keep_kernel,
        [jax.ShapeDtypeStruct((grad_groups, stat_rows, half), BF16), jax.ShapeDtypeStruct((8, blocks), jnp.int32)]
        + [piece] * 3,
        [SMEM_SPEC] * 3 + [HBM_SPEC] * 4,
        [
            pltpu.VMEM((1, blocks), jnp.int32),
            pltpu.VMEM((1, blocks), jnp.int32),
            pltpu.SMEM((1, blocks), jnp.int32),
            pltpu.SemaphoreType.DMA((3,)),
            pltpu.SemaphoreType.DMA((3, 2)),
        ],
        cost=(0, 4_000_000),
    )(
        core.reshape(1),
        x.reshape(1),
        me.reshape(1),
        in_hbm(block_slot.reshape(1, blocks)),
        in_hbm(late_grads),
        left_root,
        right_root,
    )

    parts = call(
        pair_sum_kernel,
        jax.ShapeDtypeStruct((chips, depth, shard_rows, half), BF16),
        [SMEM_SPEC, VMEM_SPEC, VMEM_SPEC],
    )(table, kept.reshape(-1, shard_rows, half), other.reshape(-1, shard_rows, half))
    both = jax.ShapeDtypeStruct((2, 2, stat_rows, width), BF16)
    parts, late_table = lax.optimization_barrier((parts, table))
    parts = exchange(parts, "x")
    beside = call(
        functools.partial(pair_roots_kernel, grad_groups, capacity),
        both,
        [SMEM_SPEC, VMEM_SPEC, VMEM_SPEC],
        cost=(0, 1000),
    )(late_table, other, beside)
    ways = [(2 * i, 2 * ((i + 1) % chips)) for i in range(chips)]
    ways += [(2 * i + 1, 2 * ((i - 1) % chips) + 1) for i in range(chips)]
    beside = lax.ppermute(beside, ("x", "core"), ways)
    outgoing = call(
        chip_sum_kernel,
        jax.ShapeDtypeStruct((owners, shard_rows, half), BF16),
        [VMEM_SPEC, VMEM_SPEC],
        [
            pltpu.VMEM((depth + 1, shard_rows, half), BF16),
            pltpu.SMEM((8, blocks), jnp.int32),
            pltpu.SemaphoreType.DMA,
        ],
    )(table, parts)

    outgoing, late_other, beside, across = lax.optimization_barrier((outgoing, other, beside, across))
    own = exchange(outgoing, ("y", "z"))
    across = turn(across, 2)
    stacked = call(
        stack_kernel,
        jax.ShapeDtypeStruct((3, 2, stat_rows, width), BF16),
        [VMEM_SPEC, VMEM_SPEC],
        cost=(0, 1_000_000),
    )(beside, across)
    others = swap_cores(stacked)
    left, right = call(
        functools.partial(merge_roots_kernel, grad_groups, capacity),
        [jax.ShapeDtypeStruct((groups, stat_rows, width), BF16)] * 2,
        [SMEM_SPEC] + [VMEM_SPEC] * 5,
        cost=(0, 2_000_000),
    )(table, late_other, mine, beside, across, others)

    own = own.reshape(width, half)
    far = swap_cores(own)
    partial, grad_sq = call(
        near_kernel,
        [jax.ShapeDtypeStruct((width, width), F32), jax.ShapeDtypeStruct((8, 128), F32)],
        [SMEM_SPEC, VMEM_SPEC, VMEM_SPEC],
        cost=(270_000_000, 4_000_000),
    )(table, own, right)
    update = call(
        direction_kernel,
        jax.ShapeDtypeStruct((width, half), BF16),
        [SMEM_SPEC] + [VMEM_SPEC] * 5,
    )(table, far, partial, left, right, grad_sq)

    update, own, far = lax.optimization_barrier((update, own, far))
    rows = exchange(update.reshape(owners, shard_rows, half), ("y", "z"))
    beside, across, mine = call(
        terms_kernel,
        [both, piece, piece],
        [SMEM_SPEC, VMEM_SPEC, VMEM_SPEC],
        [pltpu.VMEM((width, width), BF16)],
        cost=(800_000_000, 2_000_000),
    )(table, own, far)
    across = turn(across, 2)
    beside = lax.ppermute(beside, ("x", "core"), ways)
    packed = call(
        compact_kernel,
        jax.ShapeDtypeStruct((chips, depth, shard_rows, half), BF16),
        [SMEM_SPEC, VMEM_SPEC],
    )(table, rows)
    passed = swap_cores(lax.dynamic_index_in_dim(beside, 1 - core, keepdims=False))
    packed, beside, across, passed = lax.optimization_barrier((packed, beside, across, passed))
    near = exchange(packed, "x").reshape(blocks, shard_rows, half)
    near, beside, across, passed = lax.optimization_barrier((near, beside, across, passed))
    stat = jax.ShapeDtypeStruct(left_stat.shape, F32)
    left_new, right_new = call(
        stats_kernel,
        [stat, stat],
        [SMEM_SPEC] + [VMEM_SPEC] * 6,
        [
            pltpu.VMEM(left_stat.shape, F32),
            pltpu.VMEM(right_stat.shape, F32),
            pltpu.SemaphoreType.DMA((capacity, 2)),
        ],
        [HBM_SPEC, HBM_SPEC],
        cost=(10_000_000, 5_000_000),
    )(table, mine, across, beside, passed, left_stat, right_stat)
    near = call(order_kernel, half_rows, [SMEM_SPEC, VMEM_SPEC])(table, near)
    beyond = swap_cores(near)
    whole_rows = jax.ShapeDtypeStruct((blocks, shard_rows, width), BF16)
    begun = call(
        place_near_kernel,
        whole_rows,
        [SMEM_SPEC, VMEM_SPEC],
        [pltpu.SemaphoreType.DMA],
        HBM_SPEC,
        cost=(0, 4_000_000),
    )(core.reshape(1), near)
    result = call(
        place_far_kernel,
        whole_rows,
        [SMEM_SPEC, VMEM_SPEC, HBM_SPEC],
        [pltpu.SemaphoreType.DMA],
        HBM_SPEC,
        aliases={2: 0},
    )(core.reshape(1), beyond, begun)
    return (result, left_new, right_new)


def solution(mesh):
    fine = Mesh(mesh.devices.reshape(4, 2, 4, 16), ("x", "core", "y", "z"))
    replica, shard = ("x", "core"), ("y", "z")
    in_specs = (
        P(replica, None, shard, None),
        P(),
        P(shard, replica, None),
        P(shard, replica, None),
        P(shard, replica, None),
        P(shard, replica, None),
    )
    out_specs = (P(None, shard, None), P(shard, replica, None), P(shard, replica, None))
    return jax.shard_map(local, mesh=fine, in_specs=in_specs, out_specs=out_specs, check_vma=False)
```

```python
import functools

import jax
import jax.numpy as jnp
from jax import lax
from jax.experimental import pallas as pl
from jax.experimental.pallas import tpu as pltpu
from jax.sharding import Mesh, PartitionSpec as P

STAT_DECAY = 0.9
NORM_EPS = 1e-12
F32 = jnp.float32
BF16 = jnp.bfloat16
VMEM_SPEC = pl.BlockSpec(memory_space=pltpu.VMEM)
HBM_SPEC = pl.BlockSpec(memory_space=pltpu.HBM)
SMEM_SPEC = pl.BlockSpec(memory_space=pltpu.SMEM)
PARAMS = pltpu.CompilerParams(vmem_limit_bytes=32 * 1024 * 1024)


def dot(a, b, dims):
    return lax.dot_general(a, b, (dims, ((), ())), preferred_element_type=F32)


def fill_tables(slots, x, me, capacity, chips, order, source, place, owned, slot_of, chip_of, slot_done):
    blocks = slots.shape[1]
    square = (blocks, blocks)
    cap_bits, chip_bits = capacity.bit_length() - 1, chips.bit_length() - 1
    depth = blocks // chips
    lane = lax.broadcasted_iota(jnp.int32, square, 1)
    sublane = lax.broadcasted_iota(jnp.int32, square, 0)
    across = jnp.broadcast_to(slots[...], square)
    slot = across.T

    def total(mask, value):
        return jnp.sum(jnp.where(mask, value, 0), axis=0, keepdims=True)

    rank_row = total(slot < across, 1)
    rank = jnp.broadcast_to(rank_row, square).T
    chip = rank & (chips - 1)
    spot = rank >> chip_bits
    owner = slot >> cap_bits
    slot_of[...] = total((owner == me) & (chip == lane), slot & (capacity - 1))
    slot_done()
    order[...] = total(rank == lane, sublane)
    source[...] = (rank_row & (chips - 1)) * depth + (rank_row >> chip_bits)
    place[...] = total((chip == x) & (owner == lane), spot - depth) + depth
    owned[...] = total((chip == x) & (spot == lane), owner)
    chip_of[...] = total(slot == me * capacity + lane, chip + 1) - 1


def send_kernel(grads, left_root, right_root, sent, sems):
    width = sent.shape[2]
    groups = grads.shape[0]
    capacity = left_root.shape[0]
    far = pl.ds(pl.multiple_of((1 - lax.axis_index("core")) * width, 128), width)
    loads = [pltpu.make_async_copy(grads.at[:, :, far], sent.at[pl.ds(0, groups)], sems.at[0])]
    for i in range(4):
        root = (left_root, right_root)[i // 2].at[:, :, pl.ds(i % 2 * width, width)]
        loads.append(pltpu.make_async_copy(root, sent.at[pl.ds(groups + i * capacity, capacity)], sems.at[i + 1]))
    for load in loads:
        load.start()
    for load in loads:
        load.wait()


def keep_kernel(slots_hbm, grads, left_root, right_root, kept, beside, mine, across, *refs):
    tables, (slots, scalars, sems, root_sems) = refs[:6], refs[6:]
    core, x = lax.axis_index("core"), lax.axis_index("x")
    me = lax.axis_index("y") * lax.axis_size("z") + lax.axis_index("z")
    width = kept.shape[2]
    near = pl.ds(pl.multiple_of(core * width, 128), width)
    slots_load = pltpu.make_async_copy(slots_hbm, slots, sems.at[0])
    load = pltpu.make_async_copy(grads.at[:, :, near], kept, sems.at[1])
    slot_load = pltpu.make_async_copy(tables[4], scalars, sems.at[2])
    slots_load.start()
    load.start()
    slots_load.wait()
    fill_tables(slots, x, me, left_root.shape[0], 4, *tables, slot_load.start)
    slot_load.wait()
    loads = [load]
    for i, (chip, out) in enumerate(((x + 1 + 2 * core, beside), (x, mine), (x + 2, across))):
        slot = scalars[0, lax.rem(chip, 4)]
        for side, root in enumerate((left_root, right_root)):
            loads.append(pltpu.make_async_copy(root.at[slot], out.at[side], root_sems.at[i, side]))
            loads[-1].start()
    for load in loads:
        load.wait()


def from_other(groups, capacity, other, slot, side, out):
    width = other.shape[2]
    for h in range(2):
        out[:, h * width : (h + 1) * width] = other[groups + (2 * side + h) * capacity + slot]


def pair_roots_kernel(groups, capacity, slot_of, other, beside, out):
    core, x = lax.axis_index("core"), lax.axis_index("x")
    slot = slot_of[0, lax.rem(x + 1 + 2 * core, 4)]
    out[core] = beside[...]
    for side in range(2):
        from_other(groups, capacity, other, slot, side, out.at[1 - core, side])


def stack_kernel(beside, across, out):
    out[0:2] = beside[...]
    out[2] = across[...]


def merge_roots_kernel(groups, capacity, slot_of, other, mine, beside, across, others, left, right):
    core, x = lax.axis_index("core"), lax.axis_index("x")
    near, far, opposite = lax.rem(x + 3 - 2 * core, 4), lax.rem(x + 1 + 2 * core, 4), lax.rem(x + 2, 4)
    for side, out in enumerate((left, right)):
        out[2 * x + core] = mine[side]
        from_other(groups, capacity, other, slot_of[0, x], side, out.at[2 * x + 1 - core])
        for parity in range(2):
            out[2 * near + parity] = beside[parity, side]
            out[2 * far + parity] = others[parity, side]
        out[2 * opposite + core] = across[side]
        out[2 * opposite + 1 - core] = others[2, side]


def pair_sum_kernel(order, own, other, out):
    chips, depth = out.shape[:2]

    def body(i, carry):
        for x in range(chips):
            block = order[0, i * chips + x]
            out[x, i] = own[block] + other[block]
        return carry

    lax.fori_loop(0, depth, body, 0, unroll=8)


def store_in_steps(source, target, sems, dim, fill):
    steps = sems.shape[0]
    count = source.shape[dim] // steps
    stores = []
    for i in range(steps):
        fill(i * count, count)
        part = (slice(None),) * dim + (pl.ds(i * count, count),)
        stores.append(pltpu.make_async_copy(source.at[part], target.at[part], sems.at[i]))
        stores[-1].start()
    for store in stores:
        store.wait()


def chip_sum_kernel(place_vmem, parts, out, total, place, sem):
    depth = parts.shape[1]
    load = pltpu.make_async_copy(place_vmem, place, sem)
    load.start()
    acc = parts[0].astype(F32)
    for x in range(1, parts.shape[0]):
        acc = acc + parts[x].astype(F32)
    total[0:depth] = acc.astype(BF16)
    total[depth] = jnp.zeros(total.shape[1:], BF16)
    load.wait()

    def body(o, carry):
        out[o] = total[place[0, o]]
        return carry

    lax.fori_loop(0, out.shape[0], body, 0, unroll=8)


def near_kernel(own, right, partial, grad_sq):
    core = lax.axis_index("core")
    half = own.shape[1]
    groups = right.shape[0] // 2
    grad = own[...]
    grad_sq[...] = jnp.full(grad_sq.shape, jnp.sum(jnp.square(grad.astype(F32))), F32)
    upper = right[pl.ds(core * groups, groups)].reshape(half, 2 * half)
    partial[...] = dot(grad, upper, ((1,), (0,)))


def direction_kernel(other, partial, left, right, grad_sq_near, out):
    core = lax.axis_index("core")
    half = other.shape[1]
    groups = right.shape[0] // 2
    size = 2 * half
    grad = other[...]
    grad_sq = grad_sq_near[0:1, 0:1] + jnp.full((1, 1), jnp.sum(jnp.square(grad.astype(F32))), F32)
    left_mat = left[...].reshape(size, size)

    def columns(h):
        cols = pl.ds(pl.multiple_of(h * half, 128), half)
        lower = right[pl.ds((1 - core) * groups, groups), :, cols].reshape(half, half)
        shaped = partial[:, cols] + dot(grad, lower, ((1,), (0,)))
        return dot(left_mat, shaped.astype(BF16), ((1,), (0,)))

    dir_sq = jnp.sum(jnp.square(columns(1 - core)))
    near = columns(core)
    dir_sq = jnp.full((1, 1), dir_sq + jnp.sum(jnp.square(near)), F32)
    ratio = jnp.sqrt(grad_sq) / jnp.sqrt(dir_sq + NORM_EPS)
    out[...] = (-near * ratio).astype(BF16)


def terms_kernel(own, other, beside, across, mine, grad):
    core, x = lax.axis_index("core"), lax.axis_index("x")
    half = own.shape[1]
    rows = mine.shape[1]
    grad[:, pl.ds(pl.multiple_of(core * half, 128), half)] = own[...]
    grad[:, pl.ds(pl.multiple_of((1 - core) * half, 128), half)] = other[...]
    whole = grad[...]

    def of_chip(chip):
        at = pl.ds(pl.multiple_of(chip * 2 * rows, 128), 2 * rows)
        return dot(grad[at], whole, ((1,), (1,))), dot(grad[:, at], whole, ((0,), (0,)))

    for side, term in enumerate(of_chip(lax.rem(x + 1 + 2 * core, 4))):
        for parity in range(2):
            beside[parity, side] = term[parity * rows : (parity + 1) * rows].astype(BF16)
    for chip, out in ((lax.rem(x + 2, 4), across), (x, mine)):
        for side, term in enumerate(of_chip(chip)):
            out[side] = jnp.where(core == 0, term[:rows], term[rows:]).astype(BF16)


def stats_kernel(chip_of, mine, across, beside, passed, left, right, left_hbm, right_hbm, left_out, right_out, sems):
    core, x = lax.axis_index("core"), lax.axis_index("x")
    stores = []
    for j in range(left.shape[0]):
        full = chip_of[0, j] >= 0
        way = lax.rem(chip_of[0, j] + 4 - x, 4)

        def add(here, term):
            @pl.when(jnp.logical_and(full, here))
            def _():
                left_out[j] = STAT_DECAY * left[j] + (1.0 - STAT_DECAY) * term(0).astype(F32)
                right_out[j] = STAT_DECAY * right[j] + (1.0 - STAT_DECAY) * term(1).astype(F32)

        add(way == 0, lambda side: mine[side])
        add(way == 2, lambda side: across[side])
        add(way == 3 - 2 * core, lambda side: beside[core, side])
        add(way == 1 + 2 * core, lambda side: passed[side])

        @pl.when(jnp.logical_not(full))
        def _():
            left_out[j] = STAT_DECAY * left[j]
            right_out[j] = STAT_DECAY * right[j]

        for side, (result, target) in enumerate(((left_out, left_hbm), (right_out, right_hbm))):
            stores.append(pltpu.make_async_copy(result.at[j], target.at[j], sems.at[j, side]))
            stores[-1].start()
    for store in stores:
        store.wait()


def compact_kernel(owned, rows, out):
    def body(i, carry):
        block = rows[owned[0, i]]
        for x in range(out.shape[0]):
            out[x, i] = block
        return carry

    lax.fori_loop(0, out.shape[1], body, 0, unroll=8)


def order_kernel(source, rows, out):
    def body(b, carry):
        out[b] = rows[source[0, b]]
        return carry

    lax.fori_loop(0, out.shape[0], body, 0, unroll=8)


def place_half(half, rows, out_hbm, sem):
    width = rows.shape[2]
    store = pltpu.make_async_copy(rows, out_hbm.at[:, :, pl.ds(pl.multiple_of(half * width, 128), width)], sem)
    store.start()
    store.wait()


def place_near_kernel(rows, out_hbm, sem):
    place_half(lax.axis_index("core"), rows, out_hbm, sem)


def place_far_kernel(rows, begun, out_hbm, sem):
    del begun
    place_half(1 - lax.axis_index("core"), rows, out_hbm, sem)


def call(kernel, out_shape, in_specs, scratch=(), out_specs=None, cost=None, aliases=None):
    if out_specs is None:
        out_specs = [VMEM_SPEC] * len(out_shape) if isinstance(out_shape, list) else VMEM_SPEC
    if cost is not None:
        cost = pl.CostEstimate(flops=cost[0], bytes_accessed=cost[1], transcendentals=0)
    return pl.pallas_call(
        kernel,
        out_shape=out_shape,
        in_specs=in_specs,
        out_specs=out_specs,
        scratch_shapes=list(scratch),
        input_output_aliases=aliases or {},
        compiler_params=PARAMS,
        cost_estimate=cost,
    )


def exchange(value, axis):
    return lax.all_to_all(value, axis, 0, 0, tiled=True)


def in_hbm(value):
    return pltpu.with_memory_space_constraint(value, pltpu.HBM)


def turn(value, k):
    chips = lax.axis_size("x")
    return lax.ppermute(value, "x", [(i, (i + k) % chips) for i in range(chips)]) if k else value


def swap_cores(value):
    return lax.ppermute(value, "core", [(0, 1), (1, 0)])


def local(grads, block_slot, left_stat, right_stat, left_root, right_root):
    grads = grads[0]
    chips = lax.axis_size("x")
    x = lax.axis_index("x")
    core = lax.axis_index("core")
    owners = lax.axis_size("y") * lax.axis_size("z")
    me = lax.axis_index("y") * lax.axis_size("z") + lax.axis_index("z")
    capacity, stat_rows, _ = left_stat.shape
    blocks, shard_rows, width = grads.shape
    half = width // 2
    depth = blocks // chips

    piece = jax.ShapeDtypeStruct((2, stat_rows, width), BF16)
    groups = width // stat_rows
    half_rows = jax.ShapeDtypeStruct((blocks, shard_rows, half), BF16)
    grads = in_hbm(grads.reshape(-1, stat_rows, width))
    left_root, right_root = in_hbm(left_root), in_hbm(right_root)
    grad_groups = grads.shape[0]

    sent = call(
        send_kernel,
        jax.ShapeDtypeStruct((grad_groups + 4 * capacity, stat_rows, half), BF16),
        [HBM_SPEC] * 3,
        [pltpu.SemaphoreType.DMA((5,))],
    )(grads, left_root, right_root)
    sent, late_grads = lax.optimization_barrier((sent, grads))
    other = swap_cores(sent)
    kept, beside, mine, across, order, source, place, owned, slot_of, chip_of = call(
        keep_kernel,
        [jax.ShapeDtypeStruct((grad_groups, stat_rows, half), BF16)]
        + [piece] * 3
        + [jax.ShapeDtypeStruct((1, blocks), jnp.int32)] * 6,
        [HBM_SPEC] * 4,
        [
            pltpu.VMEM((1, blocks), jnp.int32),
            pltpu.SMEM((1, blocks), jnp.int32),
            pltpu.SemaphoreType.DMA((3,)),
            pltpu.SemaphoreType.DMA((3, 2)),
        ],
        cost=(0, 4_000_000),
    )(in_hbm(block_slot.reshape(1, blocks)), in_hbm(late_grads), left_root, right_root)

    parts = call(
        pair_sum_kernel,
        jax.ShapeDtypeStruct((chips, depth, shard_rows, half), BF16),
        [SMEM_SPEC, VMEM_SPEC, VMEM_SPEC],
    )(order, kept.reshape(-1, shard_rows, half), other.reshape(-1, shard_rows, half))
    both = jax.ShapeDtypeStruct((2, 2, stat_rows, width), BF16)
    parts, late_slot_of = lax.optimization_barrier((parts, slot_of))
    parts = exchange(parts, "x")
    beside = call(
        functools.partial(pair_roots_kernel, grad_groups, capacity),
        both,
        [SMEM_SPEC, VMEM_SPEC, VMEM_SPEC],
        cost=(0, 1000),
    )(late_slot_of, other, beside)
    ways = [(2 * i, 2 * ((i + 1) % chips)) for i in range(chips)]
    ways += [(2 * i + 1, 2 * ((i - 1) % chips) + 1) for i in range(chips)]
    beside = lax.ppermute(beside, ("x", "core"), ways)
    outgoing = call(
        chip_sum_kernel,
        jax.ShapeDtypeStruct((owners, shard_rows, half), BF16),
        [VMEM_SPEC, VMEM_SPEC],
        [
            pltpu.VMEM((depth + 1, shard_rows, half), BF16),
            pltpu.SMEM((1, blocks), jnp.int32),
            pltpu.SemaphoreType.DMA,
        ],
    )(place, parts)

    outgoing, late_other, beside, across = lax.optimization_barrier((outgoing, other, beside, across))
    own = exchange(outgoing, ("y", "z"))
    across = turn(across, 2)
    stacked = call(
        stack_kernel,
        jax.ShapeDtypeStruct((3, 2, stat_rows, width), BF16),
        [VMEM_SPEC, VMEM_SPEC],
        cost=(0, 1_000_000),
    )(beside, across)
    others = swap_cores(stacked)
    left, right = call(
        functools.partial(merge_roots_kernel, grad_groups, capacity),
        [jax.ShapeDtypeStruct((groups, stat_rows, width), BF16)] * 2,
        [SMEM_SPEC] + [VMEM_SPEC] * 5,
        cost=(0, 2_000_000),
    )(slot_of, late_other, mine, beside, across, others)

    own = own.reshape(width, half)
    far = swap_cores(own)
    partial, grad_sq = call(
        near_kernel,
        [jax.ShapeDtypeStruct((width, width), F32), jax.ShapeDtypeStruct((8, 128), F32)],
        [VMEM_SPEC, VMEM_SPEC],
        cost=(270_000_000, 4_000_000),
    )(own, right)
    update = call(
        direction_kernel,
        jax.ShapeDtypeStruct((width, half), BF16),
        [VMEM_SPEC] * 5,
    )(far, partial, left, right, grad_sq)

    update, own, far = lax.optimization_barrier((update, own, far))
    rows = exchange(update.reshape(owners, shard_rows, half), ("y", "z"))
    beside, across, mine = call(
        terms_kernel,
        [both, piece, piece],
        [VMEM_SPEC, VMEM_SPEC],
        [pltpu.VMEM((width, width), BF16)],
        cost=(800_000_000, 2_000_000),
    )(own, far)
    across = turn(across, 2)
    beside = lax.ppermute(beside, ("x", "core"), ways)
    packed = call(
        compact_kernel,
        jax.ShapeDtypeStruct((chips, depth, shard_rows, half), BF16),
        [SMEM_SPEC, VMEM_SPEC],
    )(owned, rows)
    passed = swap_cores(lax.dynamic_index_in_dim(beside, 1 - core, keepdims=False))
    packed, beside, across, passed = lax.optimization_barrier((packed, beside, across, passed))
    near = exchange(packed, "x").reshape(blocks, shard_rows, half)
    near, beside, across, passed = lax.optimization_barrier((near, beside, across, passed))
    stat = jax.ShapeDtypeStruct(left_stat.shape, F32)
    left_new, right_new = call(
        stats_kernel,
        [stat, stat],
        [SMEM_SPEC] + [VMEM_SPEC] * 6,
        [
            pltpu.VMEM(left_stat.shape, F32),
            pltpu.VMEM(right_stat.shape, F32),
            pltpu.SemaphoreType.DMA((capacity, 2)),
        ],
        [HBM_SPEC, HBM_SPEC],
        cost=(10_000_000, 5_000_000),
    )(chip_of, mine, across, beside, passed, left_stat, right_stat)
    near = call(order_kernel, half_rows, [SMEM_SPEC, VMEM_SPEC])(source, near)
    beyond = swap_cores(near)
    whole_rows = jax.ShapeDtypeStruct((blocks, shard_rows, width), BF16)
    begun = call(
        place_near_kernel,
        whole_rows,
        [VMEM_SPEC],
        [pltpu.SemaphoreType.DMA],
        HBM_SPEC,
        cost=(0, 4_000_000),
    )(near)
    result = call(
        place_far_kernel,
        whole_rows,
        [VMEM_SPEC, HBM_SPEC],
        [pltpu.SemaphoreType.DMA],
        HBM_SPEC,
        aliases={1: 0},
    )(beyond, begun)
    return (result, left_new, right_new)


def solution(mesh):
    fine = Mesh(mesh.devices.reshape(4, 2, 4, 16), ("x", "core", "y", "z"))
    replica, shard = ("x", "core"), ("y", "z")
    in_specs = (
        P(replica, None, shard, None),
        P(),
        P(shard, replica, None),
        P(shard, replica, None),
        P(shard, replica, None),
        P(shard, replica, None),
    )
    out_specs = (P(None, shard, None), P(shard, replica, None), P(shard, replica, None))
    return jax.shard_map(local, mesh=fine, in_specs=in_specs, out_specs=out_specs, check_vma=False)
```

```python
import functools

import jax
import jax.numpy as jnp
from jax import lax
from jax.experimental import pallas as pl
from jax.experimental.pallas import tpu as pltpu
from jax.sharding import Mesh, PartitionSpec as P

STAT_DECAY = 0.9
NORM_EPS = 1e-12
F32 = jnp.float32
BF16 = jnp.bfloat16
VMEM_SPEC = pl.BlockSpec(memory_space=pltpu.VMEM)
HBM_SPEC = pl.BlockSpec(memory_space=pltpu.HBM)
SMEM_SPEC = pl.BlockSpec(memory_space=pltpu.SMEM)
PARAMS = pltpu.CompilerParams(vmem_limit_bytes=32 * 1024 * 1024)


def dot(a, b, dims):
    return lax.dot_general(a, b, (dims, ((), ())), preferred_element_type=F32)


def fill_tables(slots, x, me, capacity, chips, order, source, place, owned, slot_of, chip_of, slot_done):
    blocks = slots.shape[1]
    square = (blocks, blocks)
    cap_bits, chip_bits = capacity.bit_length() - 1, chips.bit_length() - 1
    depth = blocks // chips
    lane = lax.broadcasted_iota(jnp.int32, square, 1)
    sublane = lax.broadcasted_iota(jnp.int32, square, 0)
    across = jnp.broadcast_to(slots[...], square)
    slot = across.T

    def total(mask, value):
        return jnp.sum(jnp.where(mask, value, 0), axis=0, keepdims=True)

    rank_row = total(slot < across, 1)
    rank = jnp.broadcast_to(rank_row, square).T
    chip = rank & (chips - 1)
    spot = rank >> chip_bits
    owner = slot >> cap_bits
    slot_of[...] = total((owner == me) & (chip == lane), slot & (capacity - 1))
    slot_done()
    order[...] = total(rank == lane, sublane)
    source[...] = (rank_row & (chips - 1)) * depth + (rank_row >> chip_bits)
    place[...] = total((chip == x) & (owner == lane), spot - depth) + depth
    owned[...] = total((chip == x) & (spot == lane), owner)
    chip_of[...] = total(slot == me * capacity + lane, chip + 1) - 1


def send_kernel(grads, left_root, right_root, sent, sems):
    width = sent.shape[2]
    groups = grads.shape[0]
    capacity = left_root.shape[0]
    far = pl.ds(pl.multiple_of((1 - lax.axis_index("core")) * width, 128), width)
    loads = [pltpu.make_async_copy(grads.at[:, :, far], sent.at[pl.ds(0, groups)], sems.at[0])]
    for i in range(4):
        root = (left_root, right_root)[i // 2].at[:, :, pl.ds(i % 2 * width, width)]
        loads.append(pltpu.make_async_copy(root, sent.at[pl.ds(groups + i * capacity, capacity)], sems.at[i + 1]))
    for load in loads:
        load.start()
    for load in loads:
        load.wait()


def keep_kernel(slots_hbm, grads, left_root, right_root, kept, beside, mine, across, *refs):
    tables, (slots, rows, sems, root_sems, table_sems) = refs[:6], refs[6:]
    core, x = lax.axis_index("core"), lax.axis_index("x")
    me = lax.axis_index("y") * lax.axis_size("z") + lax.axis_index("z")
    width = kept.shape[2]
    near = pl.ds(pl.multiple_of(core * width, 128), width)
    slots_load = pltpu.make_async_copy(slots_hbm, slots, sems.at[0])
    load = pltpu.make_async_copy(grads.at[:, :, near], kept, sems.at[1])
    to_scalars = [pltpu.make_async_copy(rows.at[i], table, table_sems.at[i]) for i, table in enumerate(tables)]
    slots_load.start()
    load.start()
    slots_load.wait()
    fill_tables(slots, x, me, left_root.shape[0], 4, *(rows.at[i] for i in range(6)), to_scalars[4].start)
    to_scalars[4].wait()
    loads = [load]
    for i, (chip, out) in enumerate(((x + 1 + 2 * core, beside), (x, mine), (x + 2, across))):
        slot = tables[4][0, lax.rem(chip, 4)]
        for side, root in enumerate((left_root, right_root)):
            loads.append(pltpu.make_async_copy(root.at[slot], out.at[side], root_sems.at[i, side]))
            loads[-1].start()
    for i in (0, 1, 2, 3, 5):
        to_scalars[i].start()
        loads.append(to_scalars[i])
    for load in loads:
        load.wait()


def from_other(groups, capacity, other, slot, side, out):
    width = other.shape[2]
    for h in range(2):
        out[:, h * width : (h + 1) * width] = other[groups + (2 * side + h) * capacity + slot]


def pair_roots_kernel(groups, capacity, slot_of, other, beside, out):
    core, x = lax.axis_index("core"), lax.axis_index("x")
    slot = slot_of[0, lax.rem(x + 1 + 2 * core, 4)]
    out[core] = beside[...]
    for side in range(2):
        from_other(groups, capacity, other, slot, side, out.at[1 - core, side])


def stack_kernel(beside, across, out):
    out[0:2] = beside[...]
    out[2] = across[...]


def merge_roots_kernel(groups, capacity, slot_of, other, mine, beside, across, others, left, right):
    core, x = lax.axis_index("core"), lax.axis_index("x")
    near, far, opposite = lax.rem(x + 3 - 2 * core, 4), lax.rem(x + 1 + 2 * core, 4), lax.rem(x + 2, 4)
    for side, out in enumerate((left, right)):
        out[2 * x + core] = mine[side]
        from_other(groups, capacity, other, slot_of[0, x], side, out.at[2 * x + 1 - core])
        for parity in range(2):
            out[2 * near + parity] = beside[parity, side]
            out[2 * far + parity] = others[parity, side]
        out[2 * opposite + core] = across[side]
        out[2 * opposite + 1 - core] = others[2, side]


def pair_sum_kernel(order, own, other, out):
    chips, depth = out.shape[:2]

    def body(i, carry):
        for x in range(chips):
            block = order[0, i * chips + x]
            out[x, i] = own[block] + other[block]
        return carry

    lax.fori_loop(0, depth, body, 0, unroll=8)


def store_in_steps(source, target, sems, dim, fill):
    steps = sems.shape[0]
    count = source.shape[dim] // steps
    stores = []
    for i in range(steps):
        fill(i * count, count)
        part = (slice(None),) * dim + (pl.ds(i * count, count),)
        stores.append(pltpu.make_async_copy(source.at[part], target.at[part], sems.at[i]))
        stores[-1].start()
    for store in stores:
        store.wait()


def chip_sum_kernel(place, parts, out, total):
    depth = parts.shape[1]
    acc = parts[0].astype(F32)
    for x in range(1, parts.shape[0]):
        acc = acc + parts[x].astype(F32)
    total[0:depth] = acc.astype(BF16)
    total[depth] = jnp.zeros(total.shape[1:], BF16)

    def body(o, carry):
        out[o] = total[place[0, o]]
        return carry

    lax.fori_loop(0, out.shape[0], body, 0, unroll=8)


def near_kernel(own, right, partial, grad_sq):
    core = lax.axis_index("core")
    half = own.shape[1]
    groups = right.shape[0] // 2
    grad = own[...]
    grad_sq[...] = jnp.full(grad_sq.shape, jnp.sum(jnp.square(grad.astype(F32))), F32)
    upper = right[pl.ds(core * groups, groups)].reshape(half, 2 * half)
    partial[...] = dot(grad, upper, ((1,), (0,)))


def direction_kernel(other, partial, left, right, grad_sq_near, out):
    core = lax.axis_index("core")
    half = other.shape[1]
    groups = right.shape[0] // 2
    size = 2 * half
    grad = other[...]
    grad_sq = grad_sq_near[0:1, 0:1] + jnp.full((1, 1), jnp.sum(jnp.square(grad.astype(F32))), F32)
    left_mat = left[...].reshape(size, size)

    def columns(h):
        cols = pl.ds(pl.multiple_of(h * half, 128), half)
        lower = right[pl.ds((1 - core) * groups, groups), :, cols].reshape(half, half)
        shaped = partial[:, cols] + dot(grad, lower, ((1,), (0,)))
        return dot(left_mat, shaped.astype(BF16), ((1,), (0,)))

    dir_sq = jnp.sum(jnp.square(columns(1 - core)))
    near = columns(core)
    dir_sq = jnp.full((1, 1), dir_sq + jnp.sum(jnp.square(near)), F32)
    ratio = jnp.sqrt(grad_sq) / jnp.sqrt(dir_sq + NORM_EPS)
    out[...] = (-near * ratio).astype(BF16)


def terms_kernel(own, other, beside, across, mine, grad):
    core, x = lax.axis_index("core"), lax.axis_index("x")
    half = own.shape[1]
    rows = mine.shape[1]
    grad[:, pl.ds(pl.multiple_of(core * half, 128), half)] = own[...]
    grad[:, pl.ds(pl.multiple_of((1 - core) * half, 128), half)] = other[...]
    whole = grad[...]

    def of_chip(chip):
        at = pl.ds(pl.multiple_of(chip * 2 * rows, 128), 2 * rows)
        return dot(grad[at], whole, ((1,), (1,))), dot(grad[:, at], whole, ((0,), (0,)))

    for side, term in enumerate(of_chip(lax.rem(x + 1 + 2 * core, 4))):
        for parity in range(2):
            beside[parity, side] = term[parity * rows : (parity + 1) * rows].astype(BF16)
    for chip, out in ((lax.rem(x + 2, 4), across), (x, mine)):
        for side, term in enumerate(of_chip(chip)):
            out[side] = jnp.where(core == 0, term[:rows], term[rows:]).astype(BF16)


def finish_kernel(
    chip_of, near, mine, across, beside, passed, left, right, out_hbm, left_hbm, right_hbm, left_out, right_out, near_sem, sems
):
    core, x = lax.axis_index("core"), lax.axis_index("x")
    stores = [place_half(core, near, out_hbm, near_sem)]
    stores[0].start()
    for j in range(left.shape[0]):
        full = chip_of[0, j] >= 0
        way = lax.rem(chip_of[0, j] + 4 - x, 4)

        def add(here, term):
            @pl.when(jnp.logical_and(full, here))
            def _():
                left_out[j] = STAT_DECAY * left[j] + (1.0 - STAT_DECAY) * term(0).astype(F32)
                right_out[j] = STAT_DECAY * right[j] + (1.0 - STAT_DECAY) * term(1).astype(F32)

        add(way == 0, lambda side: mine[side])
        add(way == 2, lambda side: across[side])
        add(way == 3 - 2 * core, lambda side: beside[core, side])
        add(way == 1 + 2 * core, lambda side: passed[side])

        @pl.when(jnp.logical_not(full))
        def _():
            left_out[j] = STAT_DECAY * left[j]
            right_out[j] = STAT_DECAY * right[j]

        for side, (result, target) in enumerate(((left_out, left_hbm), (right_out, right_hbm))):
            stores.append(pltpu.make_async_copy(result.at[j], target.at[j], sems.at[j, side]))
            stores[-1].start()
    for store in stores:
        store.wait()


def compact_kernel(owned, rows, out):
    def body(i, carry):
        block = rows[owned[0, i]]
        for x in range(out.shape[0]):
            out[x, i] = block
        return carry

    lax.fori_loop(0, out.shape[1], body, 0, unroll=8)


def order_kernel(source, rows, out):
    def body(b, carry):
        out[b] = rows[source[0, b]]
        return carry

    lax.fori_loop(0, out.shape[0], body, 0, unroll=8)


def place_half(half, rows, out_hbm, sem):
    width = rows.shape[2]
    return pltpu.make_async_copy(rows, out_hbm.at[:, :, pl.ds(pl.multiple_of(half * width, 128), width)], sem)


def place_far_kernel(rows, begun, out_hbm, sem):
    del begun
    store = place_half(1 - lax.axis_index("core"), rows, out_hbm, sem)
    store.start()
    store.wait()


def call(kernel, out_shape, in_specs, scratch=(), out_specs=None, cost=None, aliases=None):
    if out_specs is None:
        out_specs = [VMEM_SPEC] * len(out_shape) if isinstance(out_shape, list) else VMEM_SPEC
    if cost is not None:
        cost = pl.CostEstimate(flops=cost[0], bytes_accessed=cost[1], transcendentals=0)
    return pl.pallas_call(
        kernel,
        out_shape=out_shape,
        in_specs=in_specs,
        out_specs=out_specs,
        scratch_shapes=list(scratch),
        input_output_aliases=aliases or {},
        compiler_params=PARAMS,
        cost_estimate=cost,
    )


def exchange(value, axis):
    return lax.all_to_all(value, axis, 0, 0, tiled=True)


def in_hbm(value):
    return pltpu.with_memory_space_constraint(value, pltpu.HBM)


def turn(value, k):
    chips = lax.axis_size("x")
    return lax.ppermute(value, "x", [(i, (i + k) % chips) for i in range(chips)]) if k else value


def swap_cores(value):
    return lax.ppermute(value, "core", [(0, 1), (1, 0)])


def local(grads, block_slot, left_stat, right_stat, left_root, right_root):
    grads = grads[0]
    chips = lax.axis_size("x")
    x = lax.axis_index("x")
    core = lax.axis_index("core")
    owners = lax.axis_size("y") * lax.axis_size("z")
    me = lax.axis_index("y") * lax.axis_size("z") + lax.axis_index("z")
    capacity, stat_rows, _ = left_stat.shape
    blocks, shard_rows, width = grads.shape
    half = width // 2
    depth = blocks // chips

    piece = jax.ShapeDtypeStruct((2, stat_rows, width), BF16)
    groups = width // stat_rows
    half_rows = jax.ShapeDtypeStruct((blocks, shard_rows, half), BF16)
    grads = in_hbm(grads.reshape(-1, stat_rows, width))
    left_root, right_root = in_hbm(left_root), in_hbm(right_root)
    grad_groups = grads.shape[0]

    sent = call(
        send_kernel,
        jax.ShapeDtypeStruct((grad_groups + 4 * capacity, stat_rows, half), BF16),
        [HBM_SPEC] * 3,
        [pltpu.SemaphoreType.DMA((5,))],
    )(grads, left_root, right_root)
    sent, late_grads = lax.optimization_barrier((sent, grads))
    other = swap_cores(sent)
    kept, beside, mine, across, order, source, place, owned, slot_of, chip_of = call(
        keep_kernel,
        [jax.ShapeDtypeStruct((grad_groups, stat_rows, half), BF16)]
        + [piece] * 3
        + [pltpu.SMEM((1, blocks), jnp.int32)] * 6,
        [HBM_SPEC] * 4,
        [
            pltpu.VMEM((1, blocks), jnp.int32),
            pltpu.VMEM((6, 1, blocks), jnp.int32),
            pltpu.SemaphoreType.DMA((2,)),
            pltpu.SemaphoreType.DMA((3, 2)),
            pltpu.SemaphoreType.DMA((6,)),
        ],
        [VMEM_SPEC] * 4 + [SMEM_SPEC] * 6,
        cost=(0, 4_000_000),
    )(in_hbm(block_slot.reshape(1, blocks)), in_hbm(late_grads), left_root, right_root)

    parts = call(
        pair_sum_kernel,
        jax.ShapeDtypeStruct((chips, depth, shard_rows, half), BF16),
        [SMEM_SPEC, VMEM_SPEC, VMEM_SPEC],
    )(order, kept.reshape(-1, shard_rows, half), other.reshape(-1, shard_rows, half))
    both = jax.ShapeDtypeStruct((2, 2, stat_rows, width), BF16)
    parts, late_slot_of = lax.optimization_barrier((parts, slot_of))
    parts = exchange(parts, "x")
    beside = call(
        functools.partial(pair_roots_kernel, grad_groups, capacity),
        both,
        [SMEM_SPEC, VMEM_SPEC, VMEM_SPEC],
        cost=(0, 1000),
    )(late_slot_of, other, beside)
    ways = [(2 * i, 2 * ((i + 1) % chips)) for i in range(chips)]
    ways += [(2 * i + 1, 2 * ((i - 1) % chips) + 1) for i in range(chips)]
    beside = lax.ppermute(beside, ("x", "core"), ways)
    outgoing = call(
        chip_sum_kernel,
        jax.ShapeDtypeStruct((owners, shard_rows, half), BF16),
        [SMEM_SPEC, VMEM_SPEC],
        [pltpu.VMEM((depth + 1, shard_rows, half), BF16)],
    )(place, parts)

    outgoing, late_other, beside, across = lax.optimization_barrier((outgoing, other, beside, across))
    own = exchange(outgoing, ("y", "z"))
    across = turn(across, 2)
    stacked = call(
        stack_kernel,
        jax.ShapeDtypeStruct((3, 2, stat_rows, width), BF16),
        [VMEM_SPEC, VMEM_SPEC],
        cost=(0, 1_000_000),
    )(beside, across)
    others = swap_cores(stacked)
    left, right = call(
        functools.partial(merge_roots_kernel, grad_groups, capacity),
        [jax.ShapeDtypeStruct((groups, stat_rows, width), BF16)] * 2,
        [SMEM_SPEC] + [VMEM_SPEC] * 5,
        cost=(0, 2_000_000),
    )(slot_of, late_other, mine, beside, across, others)

    own = own.reshape(width, half)
    far = swap_cores(own)
    partial, grad_sq = call(
        near_kernel,
        [jax.ShapeDtypeStruct((width, width), F32), jax.ShapeDtypeStruct((8, 128), F32)],
        [VMEM_SPEC, VMEM_SPEC],
        cost=(270_000_000, 4_000_000),
    )(own, right)
    update = call(
        direction_kernel,
        jax.ShapeDtypeStruct((width, half), BF16),
        [VMEM_SPEC] * 5,
    )(far, partial, left, right, grad_sq)

    update, own, far = lax.optimization_barrier((update, own, far))
    rows = exchange(update.reshape(owners, shard_rows, half), ("y", "z"))
    beside, across, mine = call(
        terms_kernel,
        [both, piece, piece],
        [VMEM_SPEC, VMEM_SPEC],
        [pltpu.VMEM((width, width), BF16)],
        cost=(800_000_000, 2_000_000),
    )(own, far)
    across = turn(across, 2)
    beside = lax.ppermute(beside, ("x", "core"), ways)
    packed = call(
        compact_kernel,
        jax.ShapeDtypeStruct((chips, depth, shard_rows, half), BF16),
        [SMEM_SPEC, VMEM_SPEC],
    )(owned, rows)
    passed = swap_cores(lax.dynamic_index_in_dim(beside, 1 - core, keepdims=False))
    packed, beside, across, passed = lax.optimization_barrier((packed, beside, across, passed))
    near = exchange(packed, "x").reshape(blocks, shard_rows, half)
    near, beside, across, passed = lax.optimization_barrier((near, beside, across, passed))
    near = call(order_kernel, half_rows, [SMEM_SPEC, VMEM_SPEC])(source, near)
    beyond = swap_cores(near)
    stat = jax.ShapeDtypeStruct(left_stat.shape, F32)
    whole_rows = jax.ShapeDtypeStruct((blocks, shard_rows, width), BF16)
    begun, left_new, right_new = call(
        finish_kernel,
        [whole_rows, stat, stat],
        [SMEM_SPEC] + [VMEM_SPEC] * 7,
        [
            pltpu.VMEM(left_stat.shape, F32),
            pltpu.VMEM(right_stat.shape, F32),
            pltpu.SemaphoreType.DMA,
            pltpu.SemaphoreType.DMA((capacity, 2)),
        ],
        [HBM_SPEC] * 3,
        cost=(10_000_000, 5_000_000),
    )(chip_of, near, mine, across, beside, passed, left_stat, right_stat)
    result = call(
        place_far_kernel,
        whole_rows,
        [VMEM_SPEC, HBM_SPEC],
        [pltpu.SemaphoreType.DMA],
        HBM_SPEC,
        aliases={1: 0},
    )(beyond, begun)
    return (result, left_new, right_new)


def solution(mesh):
    fine = Mesh(mesh.devices.reshape(4, 2, 4, 16), ("x", "core", "y", "z"))
    replica, shard = ("x", "core"), ("y", "z")
    in_specs = (
        P(replica, None, shard, None),
        P(),
        P(shard, replica, None),
        P(shard, replica, None),
        P(shard, replica, None),
        P(shard, replica, None),
    )
    out_specs = (P(None, shard, None), P(shard, replica, None), P(shard, replica, None))
    return jax.shard_map(local, mesh=fine, in_specs=in_specs, out_specs=out_specs, check_vma=False)
```

```python
import functools

import jax
import jax.numpy as jnp
from jax import lax
from jax.experimental import pallas as pl
from jax.experimental.pallas import tpu as pltpu
from jax.sharding import Mesh, PartitionSpec as P

STAT_DECAY = 0.9
NORM_EPS = 1e-12
F32 = jnp.float32
BF16 = jnp.bfloat16
VMEM_SPEC = pl.BlockSpec(memory_space=pltpu.VMEM)
HBM_SPEC = pl.BlockSpec(memory_space=pltpu.HBM)
SMEM_SPEC = pl.BlockSpec(memory_space=pltpu.SMEM)
PARAMS = pltpu.CompilerParams(vmem_limit_bytes=32 * 1024 * 1024)


def dot(a, b, dims):
    return lax.dot_general(a, b, (dims, ((), ())), preferred_element_type=F32)


def fill_tables(slots, x, me, capacity, chips, order, source, place, owned, slot_of, chip_of, slot_done):
    blocks = slots.shape[1]
    square = (blocks, blocks)
    cap_bits, chip_bits = capacity.bit_length() - 1, chips.bit_length() - 1
    depth = blocks // chips
    lane = lax.broadcasted_iota(jnp.int32, square, 1)
    sublane = lax.broadcasted_iota(jnp.int32, square, 0)
    across = jnp.broadcast_to(slots[...], square)
    slot = across.T

    def total(mask, value):
        return jnp.sum(jnp.where(mask, value, 0), axis=0, keepdims=True)

    rank_row = total(slot < across, 1)
    rank = jnp.broadcast_to(rank_row, square).T
    chip = rank & (chips - 1)
    spot = rank >> chip_bits
    owner = slot >> cap_bits
    slot_of[...] = total((owner == me) & (chip == lane), slot & (capacity - 1))
    slot_done()
    order[...] = total(rank == lane, sublane)
    source[...] = (rank_row & (chips - 1)) * depth + (rank_row >> chip_bits)
    place[...] = total((chip == x) & (owner == lane), spot - depth) + depth
    owned[...] = total((chip == x) & (spot == lane), owner)
    chip_of[...] = total(slot == me * capacity + lane, chip + 1) - 1


def send_kernel(grads, left_root, right_root, sent, sems):
    width = sent.shape[2]
    groups = grads.shape[0]
    capacity = left_root.shape[0]
    far = pl.ds(pl.multiple_of((1 - lax.axis_index("core")) * width, 128), width)
    loads = [pltpu.make_async_copy(grads.at[:, :, far], sent.at[pl.ds(0, groups)], sems.at[0])]
    for i in range(4):
        root = (left_root, right_root)[i // 2].at[:, :, pl.ds(i % 2 * width, width)]
        loads.append(pltpu.make_async_copy(root, sent.at[pl.ds(groups + i * capacity, capacity)], sems.at[i + 1]))
    for load in loads:
        load.start()
    for load in loads:
        load.wait()


def keep_kernel(slots_hbm, grads, left_root, right_root, kept, beside, mine, across, *refs):
    tables, (slots, rows, sems, root_sems, table_sems) = refs[:6], refs[6:]
    core, x = lax.axis_index("core"), lax.axis_index("x")
    me = lax.axis_index("y") * lax.axis_size("z") + lax.axis_index("z")
    width = kept.shape[2]
    near = pl.ds(pl.multiple_of(core * width, 128), width)
    slots_load = pltpu.make_async_copy(slots_hbm, slots, sems.at[0])
    load = pltpu.make_async_copy(grads.at[:, :, near], kept, sems.at[1])
    to_scalars = [pltpu.make_async_copy(rows.at[i], table, table_sems.at[i]) for i, table in enumerate(tables)]
    slots_load.start()
    load.start()
    slots_load.wait()
    fill_tables(slots, x, me, left_root.shape[0], 4, *(rows.at[i] for i in range(6)), to_scalars[4].start)
    to_scalars[4].wait()
    loads = [load]
    for i, (chip, out) in enumerate(((x + 1 + 2 * core, beside), (x, mine), (x + 2, across))):
        slot = tables[4][0, lax.rem(chip, 4)]
        for side, root in enumerate((left_root, right_root)):
            loads.append(pltpu.make_async_copy(root.at[slot], out.at[side], root_sems.at[i, side]))
            loads[-1].start()
    for i in (0, 1, 2, 3, 5):
        to_scalars[i].start()
        loads.append(to_scalars[i])
    for load in loads:
        load.wait()


def from_other(groups, capacity, other, slot, side, out):
    width = other.shape[2]
    for h in range(2):
        out[:, h * width : (h + 1) * width] = other[groups + (2 * side + h) * capacity + slot]


def pair_roots_kernel(groups, capacity, slot_of, other, beside, out):
    core, x = lax.axis_index("core"), lax.axis_index("x")
    slot = slot_of[0, lax.rem(x + 1 + 2 * core, 4)]
    out[core] = beside[...]
    for side in range(2):
        from_other(groups, capacity, other, slot, side, out.at[1 - core, side])


def stack_kernel(beside, across, out):
    out[0:2] = beside[...]
    out[2] = across[...]


def merge_roots_kernel(groups, capacity, slot_of, other, mine, beside, across, others, left, right):
    core, x = lax.axis_index("core"), lax.axis_index("x")
    near, far, opposite = lax.rem(x + 3 - 2 * core, 4), lax.rem(x + 1 + 2 * core, 4), lax.rem(x + 2, 4)
    for side, out in enumerate((left, right)):
        out[2 * x + core] = mine[side]
        from_other(groups, capacity, other, slot_of[0, x], side, out.at[2 * x + 1 - core])
        for parity in range(2):
            out[2 * near + parity] = beside[parity, side]
            out[2 * far + parity] = others[parity, side]
        out[2 * opposite + core] = across[side]
        out[2 * opposite + 1 - core] = others[2, side]


def pair_sum_kernel(order, own, other, out):
    chips, depth = out.shape[:2]

    def body(i, carry):
        for x in range(chips):
            block = order[0, i * chips + x]
            out[x, i] = own[block] + other[block]
        return carry

    lax.fori_loop(0, depth, body, 0, unroll=8)


def store_in_steps(source, target, sems, dim, fill):
    steps = sems.shape[0]
    count = source.shape[dim] // steps
    stores = []
    for i in range(steps):
        fill(i * count, count)
        part = (slice(None),) * dim + (pl.ds(i * count, count),)
        stores.append(pltpu.make_async_copy(source.at[part], target.at[part], sems.at[i]))
        stores[-1].start()
    for store in stores:
        store.wait()


def chip_sum_kernel(place, parts, out, total):
    depth = parts.shape[1]
    acc = parts[0].astype(F32)
    for x in range(1, parts.shape[0]):
        acc = acc + parts[x].astype(F32)
    total[0:depth] = acc.astype(BF16)
    total[depth] = jnp.zeros(total.shape[1:], BF16)

    def body(o, carry):
        out[o] = total[place[0, o]]
        return carry

    lax.fori_loop(0, out.shape[0], body, 0, unroll=8)


def near_kernel(own, right, partial, grad_sq):
    core = lax.axis_index("core")
    half = own.shape[1]
    groups = right.shape[0] // 2
    grad = own[...]
    grad_sq[...] = jnp.full(grad_sq.shape, jnp.sum(jnp.square(grad.astype(F32))), F32)
    upper = right[pl.ds(core * groups, groups)].reshape(half, 2 * half)
    partial[...] = dot(grad, upper, ((1,), (0,)))


def direction_kernel(other, partial, left, right, grad_sq_near, out):
    core = lax.axis_index("core")
    half = other.shape[1]
    groups = right.shape[0] // 2
    size = 2 * half
    grad = other[...]
    grad_sq = grad_sq_near[0:1, 0:1] + jnp.full((1, 1), jnp.sum(jnp.square(grad.astype(F32))), F32)
    left_mat = left[...].reshape(size, size)

    def columns(h):
        cols = pl.ds(pl.multiple_of(h * half, 128), half)
        lower = right[pl.ds((1 - core) * groups, groups), :, cols].reshape(half, half)
        shaped = partial[:, cols] + dot(grad, lower, ((1,), (0,)))
        return dot(left_mat, shaped.astype(BF16), ((1,), (0,)))

    dir_sq = jnp.sum(jnp.square(columns(1 - core)))
    near = columns(core)
    dir_sq = jnp.full((1, 1), dir_sq + jnp.sum(jnp.square(near)), F32)
    ratio = jnp.sqrt(grad_sq) / jnp.sqrt(dir_sq + NORM_EPS)
    out[...] = (-near * ratio).astype(BF16)


def terms_kernel(own, other, beside, across, mine, grad):
    core, x = lax.axis_index("core"), lax.axis_index("x")
    half = own.shape[1]
    rows = mine.shape[1]
    grad[:, pl.ds(pl.multiple_of(core * half, 128), half)] = own[...]
    grad[:, pl.ds(pl.multiple_of((1 - core) * half, 128), half)] = other[...]
    whole = grad[...]

    def of_chip(chip):
        at = pl.ds(pl.multiple_of(chip * 2 * rows, 128), 2 * rows)
        return dot(grad[at], whole, ((1,), (1,))), dot(grad[:, at], whole, ((0,), (0,)))

    for side, term in enumerate(of_chip(lax.rem(x + 1 + 2 * core, 4))):
        for parity in range(2):
            beside[parity, side] = term[parity * rows : (parity + 1) * rows].astype(BF16)
    for chip, out in ((lax.rem(x + 2, 4), across), (x, mine)):
        for side, term in enumerate(of_chip(chip)):
            out[side] = jnp.where(core == 0, term[:rows], term[rows:]).astype(BF16)


def finish_kernel(
    chip_of, near, mine, across, beside, passed, left, right, out_hbm, left_hbm, right_hbm, left_out, right_out, near_sem, sems
):
    core, x = lax.axis_index("core"), lax.axis_index("x")
    stores = [place_half(core, near, out_hbm, near_sem)]
    stores[0].start()
    for j in range(left.shape[0]):
        full = chip_of[0, j] >= 0
        way = lax.rem(chip_of[0, j] + 4 - x, 4)

        def add(here, term):
            @pl.when(jnp.logical_and(full, here))
            def _():
                left_out[j] = STAT_DECAY * left[j] + (1.0 - STAT_DECAY) * term(0).astype(F32)
                right_out[j] = STAT_DECAY * right[j] + (1.0 - STAT_DECAY) * term(1).astype(F32)

        add(way == 0, lambda side: mine[side])
        add(way == 2, lambda side: across[side])
        add(way == 3 - 2 * core, lambda side: beside[core, side])
        add(way == 1 + 2 * core, lambda side: passed[side])

        @pl.when(jnp.logical_not(full))
        def _():
            left_out[j] = STAT_DECAY * left[j]
            right_out[j] = STAT_DECAY * right[j]

        for side, (result, target) in enumerate(((left_out, left_hbm), (right_out, right_hbm))):
            stores.append(pltpu.make_async_copy(result.at[j], target.at[j], sems.at[j, side]))
            stores[-1].start()
    for store in stores:
        store.wait()


def compact_kernel(owned, rows, out):
    def body(i, carry):
        block = rows[owned[0, i]]
        for x in range(out.shape[0]):
            out[x, i] = block
        return carry

    lax.fori_loop(0, out.shape[1], body, 0, unroll=8)


def order_kernel(source, rows, out):
    def body(b, carry):
        out[b] = rows[source[0, b]]
        return carry

    lax.fori_loop(0, out.shape[0], body, 0, unroll=8)


def place_half(half, rows, out_hbm, sem):
    width = rows.shape[2]
    return pltpu.make_async_copy(rows, out_hbm.at[:, :, pl.ds(pl.multiple_of(half * width, 128), width)], sem)


def place_far_kernel(rows, begun, out_hbm, sem):
    del begun
    store = place_half(1 - lax.axis_index("core"), rows, out_hbm, sem)
    store.start()
    store.wait()


def call(kernel, out_shape, in_specs, scratch=(), out_specs=None, cost=None, aliases=None):
    if out_specs is None:
        out_specs = [VMEM_SPEC] * len(out_shape) if isinstance(out_shape, list) else VMEM_SPEC
    if cost is not None:
        cost = pl.CostEstimate(flops=cost[0], bytes_accessed=cost[1], transcendentals=0)
    return pl.pallas_call(
        kernel,
        out_shape=out_shape,
        in_specs=in_specs,
        out_specs=out_specs,
        scratch_shapes=list(scratch),
        input_output_aliases=aliases or {},
        compiler_params=PARAMS,
        cost_estimate=cost,
    )


def exchange(value, axis):
    return lax.all_to_all(value, axis, 0, 0, tiled=True)


def in_hbm(value):
    return pltpu.with_memory_space_constraint(value, pltpu.HBM)


def turn(value, k):
    chips = lax.axis_size("x")
    return lax.ppermute(value, "x", [(i, (i + k) % chips) for i in range(chips)]) if k else value


def swap_cores(value):
    return lax.ppermute(value, "core", [(0, 1), (1, 0)])


def local(grads, block_slot, left_stat, right_stat, left_root, right_root):
    grads = grads[0]
    chips = lax.axis_size("x")
    x = lax.axis_index("x")
    core = lax.axis_index("core")
    owners = lax.axis_size("y") * lax.axis_size("z")
    me = lax.axis_index("y") * lax.axis_size("z") + lax.axis_index("z")
    capacity, stat_rows, _ = left_stat.shape
    blocks, shard_rows, width = grads.shape
    half = width // 2
    depth = blocks // chips

    piece = jax.ShapeDtypeStruct((2, stat_rows, width), BF16)
    groups = width // stat_rows
    half_rows = jax.ShapeDtypeStruct((blocks, shard_rows, half), BF16)
    grads = in_hbm(grads.reshape(-1, stat_rows, width))
    left_root, right_root = in_hbm(left_root), in_hbm(right_root)
    grad_groups = grads.shape[0]

    sent = call(
        send_kernel,
        jax.ShapeDtypeStruct((grad_groups + 4 * capacity, stat_rows, half), BF16),
        [HBM_SPEC] * 3,
        [pltpu.SemaphoreType.DMA((5,))],
    )(grads, left_root, right_root)
    sent, late_grads = lax.optimization_barrier((sent, grads))
    other = swap_cores(sent)
    kept, beside, mine, across, order, source, place, owned, slot_of, chip_of = call(
        keep_kernel,
        [jax.ShapeDtypeStruct((grad_groups, stat_rows, half), BF16)]
        + [piece] * 3
        + [pltpu.SMEM((1, blocks), jnp.int32)] * 6,
        [HBM_SPEC] * 4,
        [
            pltpu.VMEM((1, blocks), jnp.int32),
            pltpu.VMEM((6, 1, blocks), jnp.int32),
            pltpu.SemaphoreType.DMA((2,)),
            pltpu.SemaphoreType.DMA((3, 2)),
            pltpu.SemaphoreType.DMA((6,)),
        ],
        [VMEM_SPEC] * 4 + [SMEM_SPEC] * 6,
        cost=(0, 4_000_000),
    )(in_hbm(block_slot.reshape(1, blocks)), in_hbm(late_grads), left_root, right_root)

    parts = call(
        pair_sum_kernel,
        jax.ShapeDtypeStruct((chips, depth, shard_rows, half), BF16),
        [SMEM_SPEC, VMEM_SPEC, VMEM_SPEC],
    )(order, kept.reshape(-1, shard_rows, half), other.reshape(-1, shard_rows, half))
    both = jax.ShapeDtypeStruct((2, 2, stat_rows, width), BF16)
    parts, late_slot_of = lax.optimization_barrier((parts, slot_of))
    parts = exchange(parts, "x")
    beside = call(
        functools.partial(pair_roots_kernel, grad_groups, capacity),
        both,
        [SMEM_SPEC, VMEM_SPEC, VMEM_SPEC],
        cost=(0, 1000),
    )(late_slot_of, other, beside)
    ways = [(2 * i, 2 * ((i + 1) % chips)) for i in range(chips)]
    ways += [(2 * i + 1, 2 * ((i - 1) % chips) + 1) for i in range(chips)]
    beside = lax.ppermute(beside, ("x", "core"), ways)
    outgoing = call(
        chip_sum_kernel,
        jax.ShapeDtypeStruct((owners, shard_rows, half), BF16),
        [SMEM_SPEC, VMEM_SPEC],
        [pltpu.VMEM((depth + 1, shard_rows, half), BF16)],
    )(place, parts)

    outgoing, late_other, across = lax.optimization_barrier((outgoing, other, across))
    own = exchange(outgoing, ("y", "z"))
    across = turn(across, 2)
    stacked = call(
        stack_kernel,
        jax.ShapeDtypeStruct((3, 2, stat_rows, width), BF16),
        [VMEM_SPEC, VMEM_SPEC],
        cost=(0, 1_000_000),
    )(beside, across)
    others = swap_cores(stacked)
    left, right = call(
        functools.partial(merge_roots_kernel, grad_groups, capacity),
        [jax.ShapeDtypeStruct((groups, stat_rows, width), BF16)] * 2,
        [SMEM_SPEC] + [VMEM_SPEC] * 5,
        cost=(0, 2_000_000),
    )(slot_of, late_other, mine, beside, across, others)

    own = own.reshape(width, half)
    far = swap_cores(own)
    partial, grad_sq = call(
        near_kernel,
        [jax.ShapeDtypeStruct((width, width), F32), jax.ShapeDtypeStruct((8, 128), F32)],
        [VMEM_SPEC, VMEM_SPEC],
        cost=(270_000_000, 4_000_000),
    )(own, right)
    update = call(
        direction_kernel,
        jax.ShapeDtypeStruct((width, half), BF16),
        [VMEM_SPEC] * 5,
    )(far, partial, left, right, grad_sq)

    update, own, far = lax.optimization_barrier((update, own, far))
    rows = exchange(update.reshape(owners, shard_rows, half), ("y", "z"))
    beside, across, mine = call(
        terms_kernel,
        [both, piece, piece],
        [VMEM_SPEC, VMEM_SPEC],
        [pltpu.VMEM((width, width), BF16)],
        cost=(800_000_000, 2_000_000),
    )(own, far)
    across = turn(across, 2)
    beside = lax.ppermute(beside, ("x", "core"), ways)
    packed = call(
        compact_kernel,
        jax.ShapeDtypeStruct((chips, depth, shard_rows, half), BF16),
        [SMEM_SPEC, VMEM_SPEC],
    )(owned, rows)
    passed = swap_cores(lax.dynamic_index_in_dim(beside, 1 - core, keepdims=False))
    packed, beside, across, passed = lax.optimization_barrier((packed, beside, across, passed))
    near = exchange(packed, "x").reshape(blocks, shard_rows, half)
    near, beside, across, passed = lax.optimization_barrier((near, beside, across, passed))
    near = call(order_kernel, half_rows, [SMEM_SPEC, VMEM_SPEC])(source, near)
    beyond = swap_cores(near)
    stat = jax.ShapeDtypeStruct(left_stat.shape, F32)
    whole_rows = jax.ShapeDtypeStruct((blocks, shard_rows, width), BF16)
    begun, left_new, right_new = call(
        finish_kernel,
        [whole_rows, stat, stat],
        [SMEM_SPEC] + [VMEM_SPEC] * 7,
        [
            pltpu.VMEM(left_stat.shape, F32),
            pltpu.VMEM(right_stat.shape, F32),
            pltpu.SemaphoreType.DMA,
            pltpu.SemaphoreType.DMA((capacity, 2)),
        ],
        [HBM_SPEC] * 3,
        cost=(10_000_000, 5_000_000),
    )(chip_of, near, mine, across, beside, passed, left_stat, right_stat)
    result = call(
        place_far_kernel,
        whole_rows,
        [VMEM_SPEC, HBM_SPEC],
        [pltpu.SemaphoreType.DMA],
        HBM_SPEC,
        aliases={1: 0},
    )(beyond, begun)
    return (result, left_new, right_new)


def solution(mesh):
    fine = Mesh(mesh.devices.reshape(4, 2, 4, 16), ("x", "core", "y", "z"))
    replica, shard = ("x", "core"), ("y", "z")
    in_specs = (
        P(replica, None, shard, None),
        P(),
        P(shard, replica, None),
        P(shard, replica, None),
        P(shard, replica, None),
        P(shard, replica, None),
    )
    out_specs = (P(None, shard, None), P(shard, replica, None), P(shard, replica, None))
    return jax.shard_map(local, mesh=fine, in_specs=in_specs, out_specs=out_specs, check_vma=False)
```
